32 devices in a mesh: row: 8 (over y, x, core), col: 4 (over z).
Axes of the slice: x: 2, y: 2, z: 4, core: 2. Of those that a mesh axis runs over, the one named last changes fastest.
Arguments:
- inputs: bfloat16 [4096, 1792], P(('row', 'col')), may hold values from -6 to 6
- attention_norm_gain: float32 [1792], replicated, may hold values from 0.5 to 1.5
- query_key_value_weight: bfloat16 [1792, 3, 1792], P('row', None, 'col'), may hold values from -0.125 to 0.125
- filter_taps: float32 [3, 2, 1792], P(None, None, 'col'), may hold values from -3 to 3
- output_projection: bfloat16 [1792, 1792], P('col', 'row'), may hold values from -0.125 to 0.125
- window_key_value: bfloat16 [64, 2, 16, 7168], P('row', None, 'col'), may hold values from -300 to 300
- cache_valid_length: int32 [64], P('row'), may hold values from 0 to 64
- lengths: int32 [8, 8], P('row'), may hold values from 1 to 128, 512 in all within a row
- token_adapter_index: int32 [4096, 1], P('row'), may hold values from 0 to 15; in each aligned block of 128 rows (0 to 127, 128 to 255, ...) at most 16 rows name the same one
- adapter_down_map: bfloat16 [16, 1792, 16], P('row'), may hold values from -0.125 to 0.125
- adapter_up_map: bfloat16 [16, 16, 1792], P('row'), may hold values from -1.5 to 1.5
- feed_forward_gain: float32 [1792], replicated, may hold values from 0.5 to 1.5
- gate_projection: bfloat16 [1792, 4096], P('row', 'col'), may hold values from -0.125 to 0.125
- up_projection: bfloat16 [1792, 4096], P('row', 'col'), may hold values from -0.125 to 0.125
- down_projection: bfloat16 [4096, 1792], P('col', 'row'), may hold values from -0.09375 to 0.09375
Outputs:
- layer_out: bfloat16 [4096, 1792], P(('row', 'col'))
The draws below stay inside these ranges and needn't reach their ends.
Inputs may be any that keep to these rules, and one draw needn't show every extreme that they name: Each row of lengths sums to 512, and its largest entry is exactly 128. `cache_valid_length`: A request with 0 is a new prompt without cached positions. `token_adapter_index`: in each aligned block of 128 tokens no adapter serves more than 16 tokens, and some adapter serves exactly 16.
All inputs are finite; a program needn't handle non-finite values.
Results may differ from the reference program's by a relative error of at most 0.019.
Values may be sent and summed in bfloat16 or wider, within the bound.
No kernel may reach another device: no remote copies, remote signals or barrier semaphores. Data moves between devices by JAX's collectives and lax.ppermute only.
A program may use at most 64 MiB of HBM per device.

```python
import math
import jax
import jax.numpy as jnp
import numpy as np
from jax import lax

MODEL_WIDTH = 1792
HEADS = 16
HD = 112
ATT = 1792
FF = 4096
WIN = 64
KSIZE = 3
ADAPTER_RANK = 16
ADAPTER_COUNT = 16
TOK_ROW = 512
TOKENS = 4096
REQ_ROW = 8
REQUESTS = 64
LEN_MOST = 128
BLOCK = 128
MOST = 16
N_ROW = 8
N_COL = 4


def draw_window_key_value(key, part):
    key_base = jax.random.fold_in(key, 11)
    whole = jnp.clip(jax.random.normal(key_base, (REQUESTS, 2, HEADS, WIN * HD), jnp.float32), -6.0, 6.0)
    return whole.astype(jnp.bfloat16)


def with_ends(entries, key, low, top_value):
    longest = entries.shape.index(max(entries.shape))
    spots = []
    for shift in (0, 1):
        where = [jax.random.randint(jax.random.fold_in(key, axis), (), 0, length) for axis, length in enumerate(entries.shape)]
        where[longest] = (where[longest] + shift) % entries.shape[longest]
        spots.append(tuple(where))
    return entries.at[spots[0]].set(low).at[spots[1]].set(top_value)


def steps_of(own_key, shape, split, smallest, largest):
    factor_of, own = 1.0, jax.random.fold_in(own_key, 6)
    for position, blocks in split:
        draws = jnp.exp(jax.random.uniform(jax.random.fold_in(own, position), (blocks,), jnp.float32, smallest / len(split), largest / len(split)))
        factor_of = factor_of * jnp.repeat(draws, shape[position] // blocks).reshape([-1 if axis == position else 1 for axis in range(len(shape))])
    return factor_of


def split_up(count, total, limit, skew):
    weights = [(1 << 20) // math.isqrt(standing ** skew) + 1 for standing in range(2, count + 1)]
    rest, counts = total - limit - (count - 1), [1] * (count - 1)
    while rest > 0:
        free = [i for i in range(count - 1) if counts[i] < limit]
        mass, remaining = sum([weights[i] for i in free]), rest
        for i in free:
            more = min(limit - counts[i], max(1, remaining * weights[i] // mass), rest)
            counts[i] = counts[i] + more
            rest = rest - more
    return np.array([limit] + counts)


def ragged_sizes(stream_key, number_of, total, limit, slope):
    if number_of == 2:
        one = jax.random.randint(stream_key, (), max(1, total - limit), min(limit, total - 1) + 1)
        return jnp.stack([one, total - one])
    sizes = jnp.asarray(split_up(number_of, total, limit, slope), jnp.int32)
    couples = (number_of - 1) // 2
    donor, receiver = sizes[1:1 + 2 * couples:2], sizes[2:2 + 2 * couples:2]
    slack = jnp.minimum(donor - 1, limit - receiver)
    passed = jax.random.randint(jax.random.fold_in(stream_key, 1), (couples,), 0, 1 << 20) % (slack + 1)
    sizes = sizes.at[1:1 + 2 * couples:2].set(donor - passed).at[2:2 + 2 * couples:2].set(receiver + passed)
    return sizes[jax.random.permutation(jax.random.fold_in(stream_key, 2), number_of)]


def shared_out(rng, own, number, rows, amount, top, bound, skew):
    sequence = jax.random.permutation(rng, amount)
    packed, common = shares(amount, rows * top, bound, skew, True), shares(amount, rows * top, bound, skew, False)
    places = jnp.arange(amount)

    def named(sizes, offset_by):
        used = int((sizes > 0).sum())
        fixed = max(1, used // 4)
        passed = fixed + (places - fixed + offset_by * (used - fixed)) % max(1, amount - fixed)
        return jnp.zeros((amount,), jnp.int32).at[sequence[jnp.where(places < fixed, places, passed)]].set(jnp.asarray(sizes, jnp.int32))

    sizes = jnp.where(number % 4 == 0, named(packed, number // 4), named(common, number - number // 4 - 1))
    mixed = jax.random.permutation(jax.random.fold_in(own, 3), amount)
    giver, receiver = mixed[0:amount // 2 * 2:2], mixed[1:amount // 2 * 2:2]
    slack = jnp.minimum(sizes[giver] - 1, bound - sizes[receiver]) // 2
    slack = jnp.where((giver == sequence[0]) | (receiver == sequence[0]) | (sizes[receiver] == 0), 0, jnp.maximum(slack, 0))
    passed = jax.random.randint(jax.random.fold_in(own, 4), (amount // 2,), 0, 1 << 20) % (slack + 1)
    sizes = sizes.at[giver].add(-passed).at[receiver].add(passed)
    items = jnp.searchsorted(jnp.cumsum(sizes), jnp.arange(rows * top), side="right").astype(jnp.int32)
    listing = items.reshape(top, rows).T
    listing = listing[jax.random.permutation(jax.random.fold_in(own, 1), rows)]
    offset_by = jax.random.randint(jax.random.fold_in(own, 2), (rows, 1), 0, top)
    return jnp.take_along_axis(listing, (jnp.arange(top)[None, :] + offset_by) % top, axis=1)


def shares(amount, total, reach, slope, full):
    weights = [(1 << 20) // math.isqrt(grade ** slope) + 1 for grade in range(1, amount + 1)]
    largest = reach if full else min(reach, max(-(-total // amount), total * weights[0] // sum(weights)))
    least = 1 if total - largest >= amount - 1 else 0
    given, surplus = [largest] + [least] * (amount - 1), total - largest - least * (amount - 1)
    while surplus > 0:
        candidates = [i for i in range(1, amount) if given[i] < largest] or [i for i in range(1, amount) if given[i] < reach]
        pool, left = sum([weights[i] for i in candidates]), surplus
        for i in candidates:
            extra = min(reach - given[i], max(1, left * weights[i] // pool), surplus)
            given[i] = given[i] + extra
            surplus = surplus - extra
    return np.array(given)


def bell_draw(key, extent, scale, reach, pieces=(), held_as=jnp.bfloat16):
    drawn = jax.random.normal(key, extent, jnp.float32) * scale
    if len(pieces) > 0:
        drawn = steps_of(key, extent, pieces, -0.22, 0.18) * drawn
    return jnp.clip(drawn, min=-reach, max=reach).astype(held_as)


def setup_inputs(seed: int = 0) -> dict:
    key_of = jax.random.split(jax.random.key(seed), 16)
    inputs = bell_draw(key_of[0], (TOKENS, MODEL_WIDTH), 1.0, 6.0, ((0, 32),))
    attention_norm_gain = jnp.clip(1.0 + 0.1 * jax.random.normal(key_of[1], (MODEL_WIDTH,), jnp.float32), 0.5, 1.5)
    query_key_value_weight = bell_draw(key_of[2], (MODEL_WIDTH, 3, ATT), MODEL_WIDTH ** -0.5, 0.125, ((0, 8), (2, 4)))
    filter_taps = bell_draw(key_of[3], (KSIZE, 2, ATT), 0.6, 3.0, ((2, 4),), jnp.float32)
    output_projection = bell_draw(key_of[4], (ATT, MODEL_WIDTH), ATT ** -0.5, 0.125, ((0, 4), (1, 8)))
    window_key_value = draw_window_key_value(jax.random.fold_in(key_of[15], 71), 0)
    cache_valid_length = with_ends(jax.random.randint(key_of[6], (REQUESTS,), 0, WIN + 1), jax.random.fold_in(key_of[6], 1), 0, WIN).astype(jnp.int32)
    lengths = jax.vmap(lambda own: ragged_sizes(own, REQ_ROW, TOK_ROW, LEN_MOST, 2))(jax.random.split(key_of[7], N_ROW)).reshape((N_ROW, REQ_ROW)).astype(jnp.int32)
    token_adapter_index_keys = jax.random.split(jax.random.fold_in(key_of[8], 1), TOKENS // BLOCK)
    token_adapter_index_turns = jax.random.permutation(jax.random.fold_in(key_of[8], 3), TOKENS // BLOCK)
    token_adapter_index = jax.vmap(lambda own, number: shared_out(jax.random.fold_in(key_of[8], 2), own, number, BLOCK, ADAPTER_COUNT, 1, MOST, 2))(token_adapter_index_keys, token_adapter_index_turns).reshape((TOKENS, 1))
    adapter_down_map = bell_draw(key_of[9], (ADAPTER_COUNT, MODEL_WIDTH, ADAPTER_RANK), MODEL_WIDTH ** -0.5, 0.125, ((0, 8),))
    adapter_up_map = bell_draw(key_of[10], (ADAPTER_COUNT, ADAPTER_RANK, MODEL_WIDTH), ADAPTER_RANK ** -0.5, 1.5, ((0, 8),))
    feed_forward_gain = jnp.clip(1.0 + 0.1 * jax.random.normal(key_of[11], (MODEL_WIDTH,), jnp.float32), 0.5, 1.5)
    gate_projection = bell_draw(key_of[12], (MODEL_WIDTH, FF), MODEL_WIDTH ** -0.5, 0.125, ((0, 8), (1, 4)))
    up_projection = bell_draw(key_of[13], (MODEL_WIDTH, FF), MODEL_WIDTH ** -0.5, 0.125, ((0, 8), (1, 4)))
    down_projection = bell_draw(key_of[14], (FF, MODEL_WIDTH), FF ** -0.5, 0.09375, ((0, 4), (1, 8)))
    return {"inputs": inputs, "attention_norm_gain": attention_norm_gain, "query_key_value_weight": query_key_value_weight, "filter_taps": filter_taps, "output_projection": output_projection, "window_key_value": window_key_value, "cache_valid_length": cache_valid_length, "lengths": lengths, "token_adapter_index": token_adapter_index, "adapter_down_map": adapter_down_map, "adapter_up_map": adapter_up_map, "feed_forward_gain": feed_forward_gain, "gate_projection": gate_projection, "up_projection": up_projection, "down_projection": down_projection}


epsilon = 1e-05

def rms_scaled(values, gain_row):
    mean_square = lax.optimization_barrier(jnp.mean(values * values, axis=-1, keepdims=True))
    return values * lax.rsqrt(mean_square + epsilon) * gain_row.astype(jnp.float32)

def layout(lengths_row, tok_count):
    finish = jnp.cumsum(lengths_row).astype(jnp.int32)
    begins = finish - lengths_row
    places = jnp.arange(tok_count, dtype=jnp.int32)
    segment = lax.optimization_barrier(jnp.sum((places[:, None] >= finish[None, :]).astype(jnp.int32), axis=1))
    member = segment[:, None] == jnp.arange(lengths_row.shape[0], dtype=jnp.int32)[None, :]
    inside = places - lax.optimization_barrier(jnp.sum(jnp.where(member, begins[None, :], 0), axis=1)).astype(jnp.int32)
    return (segment, inside)

def shifted(values, offset, inside):
    moved_rows = jnp.pad(values[:values.shape[0] - offset], ((offset, 0), (0, 0)))
    return jnp.where((inside >= offset)[:, None], moved_rows, jnp.zeros_like(moved_rows))

def convolve(values, taps, inside):
    running = jnp.zeros_like(values)
    for offset in range(taps.shape[0]):
        running = running + taps[offset][None, :] * shifted(values, offset, inside)
    return running

def make_qkv(qkv_mixed, filter_taps, inside):
    queries = qkv_mixed[:, 0].astype(jnp.bfloat16)
    keys_used = convolve(qkv_mixed[:, 1], filter_taps[:, 0], inside).astype(jnp.bfloat16)
    raw_values = qkv_mixed[:, 2]
    gates = jax.nn.sigmoid(convolve(raw_values, filter_taps[:, 1], inside))
    values_used = (raw_values * gates).astype(jnp.bfloat16)
    return (queries, keys_used, values_used)

def split_cache(window_key_value, head_size):
    requests_here, head_count = (window_key_value.shape[0], window_key_value.shape[2])
    window = window_key_value.shape[3] // head_size
    split_kv = window_key_value.reshape(requests_here, 2, head_count, window, head_size)
    cached_key_rows = jnp.transpose(split_kv[:, 0], (0, 2, 1, 3)).reshape(requests_here * window, head_count, head_size)
    cached_value_rows = jnp.transpose(split_kv[:, 1], (0, 2, 1, 3)).reshape(requests_here * window, head_count, head_size)
    return (cached_key_rows, cached_value_rows, window)

def attend(queries, keys_used, values_used, window_key_value, segment, inside, cache_valid_length, head_size):
    tok_count = queries.shape[0]
    head_count = queries.shape[1] // head_size
    requests_here = window_key_value.shape[0]
    cached_key_rows, cached_value_rows, window = split_cache(window_key_value, head_size)
    query_per_head = queries.reshape(tok_count, head_count, head_size).astype(jnp.float32)
    key_h = keys_used.reshape(tok_count, head_count, head_size).astype(jnp.float32)
    value_per_head = values_used.reshape(tok_count, head_count, head_size).astype(jnp.float32)
    cached_key_rows = cached_key_rows.astype(jnp.float32)
    cached_value_rows = cached_value_rows.astype(jnp.float32)
    attention_score_scale = head_size ** (-0.5)
    places = jnp.arange(tok_count, dtype=jnp.int32)
    local_mask = (segment[:, None] == segment[None, :]) & (places[None, :] <= places[:, None]) & (places[None, :] > places[:, None] - window)
    slot_ids = jnp.arange(requests_here * window, dtype=jnp.int32)
    owner_req = slot_ids // window
    within = slot_ids % window
    slot_ages = jnp.repeat(cache_valid_length, window)
    cache_mask = (segment[:, None] == owner_req[None, :]) & (within[None, :] >= window - slot_ages[None, :]) & (within[None, :] > inside[:, None])
    local_scores = jnp.einsum('thd,jhd->htj', query_per_head, key_h) * attention_score_scale
    cached_score_rows = jnp.einsum('sek,yek->esy', query_per_head, cached_key_rows) * attention_score_scale
    local_scores = jnp.where(local_mask[None], local_scores, -jnp.inf)
    cached_score_rows = jnp.where(cache_mask[None], cached_score_rows, -jnp.inf)
    row_max = jnp.maximum(lax.optimization_barrier(jnp.max(local_scores, axis=-1, keepdims=True)), lax.optimization_barrier(jnp.max(cached_score_rows, axis=-1, keepdims=True)))
    local_exp = jnp.exp(local_scores - row_max)
    cache_exp = jnp.exp(cached_score_rows - row_max)
    denominator = lax.optimization_barrier(jnp.sum(local_exp, axis=-1, keepdims=True)) + lax.optimization_barrier(jnp.sum(cache_exp, axis=-1, keepdims=True))
    window_attention_weight = (local_exp / denominator).astype(jnp.bfloat16).astype(jnp.float32)
    cached_attention_weight = (cache_exp / denominator).astype(jnp.bfloat16).astype(jnp.float32)
    joined_output = jnp.einsum('zkc,czu->kzu', window_attention_weight, value_per_head) + jnp.einsum('lar,rlx->alx', cached_attention_weight, cached_value_rows)
    return joined_output.reshape(tok_count, head_count * head_size).astype(jnp.bfloat16)

def apply_low_rank(normalized_input, adapter_row_picks, adapter_down_map, adapter_up_map):
    every_adapter = adapter_down_map.shape[0]
    member = (adapter_row_picks[:, None] == jnp.arange(every_adapter, dtype=jnp.int32)[None, :]).astype(jnp.float32)
    every_low_rank = jnp.einsum('lw,bwj->lbj', normalized_input.astype(jnp.float32), adapter_down_map.astype(jnp.float32))
    low = lax.optimization_barrier(jnp.sum(member[:, :, None] * every_low_rank, axis=1)).astype(jnp.bfloat16)
    widened_low_rank = member[:, :, None] * low.astype(jnp.float32)[:, None, :]
    return jnp.einsum('bhf,hfz->bz', widened_low_rank, adapter_up_map.astype(jnp.float32)).astype(jnp.bfloat16)

def reference(inputs, attention_norm_gain, query_key_value_weight, filter_taps, output_projection, window_key_value, cache_valid_length, lengths, token_adapter_index, adapter_down_map, adapter_up_map, feed_forward_gain, gate_projection, up_projection, down_projection):

    def one_group(row_group):
        token_rows = lax.dynamic_slice_in_dim(inputs, row_group * TOK_ROW, TOK_ROW, 0)
        normalized_input = rms_scaled(token_rows.astype(jnp.float32), attention_norm_gain).astype(jnp.bfloat16)
        qkv_mixed = jnp.einsum('td,dka->tka', normalized_input.astype(jnp.float32), query_key_value_weight.astype(jnp.float32))
        lengths_row = lax.dynamic_slice_in_dim(lengths, row_group, 1, 0)[0]
        segment, inside = layout(lengths_row, TOK_ROW)
        queries, keys_used, values_used = make_qkv(qkv_mixed, filter_taps, inside)
        cache_here = lax.dynamic_slice_in_dim(window_key_value, row_group * REQ_ROW, REQ_ROW, 0)
        ages_here = lax.dynamic_slice_in_dim(cache_valid_length, row_group * REQ_ROW, REQ_ROW, 0)
        attended = attend(queries, keys_used, values_used, cache_here, segment, inside, ages_here, HD)
        adapter_row_picks = lax.dynamic_slice_in_dim(token_adapter_index[:, 0], row_group * TOK_ROW, TOK_ROW, 0)
        adapter_output = apply_low_rank(normalized_input, adapter_row_picks, adapter_down_map, adapter_up_map)
        attn_sum = jnp.dot(attended, output_projection, preferred_element_type=jnp.float32) + adapter_output.astype(jnp.float32)
        return (token_rows.astype(jnp.float32) + attn_sum).astype(jnp.bfloat16)
    residual = lax.map(one_group, jnp.arange(N_ROW, dtype=jnp.int32)).reshape(TOKENS, MODEL_WIDTH)
    normed_mlp = rms_scaled(residual.astype(jnp.float32), feed_forward_gain).astype(jnp.bfloat16)
    gate = jnp.dot(normed_mlp, gate_projection, preferred_element_type=jnp.float32)
    up_part = jnp.dot(normed_mlp, up_projection, preferred_element_type=jnp.float32)
    hidden = (jax.nn.silu(gate) * up_part).astype(jnp.bfloat16)
    group_width = FF // N_COL
    accumulated = jnp.zeros((TOKENS, MODEL_WIDTH), jnp.float32)
    for group_idx in range(N_COL):
        lower = group_idx * group_width
        down_part = jnp.dot(hidden[:, lower:lower + group_width], down_projection[lower:lower + group_width], preferred_element_type=jnp.float32).astype(jnp.bfloat16)
        accumulated = accumulated + down_part.astype(jnp.float32)
    return (residual.astype(jnp.float32) + accumulated).astype(jnp.bfloat16)
```

```python
import functools

import jax
import jax.numpy as jnp
from jax import lax
from jax.experimental import pallas as pl
from jax.experimental.pallas import tpu as pltpu
from jax.sharding import PartitionSpec as P

HD = 112


epsilon = 1e-05


def rms_scaled(values, gain_row):
    mean_square = jnp.mean(values * values, axis=-1, keepdims=True)
    return values * lax.rsqrt(mean_square + epsilon) * gain_row


def layout(lengths_row, tok_count):
    finish = jnp.cumsum(lengths_row)
    begins = finish - lengths_row
    places = jnp.arange(tok_count, dtype=jnp.int32)
    segment = jnp.sum((places[:, None] >= finish[None, :]).astype(jnp.int32), axis=1)
    member = segment[:, None] == jnp.arange(lengths_row.shape[0], dtype=jnp.int32)[None, :]
    inside = places - jnp.sum(jnp.where(member, begins[None, :], 0), axis=1)
    return (segment, inside)


def shifted(values, offset, inside):
    moved_rows = jnp.pad(values[: values.shape[0] - offset], ((offset, 0), (0, 0)))
    return jnp.where((inside >= offset)[:, None], moved_rows, jnp.zeros_like(moved_rows))


def convolve(values, taps, inside):
    running = jnp.zeros_like(values)
    for offset in range(taps.shape[0]):
        running = running + taps[offset][None, :] * shifted(values, offset, inside)
    return running


def make_qkv(qkv_mixed, filter_taps, inside):
    queries = qkv_mixed[:, 0].astype(jnp.bfloat16)
    keys_used = convolve(qkv_mixed[:, 1], filter_taps[:, 0], inside).astype(jnp.bfloat16)
    raw_values = qkv_mixed[:, 2]
    gates = jax.nn.sigmoid(convolve(raw_values, filter_taps[:, 1], inside))
    values_used = (raw_values * gates).astype(jnp.bfloat16)
    return (queries, keys_used, values_used)


def split_cache(window_key_value, head_size):
    requests_here, head_count = (window_key_value.shape[0], window_key_value.shape[2])
    window = window_key_value.shape[3] // head_size
    split_kv = window_key_value.reshape(requests_here, 2, head_count, window, head_size)
    cached_key_rows = jnp.transpose(split_kv[:, 0], (0, 2, 1, 3)).reshape(
        requests_here * window, head_count, head_size
    )
    cached_value_rows = jnp.transpose(split_kv[:, 1], (0, 2, 1, 3)).reshape(
        requests_here * window, head_count, head_size
    )
    return (cached_key_rows, cached_value_rows, window)


def attend(
    queries,
    keys_used,
    values_used,
    window_key_value,
    segment,
    inside,
    cache_valid_length,
    head_size,
):
    tok_count = queries.shape[0]
    head_count = queries.shape[1] // head_size
    requests_here = window_key_value.shape[0]
    cached_key_rows, cached_value_rows, window = split_cache(window_key_value, head_size)
    query_per_head = queries.reshape(tok_count, head_count, head_size)
    key_h = keys_used.reshape(tok_count, head_count, head_size)
    value_per_head = values_used.reshape(tok_count, head_count, head_size)
    attention_score_scale = head_size ** (-0.5)
    places = jnp.arange(tok_count, dtype=jnp.int32)
    local_mask = (
        (segment[:, None] == segment[None, :])
        & (places[None, :] <= places[:, None])
        & (places[None, :] > places[:, None] - window)
    )
    slot_ids = jnp.arange(requests_here * window, dtype=jnp.int32)
    owner_req = slot_ids // window
    within = slot_ids % window
    slot_ages = jnp.repeat(cache_valid_length, window)
    cache_mask = (
        (segment[:, None] == owner_req[None, :])
        & (within[None, :] >= window - slot_ages[None, :])
        & (within[None, :] > inside[:, None])
    )
    local_scores = (
        jnp.einsum("thd,jhd->htj", query_per_head, key_h, preferred_element_type=jnp.float32)
        * attention_score_scale
    )
    cached_score_rows = (
        jnp.einsum(
            "sek,yek->esy", query_per_head, cached_key_rows, preferred_element_type=jnp.float32
        )
        * attention_score_scale
    )
    local_scores = jnp.where(local_mask[None], local_scores, -jnp.inf)
    cached_score_rows = jnp.where(cache_mask[None], cached_score_rows, -jnp.inf)
    row_max = jnp.maximum(
        jnp.max(local_scores, axis=-1, keepdims=True),
        jnp.max(cached_score_rows, axis=-1, keepdims=True),
    )
    local_exp = jnp.exp(local_scores - row_max)
    cache_exp = jnp.exp(cached_score_rows - row_max)
    denominator = jnp.sum(local_exp, axis=-1, keepdims=True) + jnp.sum(
        cache_exp, axis=-1, keepdims=True
    )
    window_attention_weight = (local_exp / denominator).astype(jnp.bfloat16)
    cached_attention_weight = (cache_exp / denominator).astype(jnp.bfloat16)
    joined_output = jnp.einsum(
        "zkc,czu->kzu", window_attention_weight, value_per_head, preferred_element_type=jnp.float32
    )
    joined_output = joined_output + jnp.einsum(
        "lar,rlx->alx",
        cached_attention_weight,
        cached_value_rows,
        preferred_element_type=jnp.float32,
    )
    return joined_output.reshape(tok_count, head_count * head_size).astype(jnp.bfloat16)


def plain(
    inputs,
    attention_norm_gain,
    query_key_value_weight,
    filter_taps,
    output_projection,
    window_key_value,
    cache_valid_length,
    lengths,
    token_adapter_index,
    adapter_down_map,
    adapter_up_map,
    feed_forward_gain,
    gate_projection,
    up_projection,
    down_projection,
):
    own_count = inputs.shape[0]
    column = lax.axis_index("col")
    row_count = lax.axis_size("row")
    gathered = lax.all_gather(inputs, "col", axis=0, tiled=True)
    tok_count = gathered.shape[0]
    normalized_input = rms_scaled(gathered.astype(jnp.float32), attention_norm_gain).astype(
        jnp.bfloat16
    )
    qkv_mixed = jnp.einsum(
        "td,dka->tka",
        normalized_input,
        lax.all_gather(query_key_value_weight, "row", axis=0, tiled=True),
        preferred_element_type=jnp.float32,
    )
    segment, inside = layout(lengths[0], tok_count)
    queries, keys_used, values_used = make_qkv(qkv_mixed, filter_taps, inside)
    attended = attend(
        queries, keys_used, values_used, window_key_value, segment, inside, cache_valid_length, HD
    )
    kept_count = adapter_down_map.shape[0]
    every_adapter = kept_count * row_count
    capacity = max(2, 2 * own_count // every_adapter)
    first_row = column * own_count
    own_rows = lax.dynamic_slice_in_dim(normalized_input, first_row, own_count, 0)
    own_ids = lax.dynamic_slice_in_dim(token_adapter_index[:, 0], first_row, own_count, 0)
    member = (own_ids[:, None] == jnp.arange(every_adapter, dtype=jnp.int32)[None, :]).astype(
        jnp.int32
    )
    before = jnp.cumsum(member, axis=0) - member
    slot_rank = jnp.sum(before * member, axis=1)
    target = own_ids * capacity + slot_rank
    placer = (
        target[None, :] == jnp.arange(every_adapter * capacity, dtype=jnp.int32)[:, None]
    ).astype(jnp.bfloat16)
    outgoing = jnp.dot(placer, own_rows, preferred_element_type=jnp.float32).astype(jnp.bfloat16)
    outgoing = outgoing.reshape(row_count, kept_count, capacity, normalized_input.shape[1])
    reduced_rank_input = jnp.einsum(
        "sakd,adr->sakr",
        lax.all_to_all(outgoing, "row", split_axis=0, concat_axis=0, tiled=True),
        adapter_down_map,
        preferred_element_type=jnp.float32,
    ).astype(jnp.bfloat16)
    answered = jnp.einsum(
        "zjbf,jfm->zjbm", reduced_rank_input, adapter_up_map, preferred_element_type=jnp.float32
    ).astype(jnp.bfloat16)
    returned = lax.all_to_all(answered, "row", split_axis=0, concat_axis=0, tiled=True).reshape(
        every_adapter * capacity, normalized_input.shape[1]
    )
    delta_rows = jnp.dot(jnp.transpose(placer), returned, preferred_element_type=jnp.float32)
    out_term = jnp.dot(
        attended,
        lax.all_gather(output_projection, "row", axis=1, tiled=True),
        preferred_element_type=jnp.float32,
    )
    own_term = lax.dynamic_slice_in_dim(out_term, first_row, own_count, 0) + delta_rows
    out_term = lax.dynamic_update_slice_in_dim(out_term, own_term, first_row, 0)
    attn_share = lax.psum_scatter(
        out_term.astype(jnp.bfloat16), "col", scatter_dimension=0, tiled=True
    ).astype(jnp.float32)
    residual = (inputs.astype(jnp.float32) + attn_share).astype(jnp.bfloat16)
    whole_mixed = lax.all_gather(residual, "col", axis=0, tiled=True)
    normed_mlp = rms_scaled(whole_mixed.astype(jnp.float32), feed_forward_gain).astype(jnp.bfloat16)

    def add_rows(piece):
        return jnp.dot(normed_mlp, piece, preferred_element_type=jnp.float32)

    gate = add_rows(lax.all_gather(gate_projection, "row", axis=0, tiled=True))
    up_part = add_rows(lax.all_gather(up_projection, "row", axis=0, tiled=True))
    hidden = (jax.nn.silu(gate) * up_part).astype(jnp.bfloat16)
    down_term = jnp.dot(
        hidden,
        lax.all_gather(down_projection, "row", axis=1, tiled=True),
        preferred_element_type=jnp.float32,
    )
    mlp_added = lax.psum_scatter(
        down_term.astype(jnp.bfloat16), "col", scatter_dimension=0, tiled=True
    ).astype(jnp.float32)
    return (residual.astype(jnp.float32) + mlp_added).astype(jnp.bfloat16)


LANES = 128
MIB = 1 << 20


def params(mib):
    return pltpu.CompilerParams(vmem_limit_bytes=mib * MIB)


HBM = pl.BlockSpec(memory_space=pl.ANY)
VMEM = pl.BlockSpec(memory_space=pltpu.VMEM)
NT = (((1,), (1,)), ((), ()))


def rms_kernel(x_ref, gain_ref, out_ref):
    values = x_ref[...].astype(jnp.float32)
    mean_square = jnp.mean(values * values, axis=-1, keepdims=True)
    out_ref[...] = (values * lax.rsqrt(mean_square + epsilon) * gain_ref[...]).astype(out_ref.dtype)


def normed_rows(rows, gain):
    return pl.pallas_call(
        rms_kernel,
        out_shape=jax.ShapeDtypeStruct(rows.shape, jnp.bfloat16),
        in_specs=[VMEM, VMEM],
        out_specs=VMEM,
        compiler_params=params(16),
    )(rows, gain[None, :])


def xor_pairs(count, mask):
    return [(i, i ^ mask) for i in range(count)]


def swap(value, axis, mask):
    return lax.ppermute(value, axis, xor_pairs(lax.axis_size(axis), mask))


def spread_weights(own):
    half = own.shape[1] // 2
    low, high = own[:, :half], own[:, half:]
    x_low, y_high = swap(low, "row", 2), swap(high, "row", 4)
    y_low, x_high = swap(low, "row", 4), swap(high, "row", 2)
    xy_low, xy_high = swap(x_low, "row", 4), swap(y_high, "row", 2)
    pieces = [
        (own, 0, 0),
        (x_low, 2, 0),
        (y_high, 4, half),
        (y_low, 4, 0),
        (x_high, 2, half),
        (xy_low, 6, 0),
        (xy_high, 6, half),
    ]
    return pieces + [(swap(piece, "row", 1), mask ^ 1, first) for piece, mask, first in pieces]


def qkv_kernel(places, x_refs, w_refs, taps_ref, inside_ref, q_ref, k_ref, v_ref, x_all, w_all, padded, sems):
    row, col = lax.axis_index("row"), lax.axis_index("col")
    count = x_refs[0].shape[0]
    shard = x_all.shape[1] // lax.axis_size("row")
    copies = []
    for i, (ref, (mask, first)) in enumerate(zip(w_refs, places)):
        start = pl.multiple_of((row ^ mask) * shard + first, 16)
        copies.append(
            pltpu.make_async_copy(
                ref.at[pl.ds(0, 3)], w_all.at[:, pl.ds(start, ref.shape[1])], sems.at[i]
            )
        )
    for i, ref in enumerate(x_refs):
        start = pl.multiple_of((col ^ i) * count, 16)
        copies.append(
            pltpu.make_async_copy(ref, x_all.at[pl.ds(start, count)], sems.at[len(w_refs) + i])
        )
    for copy in copies:
        copy.start()
    padded[0:8, :] = jnp.zeros((8, padded.shape[1]), jnp.float32)
    for copy in copies:
        copy.wait()
    tokens = x_all.shape[0]
    inside = inside_ref[...]

    def mixed(which):
        return jnp.dot(x_all[...], w_all[which], preferred_element_type=jnp.float32)

    def convolved(raw, which):
        padded[8:, :] = raw
        running = taps_ref[which : which + 1, :] * raw
        for offset in range(1, taps_ref.shape[0] // 2):
            moved = padded[8 - offset : 8 - offset + tokens, :]
            tap = taps_ref[2 * offset + which : 2 * offset + which + 1, :]
            running = running + jnp.where(inside >= offset, tap * moved, 0.0)
        return running

    q_ref[...] = mixed(0).astype(jnp.bfloat16)
    k_ref[...] = convolved(mixed(1), 0).astype(jnp.bfloat16)
    raw_values = mixed(2)
    gates = jax.nn.sigmoid(convolved(raw_values, 1))
    v_ref[...] = (raw_values * gates).astype(jnp.bfloat16)


def qkv_call(blocks, pieces, taps, inside_col):
    tokens, width = blocks[0].shape[0] * len(blocks), blocks[0].shape[1]
    lanes = pieces[0][0].shape[2]
    places = [(mask, first) for _, mask, first in pieces]
    n_x, n_w = len(blocks), len(pieces)

    def body(*refs):
        x_refs, w_refs = refs[:n_x], refs[n_x : n_x + n_w]
        qkv_kernel(places, x_refs, w_refs, *refs[n_x + n_w :])

    one = jax.ShapeDtypeStruct((tokens, lanes), jnp.bfloat16)
    return pl.pallas_call(
        body,
        out_shape=[one, one, one],
        in_specs=[HBM] * (n_x + n_w) + [VMEM, VMEM],
        out_specs=[VMEM] * 3,
        scratch_shapes=[
            pltpu.VMEM((tokens, width), jnp.bfloat16),
            pltpu.VMEM((3, width, lanes), jnp.bfloat16),
            pltpu.VMEM((tokens + 8, lanes), jnp.float32),
            pltpu.SemaphoreType.DMA((n_x + n_w,)),
        ],
        compiler_params=params(40),
        cost_estimate=pl.CostEstimate(
            flops=2 * tokens * width * 3 * lanes, bytes_accessed=2 * width * 3 * lanes, transcendentals=0
        ),
    )(*blocks, *(piece for piece, _, _ in pieces), taps, inside_col)


def attend_kernel(
    places, masks, w_refs, q_ref, k_ref, v_ref, ck_ref, cv_ref, inside_ref, segment_ref, slot_ref, out_refs, w_all, sems
):
    row, col = lax.axis_index("row"), lax.axis_index("col")
    shard = w_all.shape[0] // lax.axis_size("row")
    copies = []
    for i, (ref, (mask, first)) in enumerate(zip(w_refs, places)):
        start = pl.multiple_of((row ^ mask) * shard + first, 16)
        copies.append(
            pltpu.make_async_copy(ref.at[3], w_all.at[pl.ds(start, ref.shape[1])], sems.at[i])
        )
    for copy in copies:
        copy.start()
    heads, slots, lanes = ck_ref.shape
    window = slots // 8
    scale = HD ** (-0.5)
    attended = []
    for mask, out_ref in zip(masks, out_refs):
        count = out_ref.shape[0]
        begin = pl.multiple_of((col ^ mask) * count, count)
        key_begin = pl.multiple_of(jnp.maximum(begin - window, 0), window)
        key_count = count + window
        inside = inside_ref[pl.ds(begin, count), :]
        segment = segment_ref[pl.ds(begin, count), :]
        place = begin + lax.broadcasted_iota(jnp.int32, (count, 1), 0)
        first_key = jnp.maximum(place - inside, place - window + 1)
        keys = key_begin + lax.broadcasted_iota(jnp.int32, (count, key_count), 1)
        local_mask = (keys >= first_key) & (keys <= place)
        owner = lax.broadcasted_iota(jnp.int32, (count, slots), 1) // window
        cache_mask = (owner == segment) & (slot_ref[...] > inside)
        outs = []
        for h in range(heads):
            cols = slice(h * lanes, (h + 1) * lanes)
            q = q_ref[pl.ds(begin, count), cols]
            k = k_ref[pl.ds(key_begin, key_count), cols]
            v = v_ref[pl.ds(key_begin, key_count), cols]
            local = lax.dot_general(q, k, NT, preferred_element_type=jnp.float32)
            cached = lax.dot_general(q, ck_ref[h], NT, preferred_element_type=jnp.float32)
            local = jnp.where(local_mask, local * scale, -jnp.inf)
            cached = jnp.where(cache_mask, cached * scale, -jnp.inf)
            top = jnp.maximum(
                jnp.max(local, axis=-1, keepdims=True), jnp.max(cached, axis=-1, keepdims=True)
            )
            local = jnp.exp(local - top)
            cached = jnp.exp(cached - top)
            total = jnp.sum(local, axis=-1, keepdims=True) + jnp.sum(cached, axis=-1, keepdims=True)
            summed = jnp.dot(local.astype(jnp.bfloat16), v, preferred_element_type=jnp.float32)
            summed = summed + jnp.dot(
                cached.astype(jnp.bfloat16), cv_ref[h], preferred_element_type=jnp.float32
            )
            outs.append((summed / total).astype(jnp.bfloat16))
        attended.append(jnp.concatenate(outs, axis=1))
    for copy in copies:
        copy.wait()
    for block, out_ref in zip(attended, out_refs):
        out_ref[...] = lax.dot_general(
            block, w_all[...], NT, preferred_element_type=jnp.float32
        ).astype(out_ref.dtype)


def attend_call(masks, out_types, count, pieces, q, k, v, ck, cv, inside_col, segment_col, slot_row):
    places = [(mask, first) for _, mask, first in pieces]
    n_w, lanes = len(pieces), pieces[0][0].shape[2]
    width = pieces[0][0].shape[1] * lax.axis_size("row")
    n_out = len(masks)

    def body(*refs):
        w_refs = refs[:n_w]
        out_refs = refs[n_w + 8 : n_w + 8 + n_out]
        attend_kernel(places, masks, w_refs, *refs[n_w : n_w + 8], out_refs, *refs[n_w + 8 + n_out :])

    return pl.pallas_call(
        body,
        out_shape=[jax.ShapeDtypeStruct((count, width), t) for t in out_types],
        in_specs=[HBM] * n_w + [VMEM] * 8,
        out_specs=[VMEM] * n_out,
        scratch_shapes=[pltpu.VMEM((width, lanes), jnp.bfloat16), pltpu.SemaphoreType.DMA((n_w,))],
        compiler_params=params(40),
        cost_estimate=pl.CostEstimate(
            flops=n_out * 2 * count * width * lanes * 2, bytes_accessed=2 * width * lanes, transcendentals=0
        ),
    )(*(piece for piece, _, _ in pieces), q, k, v, ck, cv, inside_col, segment_col, slot_row)


def feed_kernel(n_x, hidden, x_refs, w_ref, out_refs, gate_w, up_w, down_w, sems):
    copies = [
        pltpu.make_async_copy(w_ref.at[:, pl.ds(i * hidden, hidden)], dst, sems.at[i])
        for i, dst in enumerate((gate_w, up_w, down_w))
    ]
    for copy in copies:
        copy.start()
    x = jnp.concatenate([ref[...] for ref in x_refs], axis=0) if n_x > 1 else x_refs[0][...]
    copies[0].wait()
    gate = jnp.dot(x, gate_w[...], preferred_element_type=jnp.float32)
    copies[1].wait()
    up = jnp.dot(x, up_w[...], preferred_element_type=jnp.float32)
    act = (jax.nn.silu(gate) * up).astype(jnp.bfloat16)
    copies[2].wait()
    down = lax.dot_general(act, down_w[...], NT, preferred_element_type=jnp.float32)
    count = x_refs[0].shape[0]
    for i, ref in enumerate(out_refs):
        ref[...] = down[i * count : (i + 1) * count].astype(ref.dtype)


def feed_call(blocks, weights, out_types):
    n_x, (count, width) = len(blocks), blocks[0].shape
    hidden = weights.shape[1] // 3

    def body(*refs):
        feed_kernel(n_x, hidden, refs[:n_x], refs[n_x], refs[n_x + 1 : 2 * n_x + 1], *refs[2 * n_x + 1 :])

    return pl.pallas_call(
        body,
        out_shape=[jax.ShapeDtypeStruct((count, width), t) for t in out_types],
        in_specs=[VMEM] * n_x + [HBM],
        out_specs=[VMEM] * n_x,
        scratch_shapes=[pltpu.VMEM((width, hidden), jnp.bfloat16)] * 3 + [pltpu.SemaphoreType.DMA((3,))],
        compiler_params=params(48),
        cost_estimate=pl.CostEstimate(
            flops=6 * n_x * count * width * hidden, bytes_accessed=6 * width * hidden, transcendentals=0
        ),
    )(*blocks, weights)


def pad_heads(value, heads):
    lead = value.shape[:-1]
    value = value.reshape(lead + (heads, HD))
    value = jnp.pad(value, [(0, 0)] * (len(lead) + 1) + [(0, LANES - HD)])
    return value.reshape(lead + (heads * LANES,))


def spread_tokens(block):
    two = swap(block, "col", 2)
    one = swap(block, "col", 1)
    three = swap(two, "col", 1)
    return [block, one, two, three]


def tuned(
    inputs,
    attention_norm_gain,
    query_key_value_weight,
    filter_taps,
    output_projection,
    window_key_value,
    cache_valid_length,
    lengths,
    token_adapter_index,
    adapter_down_map,
    adapter_up_map,
    feed_forward_gain,
    gate_projection,
    up_projection,
    down_projection,
):
    bf16, f32 = jnp.bfloat16, jnp.float32
    row, col = lax.axis_index("row"), lax.axis_index("col")
    count, width = inputs.shape
    tokens = count * lax.axis_size("col")
    heads = window_key_value.shape[2]

    normed = normed_rows(inputs, attention_norm_gain)
    blocks = spread_tokens(normed)

    packed = jnp.concatenate(
        [
            pad_heads(jnp.transpose(query_key_value_weight, (1, 0, 2)), heads),
            pad_heads(jnp.transpose(output_projection), heads)[None],
        ],
        axis=0,
    )
    pieces = spread_weights(packed)

    feed = jnp.concatenate([gate_projection, up_projection, jnp.transpose(down_projection)], axis=1)
    feed = lax.all_gather(feed, "row", axis=0, tiled=True)

    rank = adapter_down_map.shape[2]
    kept = adapter_down_map.shape[0]
    maps = jnp.concatenate(
        [
            jnp.transpose(adapter_down_map, (0, 2, 1)).reshape(1, kept * rank, width),
            adapter_up_map.reshape(1, kept * rank, width),
        ],
        axis=1,
    )
    for mask in (2, 4, 1):
        maps = jnp.concatenate([maps, swap(maps, "row", mask)], axis=0)
    order = jnp.array([0, 2, 4, 6, 1, 3, 5, 7], jnp.int32)
    holder = jnp.bitwise_xor(order, row)
    slots = holder[:, None] * kept + jnp.arange(kept, dtype=jnp.int32)[None, :]
    slots = jnp.repeat(slots.reshape(-1), rank)
    own_ids = lax.dynamic_slice_in_dim(token_adapter_index, col * count, count, 0)
    low = lax.dot_general(
        normed, maps[:, : kept * rank].reshape(-1, width), NT, preferred_element_type=f32
    )
    low = jnp.where(own_ids == slots[None, :], low, 0.0).astype(bf16)
    adapter_term = jnp.dot(low, maps[:, kept * rank :].reshape(-1, width), preferred_element_type=f32)
    adapter_term = adapter_term.astype(bf16)

    taps = pad_heads(filter_taps, heads).reshape(-1, heads * LANES)
    segment, inside = layout(lengths[0], tokens)
    inside_col, segment_col = inside[:, None], segment[:, None]
    requests = window_key_value.shape[0]
    window = window_key_value.shape[3] // HD
    within = jnp.arange(window, dtype=jnp.int32)[None, :]
    slot_row = jnp.where(within >= window - cache_valid_length[:, None], within, -1).reshape(1, -1)
    cache = window_key_value.reshape(requests, 2, heads, window, HD)
    cache = jnp.transpose(cache, (1, 2, 0, 3, 4)).reshape(2, heads, requests * window, HD)
    cache = jnp.pad(cache, ((0, 0), (0, 0), (0, 0), (0, LANES - HD)))

    q, k, v = qkv_call(blocks, pieces, taps, inside_col)
    rest = (count, pieces, q, k, v, cache[0], cache[1], inside_col, segment_col, slot_row)
    (part_three,) = attend_call([3], [bf16], *rest)
    passed = swap(part_three, "col", 1)
    part_two, part_one, part_own = attend_call([2, 1, 0], [bf16, bf16, f32], *rest)

    def summed_up(passed, part_two, part_one):
        part_two = (part_two.astype(f32) + passed.astype(f32)).astype(bf16)
        part_two, part_one = lax.optimization_barrier((part_two, part_one))
        return swap(part_two, "col", 2), swap(part_one, "col", 1)

    got_two, got_one = summed_up(passed, part_two, part_one)
    attn_sum = part_own + adapter_term.astype(f32) + got_one.astype(f32) + got_two.astype(f32)
    residual = (inputs.astype(f32) + attn_sum).astype(bf16)

    normed_mlp = normed_rows(residual, feed_forward_gain)
    blocks = spread_tokens(normed_mlp)
    part_two, part_one, part_own = feed_call(
        [blocks[2], blocks[1], blocks[0]], feed, [bf16, bf16, f32]
    )
    (part_three,) = feed_call([blocks[3]], feed, [bf16])
    passed = swap(part_three, "col", 1)
    got_two, got_one = summed_up(passed, part_two, part_one)
    added = part_own + got_one.astype(f32) + got_two.astype(f32)
    return (residual.astype(f32) + added).astype(bf16)


def on_device(*args):
    rows, cols = lax.axis_size("row"), lax.axis_size("col")
    if (rows, cols) == (8, 4):
        return tuned(*args)
    return plain(*args)


def solution(mesh):
    placed = (
        P(("row", "col"), None),
        P(),
        P("row", None, "col"),
        P(None, None, "col"),
        P("col", "row"),
        P("row", None, "col", None),
        P("row"),
        P("row", None),
        P("row", None),
        P("row", None, None),
        P("row", None, None),
        P(),
        P("row", "col"),
        P("row", "col"),
        P("col", "row"),
    )
    return jax.shard_map(
        on_device, mesh=mesh, in_specs=placed, out_specs=P(("row", "col"), None), check_vma=False
    )
```

```python
import functools

import jax
import jax.numpy as jnp
from jax import lax
from jax.experimental import pallas as pl
from jax.experimental.pallas import tpu as pltpu
from jax.sharding import PartitionSpec as P

HD = 112


epsilon = 1e-05


def rms_scaled(values, gain_row):
    mean_square = jnp.mean(values * values, axis=-1, keepdims=True)
    return values * lax.rsqrt(mean_square + epsilon) * gain_row


def layout(lengths_row, tok_count):
    finish = jnp.cumsum(lengths_row)
    begins = finish - lengths_row
    places = jnp.arange(tok_count, dtype=jnp.int32)
    segment = jnp.sum((places[:, None] >= finish[None, :]).astype(jnp.int32), axis=1)
    member = segment[:, None] == jnp.arange(lengths_row.shape[0], dtype=jnp.int32)[None, :]
    inside = places - jnp.sum(jnp.where(member, begins[None, :], 0), axis=1)
    return (segment, inside)


def shifted(values, offset, inside):
    moved_rows = jnp.pad(values[: values.shape[0] - offset], ((offset, 0), (0, 0)))
    return jnp.where((inside >= offset)[:, None], moved_rows, jnp.zeros_like(moved_rows))


def convolve(values, taps, inside):
    running = jnp.zeros_like(values)
    for offset in range(taps.shape[0]):
        running = running + taps[offset][None, :] * shifted(values, offset, inside)
    return running


def make_qkv(qkv_mixed, filter_taps, inside):
    queries = qkv_mixed[:, 0].astype(jnp.bfloat16)
    keys_used = convolve(qkv_mixed[:, 1], filter_taps[:, 0], inside).astype(jnp.bfloat16)
    raw_values = qkv_mixed[:, 2]
    gates = jax.nn.sigmoid(convolve(raw_values, filter_taps[:, 1], inside))
    values_used = (raw_values * gates).astype(jnp.bfloat16)
    return (queries, keys_used, values_used)


def split_cache(window_key_value, head_size):
    requests_here, head_count = (window_key_value.shape[0], window_key_value.shape[2])
    window = window_key_value.shape[3] // head_size
    split_kv = window_key_value.reshape(requests_here, 2, head_count, window, head_size)
    cached_key_rows = jnp.transpose(split_kv[:, 0], (0, 2, 1, 3)).reshape(
        requests_here * window, head_count, head_size
    )
    cached_value_rows = jnp.transpose(split_kv[:, 1], (0, 2, 1, 3)).reshape(
        requests_here * window, head_count, head_size
    )
    return (cached_key_rows, cached_value_rows, window)


def attend(
    queries,
    keys_used,
    values_used,
    window_key_value,
    segment,
    inside,
    cache_valid_length,
    head_size,
):
    tok_count = queries.shape[0]
    head_count = queries.shape[1] // head_size
    requests_here = window_key_value.shape[0]
    cached_key_rows, cached_value_rows, window = split_cache(window_key_value, head_size)
    query_per_head = queries.reshape(tok_count, head_count, head_size)
    key_h = keys_used.reshape(tok_count, head_count, head_size)
    value_per_head = values_used.reshape(tok_count, head_count, head_size)
    attention_score_scale = head_size ** (-0.5)
    places = jnp.arange(tok_count, dtype=jnp.int32)
    local_mask = (
        (segment[:, None] == segment[None, :])
        & (places[None, :] <= places[:, None])
        & (places[None, :] > places[:, None] - window)
    )
    slot_ids = jnp.arange(requests_here * window, dtype=jnp.int32)
    owner_req = slot_ids // window
    within = slot_ids % window
    slot_ages = jnp.repeat(cache_valid_length, window)
    cache_mask = (
        (segment[:, None] == owner_req[None, :])
        & (within[None, :] >= window - slot_ages[None, :])
        & (within[None, :] > inside[:, None])
    )
    local_scores = (
        jnp.einsum("thd,jhd->htj", query_per_head, key_h, preferred_element_type=jnp.float32)
        * attention_score_scale
    )
    cached_score_rows = (
        jnp.einsum(
            "sek,yek->esy", query_per_head, cached_key_rows, preferred_element_type=jnp.float32
        )
        * attention_score_scale
    )
    local_scores = jnp.where(local_mask[None], local_scores, -jnp.inf)
    cached_score_rows = jnp.where(cache_mask[None], cached_score_rows, -jnp.inf)
    row_max = jnp.maximum(
        jnp.max(local_scores, axis=-1, keepdims=True),
        jnp.max(cached_score_rows, axis=-1, keepdims=True),
    )
    local_exp = jnp.exp(local_scores - row_max)
    cache_exp = jnp.exp(cached_score_rows - row_max)
    denominator = jnp.sum(local_exp, axis=-1, keepdims=True) + jnp.sum(
        cache_exp, axis=-1, keepdims=True
    )
    window_attention_weight = (local_exp / denominator).astype(jnp.bfloat16)
    cached_attention_weight = (cache_exp / denominator).astype(jnp.bfloat16)
    joined_output = jnp.einsum(
        "zkc,czu->kzu", window_attention_weight, value_per_head, preferred_element_type=jnp.float32
    )
    joined_output = joined_output + jnp.einsum(
        "lar,rlx->alx",
        cached_attention_weight,
        cached_value_rows,
        preferred_element_type=jnp.float32,
    )
    return joined_output.reshape(tok_count, head_count * head_size).astype(jnp.bfloat16)


def plain(
    inputs,
    attention_norm_gain,
    query_key_value_weight,
    filter_taps,
    output_projection,
    window_key_value,
    cache_valid_length,
    lengths,
    token_adapter_index,
    adapter_down_map,
    adapter_up_map,
    feed_forward_gain,
    gate_projection,
    up_projection,
    down_projection,
):
    own_count = inputs.shape[0]
    column = lax.axis_index("col")
    row_count = lax.axis_size("row")
    gathered = lax.all_gather(inputs, "col", axis=0, tiled=True)
    tok_count = gathered.shape[0]
    normalized_input = rms_scaled(gathered.astype(jnp.float32), attention_norm_gain).astype(
        jnp.bfloat16
    )
    qkv_mixed = jnp.einsum(
        "td,dka->tka",
        normalized_input,
        lax.all_gather(query_key_value_weight, "row", axis=0, tiled=True),
        preferred_element_type=jnp.float32,
    )
    segment, inside = layout(lengths[0], tok_count)
    queries, keys_used, values_used = make_qkv(qkv_mixed, filter_taps, inside)
    attended = attend(
        queries, keys_used, values_used, window_key_value, segment, inside, cache_valid_length, HD
    )
    kept_count = adapter_down_map.shape[0]
    every_adapter = kept_count * row_count
    capacity = max(2, 2 * own_count // every_adapter)
    first_row = column * own_count
    own_rows = lax.dynamic_slice_in_dim(normalized_input, first_row, own_count, 0)
    own_ids = lax.dynamic_slice_in_dim(token_adapter_index[:, 0], first_row, own_count, 0)
    member = (own_ids[:, None] == jnp.arange(every_adapter, dtype=jnp.int32)[None, :]).astype(
        jnp.int32
    )
    before = jnp.cumsum(member, axis=0) - member
    slot_rank = jnp.sum(before * member, axis=1)
    target = own_ids * capacity + slot_rank
    placer = (
        target[None, :] == jnp.arange(every_adapter * capacity, dtype=jnp.int32)[:, None]
    ).astype(jnp.bfloat16)
    outgoing = jnp.dot(placer, own_rows, preferred_element_type=jnp.float32).astype(jnp.bfloat16)
    outgoing = outgoing.reshape(row_count, kept_count, capacity, normalized_input.shape[1])
    reduced_rank_input = jnp.einsum(
        "sakd,adr->sakr",
        lax.all_to_all(outgoing, "row", split_axis=0, concat_axis=0, tiled=True),
        adapter_down_map,
        preferred_element_type=jnp.float32,
    ).astype(jnp.bfloat16)
    answered = jnp.einsum(
        "zjbf,jfm->zjbm", reduced_rank_input, adapter_up_map, preferred_element_type=jnp.float32
    ).astype(jnp.bfloat16)
    returned = lax.all_to_all(answered, "row", split_axis=0, concat_axis=0, tiled=True).reshape(
        every_adapter * capacity, normalized_input.shape[1]
    )
    delta_rows = jnp.dot(jnp.transpose(placer), returned, preferred_element_type=jnp.float32)
    out_term = jnp.dot(
        attended,
        lax.all_gather(output_projection, "row", axis=1, tiled=True),
        preferred_element_type=jnp.float32,
    )
    own_term = lax.dynamic_slice_in_dim(out_term, first_row, own_count, 0) + delta_rows
    out_term = lax.dynamic_update_slice_in_dim(out_term, own_term, first_row, 0)
    attn_share = lax.psum_scatter(
        out_term.astype(jnp.bfloat16), "col", scatter_dimension=0, tiled=True
    ).astype(jnp.float32)
    residual = (inputs.astype(jnp.float32) + attn_share).astype(jnp.bfloat16)
    whole_mixed = lax.all_gather(residual, "col", axis=0, tiled=True)
    normed_mlp = rms_scaled(whole_mixed.astype(jnp.float32), feed_forward_gain).astype(jnp.bfloat16)

    def add_rows(piece):
        return jnp.dot(normed_mlp, piece, preferred_element_type=jnp.float32)

    gate = add_rows(lax.all_gather(gate_projection, "row", axis=0, tiled=True))
    up_part = add_rows(lax.all_gather(up_projection, "row", axis=0, tiled=True))
    hidden = (jax.nn.silu(gate) * up_part).astype(jnp.bfloat16)
    down_term = jnp.dot(
        hidden,
        lax.all_gather(down_projection, "row", axis=1, tiled=True),
        preferred_element_type=jnp.float32,
    )
    mlp_added = lax.psum_scatter(
        down_term.astype(jnp.bfloat16), "col", scatter_dimension=0, tiled=True
    ).astype(jnp.float32)
    return (residual.astype(jnp.float32) + mlp_added).astype(jnp.bfloat16)


LANES = 128
MIB = 1 << 20


def params(mib):
    return pltpu.CompilerParams(vmem_limit_bytes=mib * MIB)


HBM = pl.BlockSpec(memory_space=pl.ANY)
VMEM = pl.BlockSpec(memory_space=pltpu.VMEM)
SMEM = pl.BlockSpec(memory_space=pltpu.SMEM)
NT = (((1,), (1,)), ((), ()))


def normed(values, gain_ref):
    mean_square = jnp.mean(values * values, axis=-1, keepdims=True)
    return (values * lax.rsqrt(mean_square + epsilon) * gain_ref[...]).astype(jnp.bfloat16)


def pack_maps(down_ref, up_ref, packed_ref):
    ranks, width = down_ref.shape
    lanes = packed_ref.shape[1]
    for c in range(width // lanes):
        cols = slice(c * lanes, (c + 1) * lanes)
        packed_ref[2 * c * ranks : (2 * c + 1) * ranks, :] = down_ref[:, cols]
        packed_ref[(2 * c + 1) * ranks : (2 * c + 2) * ranks, :] = up_ref[:, cols]
    whole = width // lanes * lanes
    packed_ref[2 * whole // lanes * ranks :, : lanes // 2] = down_ref[:, whole:]
    packed_ref[2 * whole // lanes * ranks :, lanes // 2 :] = up_ref[:, whole:]


def unpack_maps(places, w_refs, down_ref, up_ref):
    row = lax.axis_index("row")
    ranks, width = down_ref.shape[0] // lax.axis_size("row"), down_ref.shape[1]
    lanes, step = w_refs[0].shape[2], 16
    whole = width // lanes
    for ref, (mask, first) in zip(w_refs, places):
        start = (row ^ mask) * ranks
        for at in range(0, ref.shape[1], step):
            chunk, inner = divmod(first + at, 2 * ranks)
            rows = pl.ds(pl.multiple_of(start + inner % ranks, step), step)
            cols = slice(chunk * lanes, min((chunk + 1) * lanes, width))
            if chunk < whole:
                target = down_ref if inner < ranks else up_ref
                target[rows, cols] = ref[0, at : at + step, :]
            else:
                down_ref[rows, cols] = ref[0, at : at + step, : lanes // 2]
                up_ref[rows, cols] = ref[0, at : at + step, lanes // 2 :]


def entry_kernel(
    x_hbm, gain_ref, qkv_hbm, out_hbm, taps_ref, down_ref, up_ref, normed_ref, packed_ref, padded_taps_ref, x_ref, qkv_ref, out_ref, sems
):
    loads = [
        pltpu.make_async_copy(source, target, sems.at[i])
        for i, (source, target) in enumerate(
            ((x_hbm, x_ref), (qkv_hbm, qkv_ref), (out_hbm, out_ref))
        )
    ]
    for load in loads:
        load.start()
    heads = qkv_ref.shape[2] // HD
    blank = jnp.zeros((packed_ref.shape[1], LANES - HD), jnp.bfloat16)
    pack_maps(down_ref, up_ref, packed_ref.at[4])
    for h in range(heads):
        middle = h * LANES + HD
        padded_taps_ref[:, :, h * LANES : middle] = taps_ref[:, :, h * HD : (h + 1) * HD]
        padded_taps_ref[:, :, middle : (h + 1) * LANES] = jnp.zeros(
            taps_ref.shape[:2] + (LANES - HD,), jnp.float32
        )
        for i in range(4):
            packed_ref[i, :, middle : (h + 1) * LANES] = blank
    loads[0].wait()
    normed_ref[...] = normed(x_ref[...].astype(jnp.float32), gain_ref)
    loads[1].wait()
    for h in range(heads):
        for i in range(3):
            packed_ref[i, :, h * LANES : h * LANES + HD] = qkv_ref[i, :, h * HD : (h + 1) * HD]
    loads[2].wait()
    out_rows = jnp.transpose(out_ref[...].astype(jnp.float32)).astype(jnp.bfloat16)
    for h in range(heads):
        packed_ref[3, :, h * LANES : h * LANES + HD] = out_rows[:, h * HD : (h + 1) * HD]


def entry_call(rows, gain, qkv, out, taps, down, up):
    lanes = qkv.shape[2] // HD * LANES
    return pl.pallas_call(
        entry_kernel,
        out_shape=[
            jax.ShapeDtypeStruct(rows.shape, jnp.bfloat16),
            jax.ShapeDtypeStruct((5, qkv.shape[1], lanes), jnp.bfloat16),
            jax.ShapeDtypeStruct(taps.shape[:2] + (lanes,), jnp.float32),
        ],
        in_specs=[HBM, VMEM, HBM, HBM, VMEM, VMEM, VMEM],
        out_specs=[VMEM] * 3,
        scratch_shapes=[
            pltpu.VMEM(rows.shape, rows.dtype),
            pltpu.VMEM(qkv.shape, qkv.dtype),
            pltpu.VMEM(out.shape, out.dtype),
            pltpu.SemaphoreType.DMA((3,)),
        ],
        compiler_params=params(40),
    )(rows, gain[None, :], qkv, out, taps, down, up)


def residual_kernel(x_ref, own_ref, one_ref, two_ref, gain_ref, residual_ref, normed_ref):
    total = own_ref[...] + one_ref[...].astype(jnp.float32) + two_ref[...].astype(jnp.float32)
    residual = (x_ref[...].astype(jnp.float32) + total).astype(jnp.bfloat16)
    residual_ref[...] = residual
    normed_ref[...] = normed(residual.astype(jnp.float32), gain_ref)


def residual_call(rows, own, one, two, gain):
    block = jax.ShapeDtypeStruct(rows.shape, jnp.bfloat16)
    return pl.pallas_call(
        residual_kernel,
        out_shape=[block, block],
        in_specs=[VMEM] * 5,
        out_specs=[VMEM] * 2,
        compiler_params=params(12),
    )(rows, own, one, two, gain[None, :])


def adapter_term(x_ref, ids_ref, down_ref, up_ref, rank):
    low = lax.dot_general(x_ref[...], down_ref[...], NT, preferred_element_type=jnp.float32)
    adapter = lax.broadcasted_iota(jnp.int32, low.shape, 1) // rank
    low = jnp.where(ids_ref[...] == adapter, low, 0.0).astype(jnp.bfloat16)
    return jnp.dot(low, up_ref[...], preferred_element_type=jnp.float32).astype(jnp.bfloat16)


def xor_pairs(count, mask):
    return [(i, i ^ mask) for i in range(count)]


def swap(value, axis, mask):
    return lax.ppermute(value, axis, xor_pairs(lax.axis_size(axis), mask))


def first_hops(own):
    return swap(own, "row", 2), swap(own, "row", 4)


def second_hops(own, from_x, from_y):
    half = own.shape[1] // 2
    diagonal = swap(from_x[:, :half], "row", 4), swap(from_y[:, half:], "row", 2)
    return diagonal + tuple(swap(piece, "row", 1) for piece in (own, from_x, from_y))


def named_pieces(own, firsts, seconds, thirds):
    half = own.shape[1] // 2
    masks = [(0, 0), (2, 0), (4, 0), (6, 0), (6, half), (1, 0), (3, 0), (5, 0), (7, 0), (7, half)]
    return [(piece, *at) for piece, at in zip((own,) + firsts + seconds + thirds, masks)]


def assemble(places, w_refs, all_w):
    row = lax.axis_index("row")
    shard = all_w.shape[1] // lax.axis_size("row")
    for ref, (mask, first) in zip(w_refs, places):
        start = pl.multiple_of((row ^ mask) * shard + first, 16)
        for part in range(ref.shape[0]):
            all_w[part, pl.ds(start, ref.shape[1]), :] = ref[part]


def request_columns(lengths_ref, begin, count):
    place = begin + lax.broadcasted_iota(jnp.int32, (count, 1), 0)
    segment, first = jnp.zeros_like(place), jnp.zeros_like(place)
    finish = jnp.int32(0)
    for s in range(lengths_ref.shape[1]):
        finish = finish + lengths_ref[0, s]
        later = place >= finish
        segment = segment + later.astype(jnp.int32)
        first = jnp.where(later, finish, first)
    return place, segment, first


def attend_block(mask, count, lengths_ref, valid_ref, q_ref, k_ref, v_ref, cache_ref):
    col = lax.axis_index("col")
    _, heads, slots, lanes = cache_ref.shape
    requests = valid_ref.shape[0]
    window = slots // requests
    scale = HD ** (-0.5)
    begin = pl.multiple_of((col ^ mask) * count, count)
    key_begin = pl.multiple_of(jnp.maximum(begin - window, 0), window)
    key_count = count + window
    place, segment, first = request_columns(lengths_ref, begin, count)
    first_key = jnp.maximum(first, place - window + 1)
    keys = key_begin + lax.broadcasted_iota(jnp.int32, (count, key_count), 1)
    local_mask = (keys >= first_key) & (keys <= place)
    slot = lax.broadcasted_iota(jnp.int32, (1, slots), 1)
    owner, within = slot // window, slot % window
    oldest = jnp.full_like(slot, window)
    for s in range(requests):
        oldest = jnp.where(owner == s, window - valid_ref[s], oldest)
    within = jnp.where(within >= oldest, within, -1)
    cache_mask = (owner == segment) & (within > place - first)
    outs = []
    for h in range(heads):
        cols = slice(h * lanes, (h + 1) * lanes)
        q = q_ref[pl.ds(begin, count), cols]
        k = k_ref[pl.ds(key_begin, key_count), cols]
        v = v_ref[pl.ds(key_begin, key_count), cols]
        local = lax.dot_general(q, k, NT, preferred_element_type=jnp.float32)
        cached = lax.dot_general(q, cache_ref[0, h], NT, preferred_element_type=jnp.float32)
        local = jnp.where(local_mask, local * scale, -jnp.inf)
        cached = jnp.where(cache_mask, cached * scale, -jnp.inf)
        top = jnp.maximum(
            jnp.max(local, axis=-1, keepdims=True), jnp.max(cached, axis=-1, keepdims=True)
        )
        local = jnp.exp(local - top)
        cached = jnp.exp(cached - top)
        total = jnp.sum(local, axis=-1, keepdims=True) + jnp.sum(cached, axis=-1, keepdims=True)
        summed = jnp.dot(local.astype(jnp.bfloat16), v, preferred_element_type=jnp.float32)
        summed = summed + jnp.dot(
            cached.astype(jnp.bfloat16), cache_ref[1, h], preferred_element_type=jnp.float32
        )
        outs.append((summed / total).astype(jnp.bfloat16))
    return jnp.concatenate(outs, axis=1)


def first_kernel(places, n_x, n_w, *refs):
    x_refs, w_refs = refs[:n_x], refs[n_x : n_x + n_w]
    taps_ref, lengths_ref, valid_ref, cache_ref = refs[n_x + n_w : n_x + n_w + 4]
    q_ref, k_ref, v_ref, out_w, down_ref, up_ref, part_ref = refs[n_x + n_w + 4 : n_x + n_w + 11]
    x_all, w_all, padded = refs[n_x + n_w + 11 :]
    col = lax.axis_index("col")
    count, tokens = x_refs[0].shape[0], x_all.shape[0]
    for i, ref in enumerate(x_refs):
        x_all[pl.ds(pl.multiple_of((col ^ i) * count, 16), count), :] = ref[...]
    assemble(places, [ref.at[pl.ds(0, 3)] for ref in w_refs], w_all)
    assemble(places, [ref.at[pl.ds(3, 1)] for ref in w_refs], out_w)
    unpack_maps(places, [ref.at[pl.ds(4, 1)] for ref in w_refs], down_ref, up_ref)
    padded[0:8, :] = jnp.zeros((8, padded.shape[1]), jnp.float32)
    place, _, first = request_columns(lengths_ref, 0, tokens)
    inside = place - first

    def mixed(which):
        return jnp.dot(x_all[...], w_all[which], preferred_element_type=jnp.float32)

    def convolved(raw, which):
        padded[8:, :] = raw
        running = taps_ref[0, which : which + 1, :] * raw
        for offset in range(1, taps_ref.shape[0]):
            moved = padded[8 - offset : 8 - offset + tokens, :]
            tap = taps_ref[offset, which : which + 1, :]
            running = running + jnp.where(inside >= offset, tap * moved, 0.0)
        return running

    q_ref[...] = mixed(0).astype(jnp.bfloat16)
    k_ref[...] = convolved(mixed(1), 0).astype(jnp.bfloat16)
    raw_values = mixed(2)
    v_ref[...] = (raw_values * jax.nn.sigmoid(convolved(raw_values, 1))).astype(jnp.bfloat16)
    attended = attend_block(n_x - 1, count, lengths_ref, valid_ref, q_ref, k_ref, v_ref, cache_ref)
    part_ref[...] = lax.dot_general(
        attended, out_w[0], NT, preferred_element_type=jnp.float32
    ).astype(jnp.bfloat16)


def first_call(blocks, pieces, ranks, taps, lengths, valid, cache):
    (count, width), n_x, n_w = blocks[0].shape, len(blocks), len(pieces)
    tokens, lanes = count * n_x, pieces[0][0].shape[2]
    places = [(mask, first) for _, mask, first in pieces]
    one = jax.ShapeDtypeStruct((tokens, lanes), jnp.bfloat16)
    return pl.pallas_call(
        functools.partial(first_kernel, places, n_x, n_w),
        out_shape=[
            one,
            one,
            one,
            jax.ShapeDtypeStruct((1, width, lanes), jnp.bfloat16),
            jax.ShapeDtypeStruct((ranks, width), jnp.bfloat16),
            jax.ShapeDtypeStruct((ranks, width), jnp.bfloat16),
            jax.ShapeDtypeStruct((count, width), jnp.bfloat16),
        ],
        in_specs=[VMEM] * (n_x + n_w + 1) + [SMEM, SMEM, VMEM],
        out_specs=[VMEM] * 7,
        scratch_shapes=[
            pltpu.VMEM((tokens, width), jnp.bfloat16),
            pltpu.VMEM((3, width, lanes), jnp.bfloat16),
            pltpu.VMEM((tokens + 8, lanes), jnp.float32),
        ],
        compiler_params=params(36),
        cost_estimate=pl.CostEstimate(
            flops=2 * tokens * width * 4 * lanes, bytes_accessed=2 * width * 4 * lanes, transcendentals=0
        ),
    )(*blocks, *(piece for piece, _, _ in pieces), taps, lengths, valid, cache)


def attend_kernel(rank, masks, q_ref, k_ref, v_ref, out_w, x_ref, ids_ref, down_ref, up_ref, *refs):
    lengths_ref, valid_ref, cache_ref = refs[:3]
    for mask, out_ref in zip(masks, refs[3:]):
        attended = attend_block(
            mask, out_ref.shape[0], lengths_ref, valid_ref, q_ref, k_ref, v_ref, cache_ref
        )
        part = lax.dot_general(attended, out_w[0], NT, preferred_element_type=jnp.float32)
        if mask == 0:
            part = part + adapter_term(x_ref, ids_ref, down_ref, up_ref, rank).astype(jnp.float32)
        out_ref[...] = part.astype(out_ref.dtype)


def attend_call(rank, masks, out_types, q, k, v, out_w, x, ids, down, up, lengths, valid, cache):
    _, width, lanes = out_w.shape
    count = x.shape[0]
    return pl.pallas_call(
        functools.partial(attend_kernel, rank, masks),
        out_shape=[jax.ShapeDtypeStruct((count, width), t) for t in out_types],
        in_specs=[VMEM] * 8 + [SMEM, SMEM, VMEM],
        out_specs=[VMEM] * len(masks),
        compiler_params=params(20),
        cost_estimate=pl.CostEstimate(
            flops=len(masks) * 16 * count * width * lanes, bytes_accessed=2 * width * lanes, transcendentals=0
        ),
    )(q, k, v, out_w, x, ids, down, up, lengths, valid, cache)


def feed(x, all_w):
    gate = jnp.dot(x, all_w[0], preferred_element_type=jnp.float32)
    up = jnp.dot(x, all_w[1], preferred_element_type=jnp.float32)
    act = (jax.nn.silu(gate) * up).astype(jnp.bfloat16)
    return lax.dot_general(act, all_w[2], NT, preferred_element_type=jnp.float32)


def feed_first_kernel(places, n_x, n_w, *refs):
    x_refs, w_refs = refs[:n_x], refs[n_x : n_x + n_w]
    all_w, out_refs = refs[n_x + n_w], refs[n_x + n_w + 1 :]
    assemble(places, w_refs, all_w)
    down = feed(jnp.concatenate([ref[...] for ref in x_refs], axis=0), all_w)
    count = x_refs[0].shape[0]
    for i, ref in enumerate(out_refs):
        ref[...] = down[i * count : (i + 1) * count].astype(ref.dtype)


def feed_first_call(blocks, pieces, out_types):
    n_x, n_w, (count, width) = len(blocks), len(pieces), blocks[0].shape
    places = [(mask, first) for _, mask, first in pieces]
    hidden = pieces[0][0].shape[2]
    return pl.pallas_call(
        functools.partial(feed_first_kernel, places, n_x, n_w),
        out_shape=[pltpu.VMEM((3, width, hidden), jnp.bfloat16)]
        + [jax.ShapeDtypeStruct((count, width), t) for t in out_types],
        in_specs=[VMEM] * (n_x + n_w),
        out_specs=[VMEM] * (n_x + 1),
        compiler_params=params(40),
        cost_estimate=pl.CostEstimate(
            flops=6 * n_x * count * width * hidden, bytes_accessed=12 * width * hidden, transcendentals=0
        ),
    )(*blocks, *(piece for piece, _, _ in pieces))


def feed_last_kernel(x_ref, all_w, out_ref):
    out_ref[...] = feed(x_ref[...], all_w).astype(out_ref.dtype)


def feed_last_call(block, all_w):
    count, (_, width, hidden) = block.shape[0], all_w.shape
    return pl.pallas_call(
        feed_last_kernel,
        out_shape=jax.ShapeDtypeStruct((count, width), jnp.bfloat16),
        in_specs=[VMEM] * 2,
        out_specs=VMEM,
        compiler_params=params(20),
        cost_estimate=pl.CostEstimate(
            flops=6 * count * width * hidden, bytes_accessed=6 * width * hidden, transcendentals=0
        ),
    )(block, all_w)


def tuned(
    inputs,
    attention_norm_gain,
    query_key_value_weight,
    filter_taps,
    output_projection,
    window_key_value,
    cache_valid_length,
    lengths,
    token_adapter_index,
    adapter_down_map,
    adapter_up_map,
    feed_forward_gain,
    gate_projection,
    up_projection,
    down_projection,
):
    bf16, f32 = jnp.bfloat16, jnp.float32
    col = lax.axis_index("col")
    count, width = inputs.shape
    heads = window_key_value.shape[2]

    rank, kept = adapter_down_map.shape[2], adapter_down_map.shape[0]
    ranks = kept * lax.axis_size("row") * rank
    normed_attention, packed, taps = entry_call(
        inputs,
        attention_norm_gain,
        jnp.transpose(query_key_value_weight, (1, 0, 2)),
        output_projection,
        filter_taps,
        jnp.transpose(adapter_down_map, (0, 2, 1)).reshape(kept * rank, width),
        adapter_up_map.reshape(kept * rank, width),
    )
    token_two, token_one = swap(normed_attention, "col", 2), swap(normed_attention, "col", 1)
    firsts = first_hops(packed)
    requests = window_key_value.shape[0]
    window = window_key_value.shape[3] // HD
    cache = window_key_value.reshape(requests, 2, heads, window, HD)
    cache = jnp.transpose(cache, (1, 2, 0, 3, 4)).reshape(2, heads, requests * window, HD)
    cache = jnp.pad(cache, ((0, 0), (0, 0), (0, 0), (0, LANES - HD)))
    own_ids = lax.dynamic_slice_in_dim(token_adapter_index, col * count, count, 0)
    feed_own = jnp.concatenate(
        [gate_projection[None], up_projection[None], jnp.transpose(down_projection)[None]], axis=0
    )
    token_two, token_one, firsts, packed, cache, own_ids, feed_own = lax.optimization_barrier(
        (token_two, token_one, firsts, packed, cache, own_ids, feed_own)
    )
    token_three = swap(token_two, "col", 1)
    seconds = second_hops(packed, *firsts)
    token_three, diagonal, feed_own = lax.optimization_barrier((token_three, seconds[:2], feed_own))
    thirds = tuple(swap(piece, "row", 1) for piece in diagonal)
    feed_firsts = first_hops(feed_own)

    pieces = named_pieces(packed, firsts, diagonal + seconds[2:], thirds)
    blocks = [normed_attention, token_one, token_two, token_three]
    requests_here = (lengths, cache_valid_length, cache)
    q, k, v, out_w, down_maps, up_maps, part_three = first_call(
        blocks, pieces, ranks, taps, *requests_here
    )
    passed = swap(part_three, "col", 1)
    part_two, part_one, part_own = attend_call(
        rank, [2, 1, 0], [bf16, bf16, f32], q, k, v, out_w, normed_attention, own_ids, down_maps, up_maps, *requests_here
    )

    def summed_up(passed, part_two, part_one):
        part_two = (part_two.astype(f32) + passed.astype(f32)).astype(bf16)
        part_two, part_one = lax.optimization_barrier((part_two, part_one))
        return swap(part_two, "col", 2), swap(part_one, "col", 1)

    passed, part_two, part_one = lax.optimization_barrier((passed, part_two, part_one))
    got_two, got_one = summed_up(passed, part_two, part_one)
    got_one, feed_own, feed_firsts = lax.optimization_barrier((got_one, feed_own, feed_firsts))
    feed_seconds = second_hops(feed_own, *feed_firsts)
    residual, normed_mlp = residual_call(inputs, part_own, got_one, got_two, feed_forward_gain)
    token_two, token_one = swap(normed_mlp, "col", 2), swap(normed_mlp, "col", 1)
    feed_diagonal = feed_seconds[:2]
    feed_thirds = tuple(swap(piece, "row", 1) for piece in feed_diagonal)
    token_two, token_one, feed_thirds, feed_seconds = lax.optimization_barrier(
        (token_two, token_one, feed_thirds, feed_seconds[2:])
    )
    token_three = swap(token_two, "col", 1)
    feed_pieces = named_pieces(feed_own, feed_firsts, feed_diagonal + feed_seconds, feed_thirds)
    feed_w, part_two, part_one, part_own = feed_first_call(
        [token_two, token_one, normed_mlp], feed_pieces, [bf16, bf16, f32]
    )
    part_three = feed_last_call(token_three, feed_w)
    passed = swap(part_three, "col", 1)
    got_two, got_one = summed_up(passed, part_two, part_one)
    added = part_own + got_one.astype(f32) + got_two.astype(f32)
    return (residual.astype(f32) + added).astype(bf16)


def on_device(*args):
    rows, cols = lax.axis_size("row"), lax.axis_size("col")
    if (rows, cols) == (8, 4):
        return tuned(*args)
    return plain(*args)


def solution(mesh):
    placed = (
        P(("row", "col"), None),
        P(),
        P("row", None, "col"),
        P(None, None, "col"),
        P("col", "row"),
        P("row", None, "col", None),
        P("row"),
        P("row", None),
        P("row", None),
        P("row", None, None),
        P("row", None, None),
        P(),
        P("row", "col"),
        P("row", "col"),
        P("col", "row"),
    )
    return jax.shard_map(
        on_device, mesh=mesh, in_specs=placed, out_specs=P(("row", "col"), None), check_vma=False
    )
```

```python
import functools

import jax
import jax.numpy as jnp
from jax import lax
from jax.experimental import pallas as pl
from jax.experimental.pallas import tpu as pltpu
from jax.sharding import PartitionSpec as P

HD = 112


epsilon = 1e-05


def rms_scaled(values, gain_row):
    mean_square = jnp.mean(values * values, axis=-1, keepdims=True)
    return values * lax.rsqrt(mean_square + epsilon) * gain_row


def layout(lengths_row, tok_count):
    finish = jnp.cumsum(lengths_row)
    begins = finish - lengths_row
    places = jnp.arange(tok_count, dtype=jnp.int32)
    segment = jnp.sum((places[:, None] >= finish[None, :]).astype(jnp.int32), axis=1)
    member = segment[:, None] == jnp.arange(lengths_row.shape[0], dtype=jnp.int32)[None, :]
    inside = places - jnp.sum(jnp.where(member, begins[None, :], 0), axis=1)
    return (segment, inside)


def shifted(values, offset, inside):
    moved_rows = jnp.pad(values[: values.shape[0] - offset], ((offset, 0), (0, 0)))
    return jnp.where((inside >= offset)[:, None], moved_rows, jnp.zeros_like(moved_rows))


def convolve(values, taps, inside):
    running = jnp.zeros_like(values)
    for offset in range(taps.shape[0]):
        running = running + taps[offset][None, :] * shifted(values, offset, inside)
    return running


def make_qkv(qkv_mixed, filter_taps, inside):
    queries = qkv_mixed[:, 0].astype(jnp.bfloat16)
    keys_used = convolve(qkv_mixed[:, 1], filter_taps[:, 0], inside).astype(jnp.bfloat16)
    raw_values = qkv_mixed[:, 2]
    gates = jax.nn.sigmoid(convolve(raw_values, filter_taps[:, 1], inside))
    values_used = (raw_values * gates).astype(jnp.bfloat16)
    return (queries, keys_used, values_used)


def split_cache(window_key_value, head_size):
    requests_here, head_count = (window_key_value.shape[0], window_key_value.shape[2])
    window = window_key_value.shape[3] // head_size
    split_kv = window_key_value.reshape(requests_here, 2, head_count, window, head_size)
    cached_key_rows = jnp.transpose(split_kv[:, 0], (0, 2, 1, 3)).reshape(
        requests_here * window, head_count, head_size
    )
    cached_value_rows = jnp.transpose(split_kv[:, 1], (0, 2, 1, 3)).reshape(
        requests_here * window, head_count, head_size
    )
    return (cached_key_rows, cached_value_rows, window)


def attend(
    queries,
    keys_used,
    values_used,
    window_key_value,
    segment,
    inside,
    cache_valid_length,
    head_size,
):
    tok_count = queries.shape[0]
    head_count = queries.shape[1] // head_size
    requests_here = window_key_value.shape[0]
    cached_key_rows, cached_value_rows, window = split_cache(window_key_value, head_size)
    query_per_head = queries.reshape(tok_count, head_count, head_size)
    key_h = keys_used.reshape(tok_count, head_count, head_size)
    value_per_head = values_used.reshape(tok_count, head_count, head_size)
    attention_score_scale = head_size ** (-0.5)
    places = jnp.arange(tok_count, dtype=jnp.int32)
    local_mask = (
        (segment[:, None] == segment[None, :])
        & (places[None, :] <= places[:, None])
        & (places[None, :] > places[:, None] - window)
    )
    slot_ids = jnp.arange(requests_here * window, dtype=jnp.int32)
    owner_req = slot_ids // window
    within = slot_ids % window
    slot_ages = jnp.repeat(cache_valid_length, window)
    cache_mask = (
        (segment[:, None] == owner_req[None, :])
        & (within[None, :] >= window - slot_ages[None, :])
        & (within[None, :] > inside[:, None])
    )
    local_scores = (
        jnp.einsum("thd,jhd->htj", query_per_head, key_h, preferred_element_type=jnp.float32)
        * attention_score_scale
    )
    cached_score_rows = (
        jnp.einsum(
            "sek,yek->esy", query_per_head, cached_key_rows, preferred_element_type=jnp.float32
        )
        * attention_score_scale
    )
    local_scores = jnp.where(local_mask[None], local_scores, -jnp.inf)
    cached_score_rows = jnp.where(cache_mask[None], cached_score_rows, -jnp.inf)
    row_max = jnp.maximum(
        jnp.max(local_scores, axis=-1, keepdims=True),
        jnp.max(cached_score_rows, axis=-1, keepdims=True),
    )
    local_exp = jnp.exp(local_scores - row_max)
    cache_exp = jnp.exp(cached_score_rows - row_max)
    denominator = jnp.sum(local_exp, axis=-1, keepdims=True) + jnp.sum(
        cache_exp, axis=-1, keepdims=True
    )
    window_attention_weight = (local_exp / denominator).astype(jnp.bfloat16)
    cached_attention_weight = (cache_exp / denominator).astype(jnp.bfloat16)
    joined_output = jnp.einsum(
        "zkc,czu->kzu", window_attention_weight, value_per_head, preferred_element_type=jnp.float32
    )
    joined_output = joined_output + jnp.einsum(
        "lar,rlx->alx",
        cached_attention_weight,
        cached_value_rows,
        preferred_element_type=jnp.float32,
    )
    return joined_output.reshape(tok_count, head_count * head_size).astype(jnp.bfloat16)


def plain(
    inputs,
    attention_norm_gain,
    query_key_value_weight,
    filter_taps,
    output_projection,
    window_key_value,
    cache_valid_length,
    lengths,
    token_adapter_index,
    adapter_down_map,
    adapter_up_map,
    feed_forward_gain,
    gate_projection,
    up_projection,
    down_projection,
):
    own_count = inputs.shape[0]
    column = lax.axis_index("col")
    row_count = lax.axis_size("row")
    gathered = lax.all_gather(inputs, "col", axis=0, tiled=True)
    tok_count = gathered.shape[0]
    normalized_input = rms_scaled(gathered.astype(jnp.float32), attention_norm_gain).astype(
        jnp.bfloat16
    )
    qkv_mixed = jnp.einsum(
        "td,dka->tka",
        normalized_input,
        lax.all_gather(query_key_value_weight, "row", axis=0, tiled=True),
        preferred_element_type=jnp.float32,
    )
    segment, inside = layout(lengths[0], tok_count)
    queries, keys_used, values_used = make_qkv(qkv_mixed, filter_taps, inside)
    attended = attend(
        queries, keys_used, values_used, window_key_value, segment, inside, cache_valid_length, HD
    )
    kept_count = adapter_down_map.shape[0]
    every_adapter = kept_count * row_count
    capacity = max(2, 2 * own_count // every_adapter)
    first_row = column * own_count
    own_rows = lax.dynamic_slice_in_dim(normalized_input, first_row, own_count, 0)
    own_ids = lax.dynamic_slice_in_dim(token_adapter_index[:, 0], first_row, own_count, 0)
    member = (own_ids[:, None] == jnp.arange(every_adapter, dtype=jnp.int32)[None, :]).astype(
        jnp.int32
    )
    before = jnp.cumsum(member, axis=0) - member
    slot_rank = jnp.sum(before * member, axis=1)
    target = own_ids * capacity + slot_rank
    placer = (
        target[None, :] == jnp.arange(every_adapter * capacity, dtype=jnp.int32)[:, None]
    ).astype(jnp.bfloat16)
    outgoing = jnp.dot(placer, own_rows, preferred_element_type=jnp.float32).astype(jnp.bfloat16)
    outgoing = outgoing.reshape(row_count, kept_count, capacity, normalized_input.shape[1])
    reduced_rank_input = jnp.einsum(
        "sakd,adr->sakr",
        lax.all_to_all(outgoing, "row", split_axis=0, concat_axis=0, tiled=True),
        adapter_down_map,
        preferred_element_type=jnp.float32,
    ).astype(jnp.bfloat16)
    answered = jnp.einsum(
        "zjbf,jfm->zjbm", reduced_rank_input, adapter_up_map, preferred_element_type=jnp.float32
    ).astype(jnp.bfloat16)
    returned = lax.all_to_all(answered, "row", split_axis=0, concat_axis=0, tiled=True).reshape(
        every_adapter * capacity, normalized_input.shape[1]
    )
    delta_rows = jnp.dot(jnp.transpose(placer), returned, preferred_element_type=jnp.float32)
    out_term = jnp.dot(
        attended,
        lax.all_gather(output_projection, "row", axis=1, tiled=True),
        preferred_element_type=jnp.float32,
    )
    own_term = lax.dynamic_slice_in_dim(out_term, first_row, own_count, 0) + delta_rows
    out_term = lax.dynamic_update_slice_in_dim(out_term, own_term, first_row, 0)
    attn_share = lax.psum_scatter(
        out_term.astype(jnp.bfloat16), "col", scatter_dimension=0, tiled=True
    ).astype(jnp.float32)
    residual = (inputs.astype(jnp.float32) + attn_share).astype(jnp.bfloat16)
    whole_mixed = lax.all_gather(residual, "col", axis=0, tiled=True)
    normed_mlp = rms_scaled(whole_mixed.astype(jnp.float32), feed_forward_gain).astype(jnp.bfloat16)

    def add_rows(piece):
        return jnp.dot(normed_mlp, piece, preferred_element_type=jnp.float32)

    gate = add_rows(lax.all_gather(gate_projection, "row", axis=0, tiled=True))
    up_part = add_rows(lax.all_gather(up_projection, "row", axis=0, tiled=True))
    hidden = (jax.nn.silu(gate) * up_part).astype(jnp.bfloat16)
    down_term = jnp.dot(
        hidden,
        lax.all_gather(down_projection, "row", axis=1, tiled=True),
        preferred_element_type=jnp.float32,
    )
    mlp_added = lax.psum_scatter(
        down_term.astype(jnp.bfloat16), "col", scatter_dimension=0, tiled=True
    ).astype(jnp.float32)
    return (residual.astype(jnp.float32) + mlp_added).astype(jnp.bfloat16)


LANES = 128
MIB = 1 << 20


LIGHT = pl.CostEstimate(flops=1, bytes_accessed=1, transcendentals=0)


def params(mib):
    return pltpu.CompilerParams(vmem_limit_bytes=mib * MIB)


HBM = pl.BlockSpec(memory_space=pl.ANY)
VMEM = pl.BlockSpec(memory_space=pltpu.VMEM)
SMEM = pl.BlockSpec(memory_space=pltpu.SMEM)
NT = (((1,), (1,)), ((), ()))


def normed(values, gain_ref):
    mean_square = jnp.mean(values * values, axis=-1, keepdims=True)
    return (values * lax.rsqrt(mean_square + epsilon) * gain_ref[...]).astype(jnp.bfloat16)


def entry_kernel(*refs):
    sources, (normed_ref, packed_ref) = refs[:6], refs[6:8]
    targets, sems = refs[8:14], refs[14]
    loads = [
        pltpu.make_async_copy(source, target, sems.at[i])
        for i, (source, target) in enumerate(zip(sources, targets))
    ]
    for load in loads:
        load.start()
    x_ref, qkv_ref, out_ref, gain_ref, down_ref, up_ref = targets
    rows, part, ranks = qkv_ref.shape[1], qkv_ref.shape[2], down_ref.shape[0]
    for load in loads:
        load.wait()
    normed_ref[...] = normed(x_ref[...].astype(jnp.float32), gain_ref)
    for place, which in enumerate((1, 0, 2)):
        packed_ref[:rows, place * part : (place + 1) * part] = qkv_ref[which]
    out_rows = jnp.transpose(out_ref[...].astype(jnp.float32)).astype(jnp.bfloat16)
    packed_ref[:rows, 3 * part :] = out_rows
    packed_ref[rows : rows + ranks, :] = down_ref[...]
    packed_ref[rows + ranks :, :] = up_ref[...]


def entry_call(rows, qkv, out, gain, down, up):
    sources = (rows, qkv, out, gain[None, :], down, up)
    return pl.pallas_call(
        entry_kernel,
        out_shape=[
            jax.ShapeDtypeStruct(rows.shape, jnp.bfloat16),
            jax.ShapeDtypeStruct((qkv.shape[1] + 2 * down.shape[0], 4 * qkv.shape[2]), jnp.bfloat16),
        ],
        in_specs=[HBM] * len(sources),
        out_specs=[VMEM] * 2,
        scratch_shapes=[pltpu.VMEM(source.shape, source.dtype) for source in sources]
        + [pltpu.SemaphoreType.DMA((len(sources),))],
        compiler_params=params(60),
        cost_estimate=LIGHT,
    )(*sources)


def residual_kernel(x_ref, own_ref, two_ref, one_ref, gain_ref, residual_ref, normed_ref):
    total = own_ref[...] + one_ref[...].astype(jnp.float32) + two_ref[...].astype(jnp.float32)
    residual = (x_ref[...].astype(jnp.float32) + total).astype(jnp.bfloat16)
    residual_ref[...] = residual
    normed_ref[...] = normed(residual.astype(jnp.float32), gain_ref)


def residual_call(rows, own, two, one, gain):
    block = jax.ShapeDtypeStruct(rows.shape, jnp.bfloat16)
    return pl.pallas_call(
        residual_kernel,
        out_shape=[block, block],
        in_specs=[VMEM] * 5,
        out_specs=[VMEM] * 2,
        compiler_params=params(12),
        cost_estimate=LIGHT,
    )(rows, own, two, one, gain[None, :])


def adapter_term(x_ref, ids_ref, down_ref, up_ref, rank):
    low = lax.dot_general(x_ref[...], down_ref[...], NT, preferred_element_type=jnp.float32)
    adapter = lax.broadcasted_iota(jnp.int32, low.shape, 1) // rank
    low = jnp.where(ids_ref[...] == adapter, low, 0.0).astype(jnp.bfloat16)
    return jnp.dot(low, up_ref[...], preferred_element_type=jnp.float32).astype(jnp.bfloat16)


def xor_pairs(count, mask):
    return [(i, i ^ mask) for i in range(count)]


def swap(value, axis, mask):
    return lax.ppermute(value, axis, xor_pairs(lax.axis_size(axis), mask))


def first_hops(own):
    return swap(own, "row", 2), swap(own, "row", 4)


def second_hops(own, from_x, from_y):
    half = own.shape[-2] // 2
    diagonal = swap(from_x[..., :half, :], "row", 4), swap(from_y[..., half:, :], "row", 2)
    return diagonal + tuple(swap(piece, "row", 1) for piece in (own, from_x, from_y))


def named_pieces(own, firsts, seconds, thirds):
    half = own.shape[-2] // 2
    masks = [(0, 0), (2, 0), (4, 0), (6, 0), (6, half), (1, 0), (3, 0), (5, 0), (7, 0), (7, half)]
    return [(piece, *at) for piece, at in zip((own,) + firsts + seconds + thirds, masks)]


def shard_starts(places, shard):
    row = lax.axis_index("row")
    return [pl.multiple_of((row ^ mask) * shard + first, 16) for mask, first in places]


def request_columns(lengths_ref, begin, count):
    place = begin + lax.broadcasted_iota(jnp.int32, (count, 1), 0)
    segment, first = jnp.zeros_like(place), jnp.zeros_like(place)
    finish = jnp.int32(0)
    for s in range(lengths_ref.shape[1]):
        finish = finish + lengths_ref[0, s]
        later = place >= finish
        segment = segment + later.astype(jnp.int32)
        first = jnp.where(later, finish, first)
    return place, segment, first


def attend_block(mask, count, lengths_ref, valid_ref, q_ref, k_ref, v_ref, cache_ref):
    col = lax.axis_index("col")
    _, heads, slots, lanes = cache_ref.shape
    requests = valid_ref.shape[0]
    window = slots // requests
    scale = HD ** (-0.5)
    begin = pl.multiple_of((col ^ mask) * count, count)
    key_begin = pl.multiple_of(jnp.maximum(begin - window, 0), window)
    key_count = count + window
    place, segment, first = request_columns(lengths_ref, begin, count)
    first_key = jnp.maximum(first, place - window + 1)
    keys = key_begin + lax.broadcasted_iota(jnp.int32, (count, key_count), 1)
    local_mask = (keys >= first_key) & (keys <= place)
    slot = lax.broadcasted_iota(jnp.int32, (1, slots), 1)
    owner, within = slot // window, slot % window
    oldest = jnp.full_like(slot, window)
    for s in range(requests):
        oldest = jnp.where(owner == s, window - valid_ref[s], oldest)
    within = jnp.where(within >= oldest, within, -1)
    cache_mask = (owner == segment) & (within > place - first)
    outs = []
    for h in range(heads):
        cols = slice(h * lanes, (h + 1) * lanes)
        q = q_ref[pl.ds(begin, count), cols]
        k = k_ref[pl.ds(key_begin, key_count), cols]
        v = v_ref[pl.ds(key_begin, key_count), cols]
        local = lax.dot_general(q, k, NT, preferred_element_type=jnp.float32)
        cached = lax.dot_general(q, cache_ref[0, h], NT, preferred_element_type=jnp.float32)
        local = jnp.where(local_mask, local * scale, -jnp.inf)
        cached = jnp.where(cache_mask, cached * scale, -jnp.inf)
        top = jnp.maximum(
            jnp.max(local, axis=-1, keepdims=True), jnp.max(cached, axis=-1, keepdims=True)
        )
        local = jnp.exp(local - top)
        cached = jnp.exp(cached - top)
        total = jnp.sum(local, axis=-1, keepdims=True) + jnp.sum(cached, axis=-1, keepdims=True)
        summed = jnp.dot(local.astype(jnp.bfloat16), v, preferred_element_type=jnp.float32)
        summed = summed + jnp.dot(
            cached.astype(jnp.bfloat16), cache_ref[1, h], preferred_element_type=jnp.float32
        )
        outs.append((summed / total).astype(jnp.bfloat16)[:, :HD])
    blank = jnp.zeros((count, heads * (lanes - HD)), jnp.bfloat16)
    return jnp.concatenate([blank] + outs, axis=1)


def first_kernel(places, n_x, n_w, *refs):
    x_refs, w_refs = refs[:n_x], refs[n_x : n_x + n_w]
    taps_ref, lengths_ref, valid_ref, cache_ref = refs[n_x + n_w : n_x + n_w + 4]
    q_ref, k_ref, v_ref, out_w, down_ref, up_ref, part_ref = refs[n_x + n_w + 4 : n_x + n_w + 11]
    x_all, w_all, padded = refs[n_x + n_w + 11 :]
    col = lax.axis_index("col")
    count, (tokens, width) = x_refs[0].shape[0], x_all.shape
    part, lanes = taps_ref.shape[2], q_ref.shape[1]
    mixed_lanes = w_all.shape[1]
    for i, ref in enumerate(x_refs):
        x_all[pl.ds(pl.multiple_of((col ^ i) * count, 16), count), :] = ref[...]
    shard = width // lax.axis_size("row")
    ranks = down_ref.shape[0] // lax.axis_size("row")
    starts = shard_starts(places, shard)
    for ref, start, (mask, first) in zip(w_refs, starts, places):
        rows = min(ref.shape[0], shard - first)
        w_all[pl.ds(start, rows), :] = ref[:rows, :mixed_lanes]
        out_w[pl.ds(start, rows), :] = ref[:rows, ref.shape[1] - lanes :]
        if rows < ref.shape[0]:
            at = pl.multiple_of((lax.axis_index("row") ^ mask) * ranks, 16)
            down_ref[pl.ds(at, ranks), :] = ref[rows : rows + ranks, :]
            up_ref[pl.ds(at, ranks), :] = ref[rows + ranks :, :]
    padded[0:8, :] = jnp.zeros((8, part), jnp.float32)
    place, _, first = request_columns(lengths_ref, 0, tokens)
    inside = place - first
    mixed = jnp.dot(x_all[...], w_all[...], preferred_element_type=jnp.float32)

    def convolved(raw, which):
        padded[8:, :] = raw
        running = taps_ref[0, which : which + 1, :] * raw
        for offset in range(1, taps_ref.shape[0]):
            moved = padded[8 - offset : 8 - offset + tokens, :]
            tap = taps_ref[offset, which : which + 1, :]
            running = running + jnp.where(inside >= offset, tap * moved, 0.0)
        return running

    def store_heads(ref, value):
        blank = jnp.zeros((tokens, LANES - HD), jnp.bfloat16)
        for h in range(part // HD):
            ref[:, h * LANES : h * LANES + HD] = value[:, h * HD : (h + 1) * HD].astype(jnp.bfloat16)
            ref[:, h * LANES + HD : (h + 1) * LANES] = blank

    store_heads(k_ref, convolved(mixed[:, :part], 0))
    store_heads(q_ref, mixed[:, part : 2 * part])
    raw_values = mixed[:, 2 * part : 3 * part]
    store_heads(v_ref, raw_values * jax.nn.sigmoid(convolved(raw_values, 1)))
    attended = attend_block(n_x - 1, count, lengths_ref, valid_ref, q_ref, k_ref, v_ref, cache_ref)
    part_ref[...] = lax.dot_general(
        attended, out_w[...], NT, preferred_element_type=jnp.float32
    ).astype(jnp.bfloat16)


def first_call(blocks, pieces, ranks, taps, lengths, valid, cache):
    (count, width), n_x, n_w = blocks[0].shape, len(blocks), len(pieces)
    tokens, part = count * n_x, taps.shape[2]
    lanes = part // HD * LANES
    mixed_lanes = -(-3 * part // LANES) * LANES
    places = [(mask, first) for _, mask, first in pieces]
    one = jax.ShapeDtypeStruct((tokens, lanes), jnp.bfloat16)
    return pl.pallas_call(
        functools.partial(first_kernel, places, n_x, n_w),
        out_shape=[
            one,
            one,
            one,
            jax.ShapeDtypeStruct((width, lanes), jnp.bfloat16),
            jax.ShapeDtypeStruct((ranks, width), jnp.bfloat16),
            jax.ShapeDtypeStruct((ranks, width), jnp.bfloat16),
            jax.ShapeDtypeStruct((count, width), jnp.bfloat16),
        ],
        in_specs=[VMEM] * (n_x + n_w + 1) + [SMEM, SMEM, VMEM],
        out_specs=[VMEM] * 7,
        scratch_shapes=[
            pltpu.VMEM((tokens, width), jnp.bfloat16),
            pltpu.VMEM((width, mixed_lanes), jnp.bfloat16),
            pltpu.VMEM((tokens + 8, part), jnp.float32),
        ],
        compiler_params=params(36),
        cost_estimate=LIGHT,
    )(*blocks, *(piece for piece, _, _ in pieces), taps, lengths, valid, cache)


def attend_kernel(rank, masks, q_ref, k_ref, v_ref, out_w, x_ref, ids_ref, down_ref, up_ref, *refs):
    lengths_ref, valid_ref, cache_ref = refs[:3]
    for mask, out_ref in zip(masks, refs[3:]):
        attended = attend_block(
            mask, out_ref.shape[0], lengths_ref, valid_ref, q_ref, k_ref, v_ref, cache_ref
        )
        part = lax.dot_general(attended, out_w[...], NT, preferred_element_type=jnp.float32)
        if mask == 0:
            part = part + adapter_term(x_ref, ids_ref, down_ref, up_ref, rank).astype(jnp.float32)
        out_ref[...] = part.astype(out_ref.dtype)


def attend_call(rank, masks, out_types, q, k, v, out_w, x, ids, down, up, lengths, valid, cache):
    count, width = x.shape
    return pl.pallas_call(
        functools.partial(attend_kernel, rank, masks),
        out_shape=[jax.ShapeDtypeStruct((count, width), t) for t in out_types],
        in_specs=[VMEM] * 8 + [SMEM, SMEM, VMEM],
        out_specs=[VMEM] * len(masks),
        compiler_params=params(20),
        cost_estimate=LIGHT,
    )(q, k, v, out_w, x, ids, down, up, lengths, valid, cache)


def feed(x, all_w):
    gate = jnp.dot(x, all_w[0], preferred_element_type=jnp.float32)
    up = jnp.dot(x, all_w[1], preferred_element_type=jnp.float32)
    act = (jax.nn.silu(gate) * up).astype(jnp.bfloat16)
    return lax.dot_general(act, all_w[2], NT, preferred_element_type=jnp.float32)


def feed_first_kernel(places, n_x, n_w, *refs):
    x_refs, w_refs = refs[:n_x], refs[n_x : n_x + n_w]
    all_w, out_refs = refs[n_x + n_w], refs[n_x + n_w + 1 :]
    starts = shard_starts(places, all_w.shape[1] // lax.axis_size("row"))
    for part in range(3):
        for ref, start in zip(w_refs, starts):
            all_w[part, pl.ds(start, ref.shape[1]), :] = ref[part]
    down = feed(jnp.concatenate([ref[...] for ref in x_refs], axis=0), all_w)
    count = x_refs[0].shape[0]
    for i, ref in enumerate(out_refs):
        ref[...] = down[i * count : (i + 1) * count].astype(ref.dtype)


def feed_first_call(blocks, pieces, out_types):
    n_x, n_w, (count, width) = len(blocks), len(pieces), blocks[0].shape
    places = [(mask, first) for _, mask, first in pieces]
    hidden = pieces[0][0].shape[2]
    return pl.pallas_call(
        functools.partial(feed_first_kernel, places, n_x, n_w),
        out_shape=[pltpu.VMEM((3, width, hidden), jnp.bfloat16)]
        + [jax.ShapeDtypeStruct((count, width), t) for t in out_types],
        in_specs=[VMEM] * (n_x + n_w),
        out_specs=[VMEM] * (n_x + 1),
        compiler_params=params(28),
        cost_estimate=LIGHT,
    )(*blocks, *(piece for piece, _, _ in pieces))


def feed_last_kernel(x_ref, all_w, out_ref):
    out_ref[...] = feed(x_ref[...], all_w).astype(out_ref.dtype)


def feed_last_call(block, all_w):
    count, (_, width, hidden) = block.shape[0], all_w.shape
    return pl.pallas_call(
        feed_last_kernel,
        out_shape=jax.ShapeDtypeStruct((count, width), jnp.bfloat16),
        in_specs=[VMEM] * 2,
        out_specs=VMEM,
        compiler_params=params(20),
        cost_estimate=LIGHT,
    )(block, all_w)


def tuned(
    inputs,
    attention_norm_gain,
    query_key_value_weight,
    filter_taps,
    output_projection,
    window_key_value,
    cache_valid_length,
    lengths,
    token_adapter_index,
    adapter_down_map,
    adapter_up_map,
    feed_forward_gain,
    gate_projection,
    up_projection,
    down_projection,
):
    bf16, f32 = jnp.bfloat16, jnp.float32
    col = lax.axis_index("col")
    count, width = inputs.shape
    heads = window_key_value.shape[2]

    rank, kept = adapter_down_map.shape[2], adapter_down_map.shape[0]
    normed_attention, packed = entry_call(
        inputs,
        jnp.transpose(query_key_value_weight, (1, 0, 2)),
        output_projection,
        attention_norm_gain,
        jnp.transpose(adapter_down_map, (0, 2, 1)).reshape(kept * rank, width),
        adapter_up_map.reshape(kept * rank, width),
    )
    token_two, token_one = swap(normed_attention, "col", 2), swap(normed_attention, "col", 1)
    firsts = first_hops(packed)
    requests = window_key_value.shape[0]
    window = window_key_value.shape[3] // HD
    cache = window_key_value.reshape(requests, 2, heads, window, HD)
    cache = jnp.transpose(cache, (1, 2, 0, 3, 4)).reshape(2, heads, requests * window, HD)
    cache = jnp.pad(cache, ((0, 0), (0, 0), (0, 0), (0, LANES - HD)))
    own_ids = lax.dynamic_slice_in_dim(token_adapter_index, col * count, count, 0)
    feed_own = jnp.concatenate(
        [gate_projection[None], up_projection[None], jnp.transpose(down_projection)[None]], axis=0
    )
    token_two, token_one, firsts, packed, cache, own_ids, feed_own = lax.optimization_barrier(
        (token_two, token_one, firsts, packed, cache, own_ids, feed_own)
    )
    token_three = swap(token_two, "col", 1)
    seconds = second_hops(packed, *firsts)
    token_three, diagonal, feed_own = lax.optimization_barrier((token_three, seconds[:2], feed_own))
    thirds = tuple(swap(piece, "row", 1) for piece in diagonal)
    feed_firsts = first_hops(feed_own)

    pieces = named_pieces(packed, firsts, diagonal + seconds[2:], thirds)
    blocks = [normed_attention, token_one, token_two, token_three]
    requests_here = (lengths, cache_valid_length, cache)
    ranks = kept * rank * lax.axis_size("row")
    q, k, v, out_w, down_maps, up_maps, part_three = first_call(
        blocks, pieces, ranks, filter_taps, *requests_here
    )
    passed = swap(part_three, "col", 1)
    part_two, part_one, part_own = attend_call(
        rank, [2, 1, 0], [bf16, bf16, f32], q, k, v, out_w, normed_attention, own_ids, down_maps, up_maps, *requests_here
    )
    part_two = (part_two.astype(f32) + passed.astype(f32)).astype(bf16)
    part_two, part_one = lax.optimization_barrier((part_two, part_one))
    got_two, got_one = swap(part_two, "col", 2), swap(part_one, "col", 1)
    feed_seconds = second_hops(feed_own, *feed_firsts)
    residual, normed_mlp = residual_call(inputs, part_own, got_two, got_one, feed_forward_gain)
    token_two, token_one = swap(normed_mlp, "col", 2), swap(normed_mlp, "col", 1)
    feed_diagonal = feed_seconds[:2]
    feed_thirds = tuple(swap(piece, "row", 1) for piece in feed_diagonal)
    token_two, token_one = lax.optimization_barrier((token_two, token_one))
    token_three = swap(token_two, "col", 1)
    feed_pieces = named_pieces(feed_own, feed_firsts, feed_seconds, feed_thirds)
    feed_w, part_two, part_one, part_own = feed_first_call(
        [token_two, token_one, normed_mlp], feed_pieces, [bf16, bf16, f32]
    )
    part_three = feed_last_call(token_three, feed_w)
    passed = swap(part_three, "col", 1)
    part_two = (part_two.astype(f32) + passed.astype(f32)).astype(bf16)
    part_two, part_one = lax.optimization_barrier((part_two, part_one))
    got_two, got_one = swap(part_two, "col", 2), swap(part_one, "col", 1)
    added = part_own + got_one.astype(f32) + got_two.astype(f32)
    return (residual.astype(f32) + added).astype(bf16)


def on_device(*args):
    rows, cols = lax.axis_size("row"), lax.axis_size("col")
    if (rows, cols) == (8, 4):
        return tuned(*args)
    return plain(*args)


def solution(mesh):
    placed = (
        P(("row", "col"), None),
        P(),
        P("row", None, "col"),
        P(None, None, "col"),
        P("col", "row"),
        P("row", None, "col", None),
        P("row"),
        P("row", None),
        P("row", None),
        P("row", None, None),
        P("row", None, None),
        P(),
        P("row", "col"),
        P("row", "col"),
        P("col", "row"),
    )
    return jax.shard_map(
        on_device, mesh=mesh, in_specs=placed, out_specs=P(("row", "col"), None), check_vma=False
    )
```

```python
import functools

import jax
import jax.numpy as jnp
from jax import lax
from jax.experimental import pallas as pl
from jax.experimental.pallas import tpu as pltpu
from jax.sharding import PartitionSpec as P

HD = 112


epsilon = 1e-05


def rms_scaled(values, gain_row):
    mean_square = jnp.mean(values * values, axis=-1, keepdims=True)
    return values * lax.rsqrt(mean_square + epsilon) * gain_row


def layout(lengths_row, tok_count):
    finish = jnp.cumsum(lengths_row)
    begins = finish - lengths_row
    places = jnp.arange(tok_count, dtype=jnp.int32)
    segment = jnp.sum((places[:, None] >= finish[None, :]).astype(jnp.int32), axis=1)
    member = segment[:, None] == jnp.arange(lengths_row.shape[0], dtype=jnp.int32)[None, :]
    inside = places - jnp.sum(jnp.where(member, begins[None, :], 0), axis=1)
    return (segment, inside)


def shifted(values, offset, inside):
    moved_rows = jnp.pad(values[: values.shape[0] - offset], ((offset, 0), (0, 0)))
    return jnp.where((inside >= offset)[:, None], moved_rows, jnp.zeros_like(moved_rows))


def convolve(values, taps, inside):
    running = jnp.zeros_like(values)
    for offset in range(taps.shape[0]):
        running = running + taps[offset][None, :] * shifted(values, offset, inside)
    return running


def make_qkv(qkv_mixed, filter_taps, inside):
    queries = qkv_mixed[:, 0].astype(jnp.bfloat16)
    keys_used = convolve(qkv_mixed[:, 1], filter_taps[:, 0], inside).astype(jnp.bfloat16)
    raw_values = qkv_mixed[:, 2]
    gates = jax.nn.sigmoid(convolve(raw_values, filter_taps[:, 1], inside))
    values_used = (raw_values * gates).astype(jnp.bfloat16)
    return (queries, keys_used, values_used)


def split_cache(window_key_value, head_size):
    requests_here, head_count = (window_key_value.shape[0], window_key_value.shape[2])
    window = window_key_value.shape[3] // head_size
    split_kv = window_key_value.reshape(requests_here, 2, head_count, window, head_size)
    cached_key_rows = jnp.transpose(split_kv[:, 0], (0, 2, 1, 3)).reshape(
        requests_here * window, head_count, head_size
    )
    cached_value_rows = jnp.transpose(split_kv[:, 1], (0, 2, 1, 3)).reshape(
        requests_here * window, head_count, head_size
    )
    return (cached_key_rows, cached_value_rows, window)


def attend(
    queries,
    keys_used,
    values_used,
    window_key_value,
    segment,
    inside,
    cache_valid_length,
    head_size,
):
    tok_count = queries.shape[0]
    head_count = queries.shape[1] // head_size
    requests_here = window_key_value.shape[0]
    cached_key_rows, cached_value_rows, window = split_cache(window_key_value, head_size)
    query_per_head = queries.reshape(tok_count, head_count, head_size)
    key_h = keys_used.reshape(tok_count, head_count, head_size)
    value_per_head = values_used.reshape(tok_count, head_count, head_size)
    attention_score_scale = head_size ** (-0.5)
    places = jnp.arange(tok_count, dtype=jnp.int32)
    local_mask = (
        (segment[:, None] == segment[None, :])
        & (places[None, :] <= places[:, None])
        & (places[None, :] > places[:, None] - window)
    )
    slot_ids = jnp.arange(requests_here * window, dtype=jnp.int32)
    owner_req = slot_ids // window
    within = slot_ids % window
    slot_ages = jnp.repeat(cache_valid_length, window)
    cache_mask = (
        (segment[:, None] == owner_req[None, :])
        & (within[None, :] >= window - slot_ages[None, :])
        & (within[None, :] > inside[:, None])
    )
    local_scores = (
        jnp.einsum("thd,jhd->htj", query_per_head, key_h, preferred_element_type=jnp.float32)
        * attention_score_scale
    )
    cached_score_rows = (
        jnp.einsum(
            "sek,yek->esy", query_per_head, cached_key_rows, preferred_element_type=jnp.float32
        )
        * attention_score_scale
    )
    local_scores = jnp.where(local_mask[None], local_scores, -jnp.inf)
    cached_score_rows = jnp.where(cache_mask[None], cached_score_rows, -jnp.inf)
    row_max = jnp.maximum(
        jnp.max(local_scores, axis=-1, keepdims=True),
        jnp.max(cached_score_rows, axis=-1, keepdims=True),
    )
    local_exp = jnp.exp(local_scores - row_max)
    cache_exp = jnp.exp(cached_score_rows - row_max)
    denominator = jnp.sum(local_exp, axis=-1, keepdims=True) + jnp.sum(
        cache_exp, axis=-1, keepdims=True
    )
    window_attention_weight = (local_exp / denominator).astype(jnp.bfloat16)
    cached_attention_weight = (cache_exp / denominator).astype(jnp.bfloat16)
    joined_output = jnp.einsum(
        "zkc,czu->kzu", window_attention_weight, value_per_head, preferred_element_type=jnp.float32
    )
    joined_output = joined_output + jnp.einsum(
        "lar,rlx->alx",
        cached_attention_weight,
        cached_value_rows,
        preferred_element_type=jnp.float32,
    )
    return joined_output.reshape(tok_count, head_count * head_size).astype(jnp.bfloat16)


def plain(
    inputs,
    attention_norm_gain,
    query_key_value_weight,
    filter_taps,
    output_projection,
    window_key_value,
    cache_valid_length,
    lengths,
    token_adapter_index,
    adapter_down_map,
    adapter_up_map,
    feed_forward_gain,
    gate_projection,
    up_projection,
    down_projection,
):
    own_count = inputs.shape[0]
    column = lax.axis_index("col")
    row_count = lax.axis_size("row")
    gathered = lax.all_gather(inputs, "col", axis=0, tiled=True)
    tok_count = gathered.shape[0]
    normalized_input = rms_scaled(gathered.astype(jnp.float32), attention_norm_gain).astype(
        jnp.bfloat16
    )
    qkv_mixed = jnp.einsum(
        "td,dka->tka",
        normalized_input,
        lax.all_gather(query_key_value_weight, "row", axis=0, tiled=True),
        preferred_element_type=jnp.float32,
    )
    segment, inside = layout(lengths[0], tok_count)
    queries, keys_used, values_used = make_qkv(qkv_mixed, filter_taps, inside)
    attended = attend(
        queries, keys_used, values_used, window_key_value, segment, inside, cache_valid_length, HD
    )
    kept_count = adapter_down_map.shape[0]
    every_adapter = kept_count * row_count
    capacity = max(2, 2 * own_count // every_adapter)
    first_row = column * own_count
    own_rows = lax.dynamic_slice_in_dim(normalized_input, first_row, own_count, 0)
    own_ids = lax.dynamic_slice_in_dim(token_adapter_index[:, 0], first_row, own_count, 0)
    member = (own_ids[:, None] == jnp.arange(every_adapter, dtype=jnp.int32)[None, :]).astype(
        jnp.int32
    )
    before = jnp.cumsum(member, axis=0) - member
    slot_rank = jnp.sum(before * member, axis=1)
    target = own_ids * capacity + slot_rank
    placer = (
        target[None, :] == jnp.arange(every_adapter * capacity, dtype=jnp.int32)[:, None]
    ).astype(jnp.bfloat16)
    outgoing = jnp.dot(placer, own_rows, preferred_element_type=jnp.float32).astype(jnp.bfloat16)
    outgoing = outgoing.reshape(row_count, kept_count, capacity, normalized_input.shape[1])
    reduced_rank_input = jnp.einsum(
        "sakd,adr->sakr",
        lax.all_to_all(outgoing, "row", split_axis=0, concat_axis=0, tiled=True),
        adapter_down_map,
        preferred_element_type=jnp.float32,
    ).astype(jnp.bfloat16)
    answered = jnp.einsum(
        "zjbf,jfm->zjbm", reduced_rank_input, adapter_up_map, preferred_element_type=jnp.float32
    ).astype(jnp.bfloat16)
    returned = lax.all_to_all(answered, "row", split_axis=0, concat_axis=0, tiled=True).reshape(
        every_adapter * capacity, normalized_input.shape[1]
    )
    delta_rows = jnp.dot(jnp.transpose(placer), returned, preferred_element_type=jnp.float32)
    out_term = jnp.dot(
        attended,
        lax.all_gather(output_projection, "row", axis=1, tiled=True),
        preferred_element_type=jnp.float32,
    )
    own_term = lax.dynamic_slice_in_dim(out_term, first_row, own_count, 0) + delta_rows
    out_term = lax.dynamic_update_slice_in_dim(out_term, own_term, first_row, 0)
    attn_share = lax.psum_scatter(
        out_term.astype(jnp.bfloat16), "col", scatter_dimension=0, tiled=True
    ).astype(jnp.float32)
    residual = (inputs.astype(jnp.float32) + attn_share).astype(jnp.bfloat16)
    whole_mixed = lax.all_gather(residual, "col", axis=0, tiled=True)
    normed_mlp = rms_scaled(whole_mixed.astype(jnp.float32), feed_forward_gain).astype(jnp.bfloat16)

    def add_rows(piece):
        return jnp.dot(normed_mlp, piece, preferred_element_type=jnp.float32)

    gate = add_rows(lax.all_gather(gate_projection, "row", axis=0, tiled=True))
    up_part = add_rows(lax.all_gather(up_projection, "row", axis=0, tiled=True))
    hidden = (jax.nn.silu(gate) * up_part).astype(jnp.bfloat16)
    down_term = jnp.dot(
        hidden,
        lax.all_gather(down_projection, "row", axis=1, tiled=True),
        preferred_element_type=jnp.float32,
    )
    mlp_added = lax.psum_scatter(
        down_term.astype(jnp.bfloat16), "col", scatter_dimension=0, tiled=True
    ).astype(jnp.float32)
    return (residual.astype(jnp.float32) + mlp_added).astype(jnp.bfloat16)


LANES = 128
MIB = 1 << 20


LIGHT = pl.CostEstimate(flops=1, bytes_accessed=1, transcendentals=0)


def params(mib):
    return pltpu.CompilerParams(vmem_limit_bytes=mib * MIB)


HBM = pl.BlockSpec(memory_space=pl.ANY)
VMEM = pl.BlockSpec(memory_space=pltpu.VMEM)
SMEM = pl.BlockSpec(memory_space=pltpu.SMEM)
NT = (((1,), (1,)), ((), ()))


def normed(values, gain):
    mean_square = jnp.mean(values * values, axis=-1, keepdims=True)
    return (values * lax.rsqrt(mean_square + epsilon) * gain).astype(jnp.bfloat16)


def entry_kernel(*refs):
    sources, (normed_ref, packed_ref) = refs[:6], refs[6:8]
    targets, sems = refs[8:14], refs[14]
    loads = [
        pltpu.make_async_copy(source, target, sems.at[i])
        for i, (source, target) in enumerate(zip(sources, targets))
    ]
    for load in loads:
        load.start()
    x_ref, qkv_ref, out_ref, gain_ref, down_ref, up_ref = targets
    rows, part, ranks = qkv_ref.shape[1], qkv_ref.shape[2], down_ref.shape[0]
    for load in loads:
        load.wait()
    normed_ref[...] = normed(x_ref[...].astype(jnp.float32), gain_ref[...][None, :])
    for place, which in enumerate((1, 0, 2)):
        packed_ref[:rows, place * part : (place + 1) * part] = qkv_ref[which]
    out_rows = jnp.transpose(out_ref[...].astype(jnp.float32)).astype(jnp.bfloat16)
    packed_ref[:rows, 3 * part :] = out_rows
    packed_ref[rows : rows + ranks, :] = down_ref[...]
    packed_ref[rows + ranks :, :] = up_ref[...]


def entry_call(rows, qkv, out, gain, down, up):
    sources = (rows, qkv, out, gain, down, up)
    return pl.pallas_call(
        entry_kernel,
        out_shape=[
            jax.ShapeDtypeStruct(rows.shape, jnp.bfloat16),
            jax.ShapeDtypeStruct((qkv.shape[1] + 2 * down.shape[0], 4 * qkv.shape[2]), jnp.bfloat16),
        ],
        in_specs=[HBM] * len(sources),
        out_specs=[VMEM] * 2,
        scratch_shapes=[pltpu.VMEM(source.shape, source.dtype) for source in sources]
        + [pltpu.SemaphoreType.DMA((len(sources),))],
        compiler_params=params(60),
        cost_estimate=LIGHT,
    )(*sources)


def residual_kernel(x_ref, own_ref, two_ref, one_ref, gain_ref, residual_ref, normed_ref):
    total = own_ref[...] + one_ref[...].astype(jnp.float32) + two_ref[...].astype(jnp.float32)
    residual = (x_ref[...].astype(jnp.float32) + total).astype(jnp.bfloat16)
    residual_ref[...] = residual
    normed_ref[...] = normed(residual.astype(jnp.float32), gain_ref[...])


def residual_call(rows, own, two, one, gain):
    block = jax.ShapeDtypeStruct(rows.shape, jnp.bfloat16)
    return pl.pallas_call(
        residual_kernel,
        out_shape=[block, block],
        in_specs=[VMEM] * 5,
        out_specs=[VMEM] * 2,
        compiler_params=params(12),
        cost_estimate=LIGHT,
    )(rows, own, two, one, gain[None, :])


def adapter_term(x_ref, ids_ref, down_ref, up_ref, rank):
    low = lax.dot_general(x_ref[...], down_ref[...], NT, preferred_element_type=jnp.float32)
    adapter = lax.broadcasted_iota(jnp.int32, low.shape, 1) // rank
    low = jnp.where(ids_ref[...] == adapter, low, 0.0).astype(jnp.bfloat16)
    return jnp.dot(low, up_ref[...], preferred_element_type=jnp.float32).astype(jnp.bfloat16)


def xor_pairs(count, mask):
    return [(i, i ^ mask) for i in range(count)]


def swap(value, axis, mask):
    return lax.ppermute(value, axis, xor_pairs(lax.axis_size(axis), mask))


def first_hops(own):
    return swap(own, "row", 2), swap(own, "row", 4)


def second_hops(own, from_x, from_y):
    half = own.shape[-2] // 2
    diagonal = swap(from_x[..., :half, :], "row", 4), swap(from_y[..., half:, :], "row", 2)
    return diagonal + tuple(swap(piece, "row", 1) for piece in (own, from_x, from_y))


def named_pieces(own, firsts, seconds, thirds):
    half = own.shape[-2] // 2
    masks = [(0, 0), (2, 0), (4, 0), (6, 0), (6, half), (1, 0), (3, 0), (5, 0), (7, 0), (7, half)]
    return [(piece, *at) for piece, at in zip((own,) + firsts + seconds + thirds, masks)]


def shard_starts(places, shard):
    row = lax.axis_index("row")
    return [pl.multiple_of((row ^ mask) * shard + first, 16) for mask, first in places]


def request_columns(lengths_ref, begin, count):
    place = begin + lax.broadcasted_iota(jnp.int32, (count, 1), 0)
    segment, first = jnp.zeros_like(place), jnp.zeros_like(place)
    finish = jnp.int32(0)
    for s in range(lengths_ref.shape[1]):
        finish = finish + lengths_ref[0, s]
        later = place >= finish
        segment = segment + later.astype(jnp.int32)
        first = jnp.where(later, finish, first)
    return place, segment, first


def attend_block(mask, count, base, lengths_ref, valid_ref, q_ref, k_ref, v_ref, cache_ref):
    col = lax.axis_index("col")
    _, heads, slots, lanes = cache_ref.shape
    requests = valid_ref.shape[0]
    window = slots // requests
    scale = HD ** (-0.5)
    begin = pl.multiple_of((col ^ mask) * count, count)
    key_begin = pl.multiple_of(jnp.maximum(begin - window, 0), window)
    key_count = count + window
    place, segment, first = request_columns(lengths_ref, begin, count)
    first_key = jnp.maximum(first, place - window + 1)
    keys = key_begin + lax.broadcasted_iota(jnp.int32, (count, key_count), 1)
    local_mask = (keys >= first_key) & (keys <= place)
    slot = lax.broadcasted_iota(jnp.int32, (1, slots), 1)
    owner, within = slot // window, slot % window
    oldest = jnp.full_like(slot, window)
    for s in range(requests):
        oldest = jnp.where(owner == s, window - valid_ref[s], oldest)
    within = jnp.where(within >= oldest, within, -1)
    cache_mask = (owner == segment) & (within > place - first)
    outs = []
    own_rows = pl.ds(pl.multiple_of(begin - base, count), count)
    key_rows = pl.ds(pl.multiple_of(key_begin - base, window), key_count)
    for h in range(heads):
        cols = slice(h * lanes, (h + 1) * lanes)
        q, k, v = q_ref[own_rows, cols], k_ref[key_rows, cols], v_ref[key_rows, cols]
        local = lax.dot_general(q, k, NT, preferred_element_type=jnp.float32)
        cached = lax.dot_general(q, cache_ref[0, h], NT, preferred_element_type=jnp.float32)
        local = jnp.where(local_mask, local * scale, -jnp.inf)
        cached = jnp.where(cache_mask, cached * scale, -jnp.inf)
        top = jnp.maximum(
            jnp.max(local, axis=-1, keepdims=True), jnp.max(cached, axis=-1, keepdims=True)
        )
        local = jnp.exp(local - top)
        cached = jnp.exp(cached - top)
        total = jnp.sum(local, axis=-1, keepdims=True) + jnp.sum(cached, axis=-1, keepdims=True)
        summed = jnp.dot(local.astype(jnp.bfloat16), v, preferred_element_type=jnp.float32)
        summed = summed + jnp.dot(
            cached.astype(jnp.bfloat16), cache_ref[1, h], preferred_element_type=jnp.float32
        )
        outs.append((summed / total).astype(jnp.bfloat16)[:, :HD])
    blank = jnp.zeros((count, heads * (lanes - HD)), jnp.bfloat16)
    return jnp.concatenate([blank] + outs, axis=1)


def mix_rows(x, base, w_ref, taps_ref, lengths_ref, q_ref, k_ref, v_ref, padded):
    rows, part = x.shape[0], taps_ref.shape[2]
    padded[0:8, :] = jnp.zeros((8, part), jnp.float32)
    place, _, first = request_columns(lengths_ref, base, rows)
    inside = place - first
    mixed = jnp.dot(x, w_ref[...], preferred_element_type=jnp.float32)

    def convolved(raw, which):
        padded[8:, :] = raw
        running = taps_ref[0, which : which + 1, :] * raw
        for offset in range(1, taps_ref.shape[0]):
            moved = padded[8 - offset : 8 - offset + rows, :]
            tap = taps_ref[offset, which : which + 1, :]
            running = running + jnp.where(inside >= offset, tap * moved, 0.0)
        return running

    def store_heads(ref, value):
        blank = jnp.zeros((rows, LANES - HD), jnp.bfloat16)
        for h in range(part // HD):
            ref[:, h * LANES : h * LANES + HD] = value[:, h * HD : (h + 1) * HD].astype(jnp.bfloat16)
            ref[:, h * LANES + HD : (h + 1) * LANES] = blank

    store_heads(k_ref, convolved(mixed[:, :part], 0))
    store_heads(q_ref, mixed[:, part : 2 * part])
    raw_values = mixed[:, 2 * part : 3 * part]
    store_heads(v_ref, raw_values * jax.nn.sigmoid(convolved(raw_values, 1)))


def first_kernel(places, n_x, n_w, *refs):
    x_refs, w_refs = refs[:n_x], refs[n_x : n_x + n_w]
    taps_ref, lengths_ref, valid_ref, cache_ref = refs[n_x + n_w : n_x + n_w + 4]
    x_all, w_all, out_w, down_ref, up_ref, part_ref, q_ref, k_ref, v_ref, padded = refs[n_x + n_w + 4 :]
    col = lax.axis_index("col")
    count, width = x_refs[0].shape
    lanes, mixed_lanes = out_w.shape[1], w_all.shape[1]
    for i, ref in enumerate(x_refs):
        x_all[pl.ds(pl.multiple_of((col ^ i) * count, 16), count), :] = ref[...]
    shard = width // lax.axis_size("row")
    ranks = down_ref.shape[0] // lax.axis_size("row")
    starts = shard_starts(places, shard)
    for ref, start, (mask, first) in zip(w_refs, starts, places):
        rows = min(ref.shape[0], shard - first)
        w_all[pl.ds(start, rows), :] = ref[:rows, :mixed_lanes]
        out_w[pl.ds(start, rows), :] = ref[:rows, ref.shape[1] - lanes :]
        if rows < ref.shape[0]:
            at = pl.multiple_of((lax.axis_index("row") ^ mask) * ranks, 16)
            down_ref[pl.ds(at, ranks), :] = ref[rows : rows + ranks, :]
            up_ref[pl.ds(at, ranks), :] = ref[rows + ranks :, :]
    base = pl.multiple_of(jnp.maximum((col ^ (n_x - 1)) * count - count, 0), count)
    x = x_all[pl.ds(base, 2 * count), :]
    mix_rows(x, base, w_all, taps_ref, lengths_ref, q_ref, k_ref, v_ref, padded)
    attended = attend_block(
        n_x - 1, count, base, lengths_ref, valid_ref, q_ref, k_ref, v_ref, cache_ref
    )
    part_ref[...] = lax.dot_general(
        attended, out_w[...], NT, preferred_element_type=jnp.float32
    ).astype(jnp.bfloat16)


def first_call(blocks, pieces, ranks, taps, lengths, valid, cache):
    (count, width), n_x, n_w = blocks[0].shape, len(blocks), len(pieces)
    tokens, part = count * n_x, taps.shape[2]
    lanes = part // HD * LANES
    mixed_lanes = -(-3 * part // LANES) * LANES
    places = [(mask, first) for _, mask, first in pieces]
    shapes = [(tokens, width), (width, mixed_lanes), (width, lanes), (ranks, width), (ranks, width), (count, width)]
    return pl.pallas_call(
        functools.partial(first_kernel, places, n_x, n_w),
        out_shape=[pltpu.VMEM(shape, jnp.bfloat16) for shape in shapes[:3]]
        + [jax.ShapeDtypeStruct(shape, jnp.bfloat16) for shape in shapes[3:]],
        in_specs=[VMEM] * (n_x + n_w + 1) + [SMEM, SMEM, VMEM],
        out_specs=[VMEM] * len(shapes),
        scratch_shapes=[pltpu.VMEM((2 * count, lanes), jnp.bfloat16)] * 3
        + [pltpu.VMEM((2 * count + 8, part), jnp.float32)],
        compiler_params=params(28),
        cost_estimate=LIGHT,
    )(*blocks, *(piece for piece, _, _ in pieces), taps, lengths, valid, cache)


def rest_kernel(masks, x_all, w_all, out_w, taps_ref, lengths_ref, valid_ref, cache_ref, *refs):
    q_ref, k_ref, v_ref = refs[:3]
    out_refs, padded = refs[3:-1], refs[-1]
    mix_rows(x_all[...], 0, w_all, taps_ref, lengths_ref, q_ref, k_ref, v_ref, padded)
    for mask, out_ref in zip(masks, out_refs):
        attended = attend_block(
            mask, out_ref.shape[0], 0, lengths_ref, valid_ref, q_ref, k_ref, v_ref, cache_ref
        )
        out_ref[...] = lax.dot_general(
            attended, out_w[...], NT, preferred_element_type=jnp.float32
        ).astype(out_ref.dtype)


def rest_call(masks, count, x_all, w_all, out_w, taps, lengths, valid, cache):
    (tokens, width), lanes = x_all.shape, out_w.shape[1]
    shapes = [(tokens, lanes)] * 3 + [(count, width)] * len(masks)
    return pl.pallas_call(
        functools.partial(rest_kernel, masks),
        out_shape=[jax.ShapeDtypeStruct(shape, jnp.bfloat16) for shape in shapes],
        in_specs=[VMEM] * 4 + [SMEM, SMEM, VMEM],
        out_specs=[VMEM] * len(shapes),
        scratch_shapes=[pltpu.VMEM((tokens + 8, taps.shape[2]), jnp.float32)],
        compiler_params=params(32),
        cost_estimate=LIGHT,
    )(x_all, w_all, out_w, taps, lengths, valid, cache)


def own_kernel(rank, q_ref, k_ref, v_ref, out_w, x_ref, ids_ref, down_ref, up_ref, *refs):
    lengths_ref, valid_ref, cache_ref, out_ref = refs
    attended = attend_block(
        0, out_ref.shape[0], 0, lengths_ref, valid_ref, q_ref, k_ref, v_ref, cache_ref
    )
    part = lax.dot_general(attended, out_w[...], NT, preferred_element_type=jnp.float32)
    out_ref[...] = part + adapter_term(x_ref, ids_ref, down_ref, up_ref, rank).astype(jnp.float32)


def own_call(rank, q, k, v, out_w, x, ids, down, up, lengths, valid, cache):
    return pl.pallas_call(
        functools.partial(own_kernel, rank),
        out_shape=jax.ShapeDtypeStruct(x.shape, jnp.float32),
        in_specs=[VMEM] * 8 + [SMEM, SMEM, VMEM],
        out_specs=VMEM,
        compiler_params=params(20),
        cost_estimate=LIGHT,
    )(q, k, v, out_w, x, ids, down, up, lengths, valid, cache)


def feed(x, all_w):
    gate = jnp.dot(x, all_w[0], preferred_element_type=jnp.float32)
    up = jnp.dot(x, all_w[1], preferred_element_type=jnp.float32)
    act = (jax.nn.silu(gate) * up).astype(jnp.bfloat16)
    return lax.dot_general(act, all_w[2], NT, preferred_element_type=jnp.float32)


def feed_first_kernel(places, n_x, n_w, *refs):
    x_refs, w_refs = refs[:n_x], refs[n_x : n_x + n_w]
    all_w, out_refs = refs[n_x + n_w], refs[n_x + n_w + 1 :]
    starts = shard_starts(places, all_w.shape[1] // lax.axis_size("row"))
    for part in range(3):
        for ref, start in zip(w_refs, starts):
            all_w[part, pl.ds(start, ref.shape[1]), :] = ref[part]
    down = feed(jnp.concatenate([ref[...] for ref in x_refs], axis=0), all_w)
    count = x_refs[0].shape[0]
    for i, ref in enumerate(out_refs):
        ref[...] = down[i * count : (i + 1) * count].astype(ref.dtype)


def feed_first_call(blocks, pieces, out_types):
    n_x, n_w, (count, width) = len(blocks), len(pieces), blocks[0].shape
    places = [(mask, first) for _, mask, first in pieces]
    hidden = pieces[0][0].shape[2]
    return pl.pallas_call(
        functools.partial(feed_first_kernel, places, n_x, n_w),
        out_shape=[pltpu.VMEM((3, width, hidden), jnp.bfloat16)]
        + [jax.ShapeDtypeStruct((count, width), t) for t in out_types],
        in_specs=[VMEM] * (n_x + n_w),
        out_specs=[VMEM] * (n_x + 1),
        compiler_params=params(28),
        cost_estimate=LIGHT,
    )(*blocks, *(piece for piece, _, _ in pieces))


def feed_last_kernel(x_ref, all_w, out_ref):
    out_ref[...] = feed(x_ref[...], all_w).astype(out_ref.dtype)


def feed_last_call(block, all_w):
    count, (_, width, hidden) = block.shape[0], all_w.shape
    return pl.pallas_call(
        feed_last_kernel,
        out_shape=jax.ShapeDtypeStruct((count, width), jnp.bfloat16),
        in_specs=[VMEM] * 2,
        out_specs=VMEM,
        compiler_params=params(20),
        cost_estimate=LIGHT,
    )(block, all_w)


def tuned(
    inputs,
    attention_norm_gain,
    query_key_value_weight,
    filter_taps,
    output_projection,
    window_key_value,
    cache_valid_length,
    lengths,
    token_adapter_index,
    adapter_down_map,
    adapter_up_map,
    feed_forward_gain,
    gate_projection,
    up_projection,
    down_projection,
):
    bf16, f32 = jnp.bfloat16, jnp.float32
    col = lax.axis_index("col")
    count, width = inputs.shape
    heads = window_key_value.shape[2]

    rank, kept = adapter_down_map.shape[2], adapter_down_map.shape[0]
    normed_attention, packed = entry_call(
        inputs,
        jnp.transpose(query_key_value_weight, (1, 0, 2)),
        output_projection,
        attention_norm_gain,
        jnp.transpose(adapter_down_map, (0, 2, 1)).reshape(kept * rank, width),
        adapter_up_map.reshape(kept * rank, width),
    )
    token_two, token_one = swap(normed_attention, "col", 2), swap(normed_attention, "col", 1)
    firsts = first_hops(packed)
    requests = window_key_value.shape[0]
    window = window_key_value.shape[3] // HD
    cache = window_key_value.reshape(requests, 2, heads, window, HD)
    cache = jnp.transpose(cache, (1, 2, 0, 3, 4)).reshape(2, heads, requests * window, HD)
    cache = jnp.pad(cache, ((0, 0), (0, 0), (0, 0), (0, LANES - HD)))
    own_ids = lax.dynamic_slice_in_dim(token_adapter_index, col * count, count, 0)
    feed_own = jnp.concatenate(
        [gate_projection[None], up_projection[None], jnp.transpose(down_projection)[None]], axis=0
    )
    firsts, cache, own_ids, feed_own = lax.optimization_barrier((firsts, cache, own_ids, feed_own))
    token_two, token_one, cache = lax.optimization_barrier((token_two, token_one, cache))
    token_three = swap(token_two, "col", 1)
    seconds = second_hops(packed, *firsts)
    token_three, diagonal, feed_own = lax.optimization_barrier((token_three, seconds[:2], feed_own))
    seconds = diagonal + seconds[2:]
    thirds = tuple(swap(piece, "row", 1) for piece in diagonal)
    feed_firsts = first_hops(feed_own)

    pieces = named_pieces(packed, firsts, seconds, thirds)
    blocks = [normed_attention, token_one, token_two, token_three]
    requests_here = (lengths, cache_valid_length, cache)
    ranks = kept * rank * lax.axis_size("row")
    x_all, w_all, out_w, down_maps, up_maps, part_three = first_call(
        blocks, pieces, ranks, filter_taps, *requests_here
    )
    passed = swap(part_three, "col", 1)
    q, k, v, part_two, part_one = rest_call(
        [2, 1], count, x_all, w_all, out_w, filter_taps, *requests_here
    )
    part_own = own_call(
        rank, q, k, v, out_w, normed_attention, own_ids, down_maps, up_maps, *requests_here
    )
    got_one = swap(part_one, "col", 1)
    got_two = swap((part_two.astype(f32) + passed.astype(f32)).astype(bf16), "col", 2)
    got_one, *hops = lax.optimization_barrier((got_one, *feed_firsts))
    feed_seconds = second_hops(feed_own, *hops)
    residual, normed_mlp = residual_call(inputs, part_own, got_two, got_one, feed_forward_gain)
    token_two, token_one = swap(normed_mlp, "col", 2), swap(normed_mlp, "col", 1)
    feed_thirds = tuple(swap(piece, "row", 1) for piece in feed_seconds[:2])
    token_two, token_one = lax.optimization_barrier((token_two, token_one))
    token_three = swap(token_two, "col", 1)
    feed_pieces = named_pieces(feed_own, feed_firsts, feed_seconds, feed_thirds)
    feed_w, part_two, part_one, part_own = feed_first_call(
        [token_two, token_one, normed_mlp], feed_pieces, [bf16, bf16, f32]
    )
    part_three = feed_last_call(token_three, feed_w)
    passed = swap(part_three, "col", 1)
    part_two = (part_two.astype(f32) + passed.astype(f32)).astype(bf16)
    part_two, part_one = lax.optimization_barrier((part_two, part_one))
    got_two, got_one = swap(part_two, "col", 2), swap(part_one, "col", 1)
    added = part_own + got_one.astype(f32) + got_two.astype(f32)
    return (residual.astype(f32) + added).astype(bf16)


def on_device(*args):
    rows, cols = lax.axis_size("row"), lax.axis_size("col")
    if (rows, cols) == (8, 4):
        return tuned(*args)
    return plain(*args)


def solution(mesh):
    placed = (
        P(("row", "col"), None),
        P(),
        P("row", None, "col"),
        P(None, None, "col"),
        P("col", "row"),
        P("row", None, "col", None),
        P("row"),
        P("row", None),
        P("row", None),
        P("row", None, None),
        P("row", None, None),
        P(),
        P("row", "col"),
        P("row", "col"),
        P("col", "row"),
    )
    return jax.shard_map(
        on_device, mesh=mesh, in_specs=placed, out_specs=P(("row", "col"), None), check_vma=False
    )
```

```python
import functools

import jax
import jax.numpy as jnp
from jax import lax
from jax.experimental import pallas as pl
from jax.experimental.pallas import tpu as pltpu
from jax.sharding import PartitionSpec as P

HD = 112


epsilon = 1e-05


def rms_scaled(values, gain_row):
    mean_square = jnp.mean(values * values, axis=-1, keepdims=True)
    return values * lax.rsqrt(mean_square + epsilon) * gain_row


def layout(lengths_row, tok_count):
    finish = jnp.cumsum(lengths_row)
    begins = finish - lengths_row
    places = jnp.arange(tok_count, dtype=jnp.int32)
    segment = jnp.sum((places[:, None] >= finish[None, :]).astype(jnp.int32), axis=1)
    member = segment[:, None] == jnp.arange(lengths_row.shape[0], dtype=jnp.int32)[None, :]
    inside = places - jnp.sum(jnp.where(member, begins[None, :], 0), axis=1)
    return (segment, inside)


def shifted(values, offset, inside):
    moved_rows = jnp.pad(values[: values.shape[0] - offset], ((offset, 0), (0, 0)))
    return jnp.where((inside >= offset)[:, None], moved_rows, jnp.zeros_like(moved_rows))


def convolve(values, taps, inside):
    running = jnp.zeros_like(values)
    for offset in range(taps.shape[0]):
        running = running + taps[offset][None, :] * shifted(values, offset, inside)
    return running


def make_qkv(qkv_mixed, filter_taps, inside):
    queries = qkv_mixed[:, 0].astype(jnp.bfloat16)
    keys_used = convolve(qkv_mixed[:, 1], filter_taps[:, 0], inside).astype(jnp.bfloat16)
    raw_values = qkv_mixed[:, 2]
    gates = jax.nn.sigmoid(convolve(raw_values, filter_taps[:, 1], inside))
    values_used = (raw_values * gates).astype(jnp.bfloat16)
    return (queries, keys_used, values_used)


def split_cache(window_key_value, head_size):
    requests_here, head_count = (window_key_value.shape[0], window_key_value.shape[2])
    window = window_key_value.shape[3] // head_size
    split_kv = window_key_value.reshape(requests_here, 2, head_count, window, head_size)
    cached_key_rows = jnp.transpose(split_kv[:, 0], (0, 2, 1, 3)).reshape(
        requests_here * window, head_count, head_size
    )
    cached_value_rows = jnp.transpose(split_kv[:, 1], (0, 2, 1, 3)).reshape(
        requests_here * window, head_count, head_size
    )
    return (cached_key_rows, cached_value_rows, window)


def attend(
    queries,
    keys_used,
    values_used,
    window_key_value,
    segment,
    inside,
    cache_valid_length,
    head_size,
):
    tok_count = queries.shape[0]
    head_count = queries.shape[1] // head_size
    requests_here = window_key_value.shape[0]
    cached_key_rows, cached_value_rows, window = split_cache(window_key_value, head_size)
    query_per_head = queries.reshape(tok_count, head_count, head_size)
    key_h = keys_used.reshape(tok_count, head_count, head_size)
    value_per_head = values_used.reshape(tok_count, head_count, head_size)
    attention_score_scale = head_size ** (-0.5)
    places = jnp.arange(tok_count, dtype=jnp.int32)
    local_mask = (
        (segment[:, None] == segment[None, :])
        & (places[None, :] <= places[:, None])
        & (places[None, :] > places[:, None] - window)
    )
    slot_ids = jnp.arange(requests_here * window, dtype=jnp.int32)
    owner_req = slot_ids // window
    within = slot_ids % window
    slot_ages = jnp.repeat(cache_valid_length, window)
    cache_mask = (
        (segment[:, None] == owner_req[None, :])
        & (within[None, :] >= window - slot_ages[None, :])
        & (within[None, :] > inside[:, None])
    )
    local_scores = (
        jnp.einsum("thd,jhd->htj", query_per_head, key_h, preferred_element_type=jnp.float32)
        * attention_score_scale
    )
    cached_score_rows = (
        jnp.einsum(
            "sek,yek->esy", query_per_head, cached_key_rows, preferred_element_type=jnp.float32
        )
        * attention_score_scale
    )
    local_scores = jnp.where(local_mask[None], local_scores, -jnp.inf)
    cached_score_rows = jnp.where(cache_mask[None], cached_score_rows, -jnp.inf)
    row_max = jnp.maximum(
        jnp.max(local_scores, axis=-1, keepdims=True),
        jnp.max(cached_score_rows, axis=-1, keepdims=True),
    )
    local_exp = jnp.exp(local_scores - row_max)
    cache_exp = jnp.exp(cached_score_rows - row_max)
    denominator = jnp.sum(local_exp, axis=-1, keepdims=True) + jnp.sum(
        cache_exp, axis=-1, keepdims=True
    )
    window_attention_weight = (local_exp / denominator).astype(jnp.bfloat16)
    cached_attention_weight = (cache_exp / denominator).astype(jnp.bfloat16)
    joined_output = jnp.einsum(
        "zkc,czu->kzu", window_attention_weight, value_per_head, preferred_element_type=jnp.float32
    )
    joined_output = joined_output + jnp.einsum(
        "lar,rlx->alx",
        cached_attention_weight,
        cached_value_rows,
        preferred_element_type=jnp.float32,
    )
    return joined_output.reshape(tok_count, head_count * head_size).astype(jnp.bfloat16)


def plain(
    inputs,
    attention_norm_gain,
    query_key_value_weight,
    filter_taps,
    output_projection,
    window_key_value,
    cache_valid_length,
    lengths,
    token_adapter_index,
    adapter_down_map,
    adapter_up_map,
    feed_forward_gain,
    gate_projection,
    up_projection,
    down_projection,
):
    own_count = inputs.shape[0]
    column = lax.axis_index("col")
    row_count = lax.axis_size("row")
    gathered = lax.all_gather(inputs, "col", axis=0, tiled=True)
    tok_count = gathered.shape[0]
    normalized_input = rms_scaled(gathered.astype(jnp.float32), attention_norm_gain).astype(
        jnp.bfloat16
    )
    qkv_mixed = jnp.einsum(
        "td,dka->tka",
        normalized_input,
        lax.all_gather(query_key_value_weight, "row", axis=0, tiled=True),
        preferred_element_type=jnp.float32,
    )
    segment, inside = layout(lengths[0], tok_count)
    queries, keys_used, values_used = make_qkv(qkv_mixed, filter_taps, inside)
    attended = attend(
        queries, keys_used, values_used, window_key_value, segment, inside, cache_valid_length, HD
    )
    kept_count = adapter_down_map.shape[0]
    every_adapter = kept_count * row_count
    capacity = max(2, 2 * own_count // every_adapter)
    first_row = column * own_count
    own_rows = lax.dynamic_slice_in_dim(normalized_input, first_row, own_count, 0)
    own_ids = lax.dynamic_slice_in_dim(token_adapter_index[:, 0], first_row, own_count, 0)
    member = (own_ids[:, None] == jnp.arange(every_adapter, dtype=jnp.int32)[None, :]).astype(
        jnp.int32
    )
    before = jnp.cumsum(member, axis=0) - member
    slot_rank = jnp.sum(before * member, axis=1)
    target = own_ids * capacity + slot_rank
    placer = (
        target[None, :] == jnp.arange(every_adapter * capacity, dtype=jnp.int32)[:, None]
    ).astype(jnp.bfloat16)
    outgoing = jnp.dot(placer, own_rows, preferred_element_type=jnp.float32).astype(jnp.bfloat16)
    outgoing = outgoing.reshape(row_count, kept_count, capacity, normalized_input.shape[1])
    reduced_rank_input = jnp.einsum(
        "sakd,adr->sakr",
        lax.all_to_all(outgoing, "row", split_axis=0, concat_axis=0, tiled=True),
        adapter_down_map,
        preferred_element_type=jnp.float32,
    ).astype(jnp.bfloat16)
    answered = jnp.einsum(
        "zjbf,jfm->zjbm", reduced_rank_input, adapter_up_map, preferred_element_type=jnp.float32
    ).astype(jnp.bfloat16)
    returned = lax.all_to_all(answered, "row", split_axis=0, concat_axis=0, tiled=True).reshape(
        every_adapter * capacity, normalized_input.shape[1]
    )
    delta_rows = jnp.dot(jnp.transpose(placer), returned, preferred_element_type=jnp.float32)
    out_term = jnp.dot(
        attended,
        lax.all_gather(output_projection, "row", axis=1, tiled=True),
        preferred_element_type=jnp.float32,
    )
    own_term = lax.dynamic_slice_in_dim(out_term, first_row, own_count, 0) + delta_rows
    out_term = lax.dynamic_update_slice_in_dim(out_term, own_term, first_row, 0)
    attn_share = lax.psum_scatter(
        out_term.astype(jnp.bfloat16), "col", scatter_dimension=0, tiled=True
    ).astype(jnp.float32)
    residual = (inputs.astype(jnp.float32) + attn_share).astype(jnp.bfloat16)
    whole_mixed = lax.all_gather(residual, "col", axis=0, tiled=True)
    normed_mlp = rms_scaled(whole_mixed.astype(jnp.float32), feed_forward_gain).astype(jnp.bfloat16)

    def add_rows(piece):
        return jnp.dot(normed_mlp, piece, preferred_element_type=jnp.float32)

    gate = add_rows(lax.all_gather(gate_projection, "row", axis=0, tiled=True))
    up_part = add_rows(lax.all_gather(up_projection, "row", axis=0, tiled=True))
    hidden = (jax.nn.silu(gate) * up_part).astype(jnp.bfloat16)
    down_term = jnp.dot(
        hidden,
        lax.all_gather(down_projection, "row", axis=1, tiled=True),
        preferred_element_type=jnp.float32,
    )
    mlp_added = lax.psum_scatter(
        down_term.astype(jnp.bfloat16), "col", scatter_dimension=0, tiled=True
    ).astype(jnp.float32)
    return (residual.astype(jnp.float32) + mlp_added).astype(jnp.bfloat16)


LANES = 128
MIB = 1 << 20


LIGHT = pl.CostEstimate(flops=1, bytes_accessed=1, transcendentals=0)


def params(mib):
    return pltpu.CompilerParams(vmem_limit_bytes=mib * MIB)


HBM = pl.BlockSpec(memory_space=pl.ANY)
VMEM = pl.BlockSpec(memory_space=pltpu.VMEM)
SMEM = pl.BlockSpec(memory_space=pltpu.SMEM)
NT = (((1,), (1,)), ((), ()))


def normed(values, gain):
    mean_square = jnp.mean(values * values, axis=-1, keepdims=True)
    return (values * lax.rsqrt(mean_square + epsilon) * gain).astype(jnp.bfloat16)


def entry_kernel(*refs):
    sources, (normed_ref, packed_ref) = refs[:6], refs[6:8]
    targets, sems = refs[8:14], refs[14]
    loads = [
        pltpu.make_async_copy(source, target, sems.at[i])
        for i, (source, target) in enumerate(zip(sources, targets))
    ]
    for load in loads:
        load.start()
    x_ref, qkv_ref, out_ref, gain_ref, down_ref, up_ref = targets
    rows, part, ranks = qkv_ref.shape[1], qkv_ref.shape[2], down_ref.shape[0]
    for load in loads:
        load.wait()
    normed_ref[...] = normed(x_ref[...].astype(jnp.float32), gain_ref[...][None, :])
    for place, which in enumerate((1, 0, 2)):
        packed_ref[:rows, place * part : (place + 1) * part] = qkv_ref[which]
    out_rows = jnp.transpose(out_ref[...].astype(jnp.float32)).astype(jnp.bfloat16)
    packed_ref[:rows, 3 * part :] = out_rows
    packed_ref[rows : rows + ranks, :] = down_ref[...]
    packed_ref[rows + ranks :, :] = up_ref[...]


def entry_call(rows, qkv, out, gain, down, up):
    sources = (rows, qkv, out, gain, down, up)
    return pl.pallas_call(
        entry_kernel,
        out_shape=[
            jax.ShapeDtypeStruct(rows.shape, jnp.bfloat16),
            jax.ShapeDtypeStruct((qkv.shape[1] + 2 * down.shape[0], 4 * qkv.shape[2]), jnp.bfloat16),
        ],
        in_specs=[HBM] * len(sources),
        out_specs=[VMEM] * 2,
        scratch_shapes=[pltpu.VMEM(source.shape, source.dtype) for source in sources]
        + [pltpu.SemaphoreType.DMA((len(sources),))],
        compiler_params=params(60),
        cost_estimate=LIGHT,
    )(*sources)


def residual_kernel(x_ref, own_ref, two_ref, one_ref, gain_ref, residual_ref, normed_ref):
    total = own_ref[...] + one_ref[...].astype(jnp.float32) + two_ref[...].astype(jnp.float32)
    residual = (x_ref[...].astype(jnp.float32) + total).astype(jnp.bfloat16)
    residual_ref[...] = residual
    normed_ref[...] = normed(residual.astype(jnp.float32), gain_ref[...])


def residual_call(rows, own, two, one, gain):
    block = jax.ShapeDtypeStruct(rows.shape, jnp.bfloat16)
    return pl.pallas_call(
        residual_kernel,
        out_shape=[block, block],
        in_specs=[VMEM] * 5,
        out_specs=[VMEM] * 2,
        compiler_params=params(12),
        cost_estimate=LIGHT,
    )(rows, own, two, one, gain[None, :])


def adapter_term(x_ref, ids_ref, down_ref, up_ref, rank):
    low = lax.dot_general(x_ref[...], down_ref[...], NT, preferred_element_type=jnp.float32)
    adapter = lax.broadcasted_iota(jnp.int32, low.shape, 1) // rank
    low = jnp.where(ids_ref[...] == adapter, low, 0.0).astype(jnp.bfloat16)
    return jnp.dot(low, up_ref[...], preferred_element_type=jnp.float32).astype(jnp.bfloat16)


def xor_pairs(count, mask):
    return [(i, i ^ mask) for i in range(count)]


def swap(value, axis, mask):
    return lax.ppermute(value, axis, xor_pairs(lax.axis_size(axis), mask))


def first_hops(own):
    return swap(own, "row", 2), swap(own, "row", 4)


def second_hops(own, from_x, from_y):
    half = own.shape[-2] // 2
    diagonal = swap(from_x[..., :half, :], "row", 4), swap(from_y[..., half:, :], "row", 2)
    return diagonal + tuple(swap(piece, "row", 1) for piece in (own, from_x, from_y))


def named_pieces(own, firsts, seconds, thirds):
    half = own.shape[-2] // 2
    masks = [(0, 0), (2, 0), (4, 0), (6, 0), (6, half), (1, 0), (3, 0), (5, 0), (7, 0), (7, half)]
    return [(piece, *at) for piece, at in zip((own,) + firsts + seconds + thirds, masks)]


def shard_starts(places, shard):
    row = lax.axis_index("row")
    return [pl.multiple_of((row ^ mask) * shard + first, 16) for mask, first in places]


def request_columns(lengths_ref, begin, count):
    place = begin + lax.broadcasted_iota(jnp.int32, (count, 1), 0)
    segment, first = jnp.zeros_like(place), jnp.zeros_like(place)
    finish = jnp.int32(0)
    for s in range(lengths_ref.shape[1]):
        finish = finish + lengths_ref[0, s]
        later = place >= finish
        segment = segment + later.astype(jnp.int32)
        first = jnp.where(later, finish, first)
    return place, segment, first


def attend_block(mask, count, base, lengths_ref, valid_ref, q_ref, k_ref, v_ref, cache_ref):
    col = lax.axis_index("col")
    _, heads, slots, lanes = cache_ref.shape
    requests = valid_ref.shape[0]
    window = slots // requests
    scale = HD ** (-0.5)
    begin = pl.multiple_of((col ^ mask) * count, count)
    key_begin = pl.multiple_of(jnp.maximum(begin - window, 0), window)
    key_count = count + window
    place, segment, first = request_columns(lengths_ref, begin, count)
    first_key = jnp.maximum(first, place - window + 1)
    keys = key_begin + lax.broadcasted_iota(jnp.int32, (count, key_count), 1)
    local_mask = (keys >= first_key) & (keys <= place)
    slot = lax.broadcasted_iota(jnp.int32, (1, slots), 1)
    owner, within = slot // window, slot % window
    oldest = jnp.full_like(slot, window)
    for s in range(requests):
        oldest = jnp.where(owner == s, window - valid_ref[s], oldest)
    within = jnp.where(within >= oldest, within, -1)
    cache_mask = (owner == segment) & (within > place - first)
    outs = []
    own_rows = pl.ds(pl.multiple_of(begin - base, count), count)
    key_rows = pl.ds(pl.multiple_of(key_begin - base, window), key_count)
    for h in range(heads):
        cols = slice(h * lanes, (h + 1) * lanes)
        q, k, v = q_ref[own_rows, cols], k_ref[key_rows, cols], v_ref[key_rows, cols]
        local = lax.dot_general(q, k, NT, preferred_element_type=jnp.float32)
        cached = lax.dot_general(q, cache_ref[0, h], NT, preferred_element_type=jnp.float32)
        local = jnp.where(local_mask, local * scale, -jnp.inf)
        cached = jnp.where(cache_mask, cached * scale, -jnp.inf)
        top = jnp.maximum(
            jnp.max(local, axis=-1, keepdims=True), jnp.max(cached, axis=-1, keepdims=True)
        )
        local = jnp.exp(local - top)
        cached = jnp.exp(cached - top)
        total = jnp.sum(local, axis=-1, keepdims=True) + jnp.sum(cached, axis=-1, keepdims=True)
        summed = jnp.dot(local.astype(jnp.bfloat16), v, preferred_element_type=jnp.float32)
        summed = summed + jnp.dot(
            cached.astype(jnp.bfloat16), cache_ref[1, h], preferred_element_type=jnp.float32
        )
        outs.append((summed / total).astype(jnp.bfloat16)[:, :HD])
    blank = jnp.zeros((count, heads * (lanes - HD)), jnp.bfloat16)
    return jnp.concatenate([blank] + outs, axis=1)


def mix_rows(x, base, w_ref, taps_ref, lengths_ref, q_ref, k_ref, v_ref, padded):
    rows, part = x.shape[0], taps_ref.shape[2]
    padded[0:8, :] = jnp.zeros((8, part), jnp.float32)
    place, _, first = request_columns(lengths_ref, base, rows)
    inside = place - first
    mixed = jnp.dot(x, w_ref[...], preferred_element_type=jnp.float32)

    def convolved(raw, which):
        padded[8:, :] = raw
        running = taps_ref[0, which : which + 1, :] * raw
        for offset in range(1, taps_ref.shape[0]):
            moved = padded[8 - offset : 8 - offset + rows, :]
            tap = taps_ref[offset, which : which + 1, :]
            running = running + jnp.where(inside >= offset, tap * moved, 0.0)
        return running

    def store_heads(ref, value):
        blank = jnp.zeros((rows, LANES - HD), jnp.bfloat16)
        for h in range(part // HD):
            ref[:, h * LANES : h * LANES + HD] = value[:, h * HD : (h + 1) * HD].astype(jnp.bfloat16)
            ref[:, h * LANES + HD : (h + 1) * LANES] = blank

    store_heads(k_ref, convolved(mixed[:, :part], 0))
    store_heads(q_ref, mixed[:, part : 2 * part])
    raw_values = mixed[:, 2 * part : 3 * part]
    store_heads(v_ref, raw_values * jax.nn.sigmoid(convolved(raw_values, 1)))


def first_kernel(places, n_x, n_w, *refs):
    x_refs, w_refs = refs[:n_x], refs[n_x : n_x + n_w]
    taps_ref, lengths_ref, valid_ref, cache_ref = refs[n_x + n_w : n_x + n_w + 4]
    x_all, w_all, out_w, down_ref, up_ref, part_ref, q_ref, k_ref, v_ref, padded = refs[n_x + n_w + 4 :]
    col = lax.axis_index("col")
    count, width = x_refs[0].shape
    lanes, mixed_lanes = out_w.shape[1], w_all.shape[1]
    for i, ref in enumerate(x_refs):
        x_all[pl.ds(pl.multiple_of((col ^ i) * count, 16), count), :] = ref[...]
    shard = width // lax.axis_size("row")
    ranks = down_ref.shape[0] // lax.axis_size("row")
    starts = shard_starts(places, shard)
    for ref, start, (mask, first) in zip(w_refs, starts, places):
        rows = min(ref.shape[0], shard - first)
        w_all[pl.ds(start, rows), :] = ref[:rows, :mixed_lanes]
        out_w[pl.ds(start, rows), :] = ref[:rows, ref.shape[1] - lanes :]
        if rows < ref.shape[0]:
            at = pl.multiple_of((lax.axis_index("row") ^ mask) * ranks, 16)
            down_ref[pl.ds(at, ranks), :] = ref[rows : rows + ranks, :]
            up_ref[pl.ds(at, ranks), :] = ref[rows + ranks :, :]
    base = pl.multiple_of(jnp.maximum((col ^ (n_x - 1)) * count - count, 0), count)
    x = x_all[pl.ds(base, 2 * count), :]
    mix_rows(x, base, w_all, taps_ref, lengths_ref, q_ref, k_ref, v_ref, padded)
    attended = attend_block(
        n_x - 1, count, base, lengths_ref, valid_ref, q_ref, k_ref, v_ref, cache_ref
    )
    part_ref[...] = lax.dot_general(
        attended, out_w[...], NT, preferred_element_type=jnp.float32
    ).astype(jnp.bfloat16)


def first_call(blocks, pieces, ranks, taps, lengths, valid, cache):
    (count, width), n_x, n_w = blocks[0].shape, len(blocks), len(pieces)
    tokens, part = count * n_x, taps.shape[2]
    lanes = part // HD * LANES
    mixed_lanes = -(-3 * part // LANES) * LANES
    places = [(mask, first) for _, mask, first in pieces]
    shapes = [(tokens, width), (width, mixed_lanes), (width, lanes), (ranks, width), (ranks, width), (count, width)]
    return pl.pallas_call(
        functools.partial(first_kernel, places, n_x, n_w),
        out_shape=[pltpu.VMEM(shape, jnp.bfloat16) for shape in shapes[:3]]
        + [jax.ShapeDtypeStruct(shape, jnp.bfloat16) for shape in shapes[3:]],
        in_specs=[VMEM] * (n_x + n_w + 1) + [SMEM, SMEM, VMEM],
        out_specs=[VMEM] * len(shapes),
        scratch_shapes=[pltpu.VMEM((2 * count, lanes), jnp.bfloat16)] * 3
        + [pltpu.VMEM((2 * count + 8, part), jnp.float32)],
        compiler_params=params(28),
        cost_estimate=LIGHT,
    )(*blocks, *(piece for piece, _, _ in pieces), taps, lengths, valid, cache)


def rest_kernel(masks, x_all, w_all, out_w, taps_ref, lengths_ref, valid_ref, cache_ref, *refs):
    q_ref, k_ref, v_ref = refs[:3]
    out_refs, padded = refs[3:-1], refs[-1]
    mix_rows(x_all[...], 0, w_all, taps_ref, lengths_ref, q_ref, k_ref, v_ref, padded)
    for mask, out_ref in zip(masks, out_refs):
        attended = attend_block(
            mask, out_ref.shape[0], 0, lengths_ref, valid_ref, q_ref, k_ref, v_ref, cache_ref
        )
        out_ref[...] = lax.dot_general(
            attended, out_w[...], NT, preferred_element_type=jnp.float32
        ).astype(out_ref.dtype)


def rest_call(masks, count, x_all, w_all, out_w, taps, lengths, valid, cache):
    (tokens, width), lanes = x_all.shape, out_w.shape[1]
    shapes = [(tokens, lanes)] * 3 + [(count, width)] * len(masks)
    return pl.pallas_call(
        functools.partial(rest_kernel, masks),
        out_shape=[jax.ShapeDtypeStruct(shape, jnp.bfloat16) for shape in shapes],
        in_specs=[VMEM] * 4 + [SMEM, SMEM, VMEM],
        out_specs=[VMEM] * len(shapes),
        scratch_shapes=[pltpu.VMEM((tokens + 8, taps.shape[2]), jnp.float32)],
        compiler_params=params(32),
        cost_estimate=LIGHT,
    )(x_all, w_all, out_w, taps, lengths, valid, cache)


def own_kernel(rank, q_ref, k_ref, v_ref, out_w, x_ref, ids_ref, down_ref, up_ref, *refs):
    lengths_ref, valid_ref, cache_ref, out_ref = refs
    attended = attend_block(
        0, out_ref.shape[0], 0, lengths_ref, valid_ref, q_ref, k_ref, v_ref, cache_ref
    )
    part = lax.dot_general(attended, out_w[...], NT, preferred_element_type=jnp.float32)
    out_ref[...] = part + adapter_term(x_ref, ids_ref, down_ref, up_ref, rank).astype(jnp.float32)


def own_call(rank, q, k, v, out_w, x, ids, down, up, lengths, valid, cache):
    return pl.pallas_call(
        functools.partial(own_kernel, rank),
        out_shape=jax.ShapeDtypeStruct(x.shape, jnp.float32),
        in_specs=[VMEM] * 8 + [SMEM, SMEM, VMEM],
        out_specs=VMEM,
        compiler_params=params(20),
        cost_estimate=LIGHT,
    )(q, k, v, out_w, x, ids, down, up, lengths, valid, cache)


def feed(x, all_w):
    gate = jnp.dot(x, all_w[0], preferred_element_type=jnp.float32)
    up = jnp.dot(x, all_w[1], preferred_element_type=jnp.float32)
    act = (jax.nn.silu(gate) * up).astype(jnp.bfloat16)
    return lax.dot_general(act, all_w[2], NT, preferred_element_type=jnp.float32)


def feed_first_kernel(places, n_x, n_w, *refs):
    x_refs, w_refs = refs[:n_x], refs[n_x : n_x + n_w]
    all_w, out_refs = refs[n_x + n_w], refs[n_x + n_w + 1 :]
    starts = shard_starts(places, all_w.shape[1] // lax.axis_size("row"))
    for part in range(3):
        for ref, start in zip(w_refs, starts):
            all_w[part, pl.ds(start, ref.shape[1]), :] = ref[part]
    down = feed(jnp.concatenate([ref[...] for ref in x_refs], axis=0), all_w)
    count = x_refs[0].shape[0]
    for i, ref in enumerate(out_refs):
        ref[...] = down[i * count : (i + 1) * count].astype(ref.dtype)


def feed_first_call(blocks, pieces, out_types):
    n_x, n_w, (count, width) = len(blocks), len(pieces), blocks[0].shape
    places = [(mask, first) for _, mask, first in pieces]
    hidden = pieces[0][0].shape[2]
    return pl.pallas_call(
        functools.partial(feed_first_kernel, places, n_x, n_w),
        out_shape=[pltpu.VMEM((3, width, hidden), jnp.bfloat16)]
        + [jax.ShapeDtypeStruct((count, width), t) for t in out_types],
        in_specs=[VMEM] * (n_x + n_w),
        out_specs=[VMEM] * (n_x + 1),
        compiler_params=params(28),
        cost_estimate=LIGHT,
    )(*blocks, *(piece for piece, _, _ in pieces))


def feed_last_kernel(x_ref, all_w, near_ref, far_ref):
    down = feed(x_ref[...], all_w).astype(near_ref.dtype)
    near_ref[...] = down[: near_ref.shape[0]]
    far_ref[...] = down[near_ref.shape[0] :]


def feed_last_call(block, all_w, near):
    count, width = block.shape
    return pl.pallas_call(
        feed_last_kernel,
        out_shape=[
            jax.ShapeDtypeStruct((rows, width), jnp.bfloat16) for rows in (near, count - near)
        ],
        in_specs=[VMEM] * 2,
        out_specs=[VMEM] * 2,
        compiler_params=params(20),
        cost_estimate=LIGHT,
    )(block, all_w)


def sum_kernel(part_ref, passed_ref, out_ref):
    near = passed_ref.shape[0]
    both = part_ref[:near].astype(jnp.float32) + passed_ref[...].astype(jnp.float32)
    out_ref[:near] = both.astype(out_ref.dtype)
    out_ref[near:] = part_ref[near:]


def sum_call(part, passed):
    return pl.pallas_call(
        sum_kernel,
        out_shape=jax.ShapeDtypeStruct(part.shape, jnp.bfloat16),
        in_specs=[VMEM] * 2,
        out_specs=VMEM,
        compiler_params=params(12),
        cost_estimate=LIGHT,
    )(part, passed)


def last_kernel(residual_ref, own_ref, two_ref, one_ref, far_ref, out_ref):
    near = out_ref.shape[0] - far_ref.shape[0]
    total = own_ref[...] + one_ref[...].astype(jnp.float32) + two_ref[...].astype(jnp.float32)
    residual = residual_ref[...].astype(jnp.float32)
    far = total[near:] + far_ref[...].astype(jnp.float32)
    out_ref[:near] = (residual[:near] + total[:near]).astype(out_ref.dtype)
    out_ref[near:] = (residual[near:] + far).astype(out_ref.dtype)


def last_call(residual, own, two, one, far):
    return pl.pallas_call(
        last_kernel,
        out_shape=jax.ShapeDtypeStruct(residual.shape, jnp.bfloat16),
        in_specs=[VMEM] * 5,
        out_specs=VMEM,
        compiler_params=params(12),
        cost_estimate=LIGHT,
    )(residual, own, two, one, far)


def tuned(
    inputs,
    attention_norm_gain,
    query_key_value_weight,
    filter_taps,
    output_projection,
    window_key_value,
    cache_valid_length,
    lengths,
    token_adapter_index,
    adapter_down_map,
    adapter_up_map,
    feed_forward_gain,
    gate_projection,
    up_projection,
    down_projection,
):
    bf16, f32 = jnp.bfloat16, jnp.float32
    col = lax.axis_index("col")
    count, width = inputs.shape
    heads = window_key_value.shape[2]

    rank, kept = adapter_down_map.shape[2], adapter_down_map.shape[0]
    normed_attention, packed = entry_call(
        inputs,
        jnp.transpose(query_key_value_weight, (1, 0, 2)),
        output_projection,
        attention_norm_gain,
        jnp.transpose(adapter_down_map, (0, 2, 1)).reshape(kept * rank, width),
        adapter_up_map.reshape(kept * rank, width),
    )
    token_two, token_one = swap(normed_attention, "col", 2), swap(normed_attention, "col", 1)
    firsts = first_hops(packed)
    requests = window_key_value.shape[0]
    window = window_key_value.shape[3] // HD
    cache = window_key_value.reshape(requests, 2, heads, window, HD)
    cache = jnp.transpose(cache, (1, 2, 0, 3, 4)).reshape(2, heads, requests * window, HD)
    cache = jnp.pad(cache, ((0, 0), (0, 0), (0, 0), (0, LANES - HD)))
    own_ids = lax.dynamic_slice_in_dim(token_adapter_index, col * count, count, 0)
    feed_own = jnp.concatenate(
        [gate_projection[None], up_projection[None], jnp.transpose(down_projection)[None]], axis=0
    )
    firsts, cache, own_ids, feed_own = lax.optimization_barrier((firsts, cache, own_ids, feed_own))
    token_two, token_one, cache = lax.optimization_barrier((token_two, token_one, cache))
    token_three = swap(token_two, "col", 1)
    seconds = second_hops(packed, *firsts)
    token_three, diagonal, feed_own = lax.optimization_barrier((token_three, seconds[:2], feed_own))
    seconds = diagonal + seconds[2:]
    thirds = tuple(swap(piece, "row", 1) for piece in diagonal)
    feed_firsts = first_hops(feed_own)

    pieces = named_pieces(packed, firsts, seconds, thirds)
    blocks = [normed_attention, token_one, token_two, token_three]
    requests_here = (lengths, cache_valid_length, cache)
    ranks = kept * rank * lax.axis_size("row")
    x_all, w_all, out_w, down_maps, up_maps, part_three = first_call(
        blocks, pieces, ranks, filter_taps, *requests_here
    )
    passed = swap(part_three, "col", 1)
    q, k, v, part_two, part_one = rest_call(
        [2, 1], count, x_all, w_all, out_w, filter_taps, *requests_here
    )
    part_own = own_call(
        rank, q, k, v, out_w, normed_attention, own_ids, down_maps, up_maps, *requests_here
    )
    got_one = swap(part_one, "col", 1)
    got_two = swap((part_two.astype(f32) + passed.astype(f32)).astype(bf16), "col", 2)
    got_one, *hops = lax.optimization_barrier((got_one, *feed_firsts))
    feed_seconds = second_hops(feed_own, *hops)
    residual, normed_mlp = residual_call(inputs, part_own, got_two, got_one, feed_forward_gain)
    token_two, token_one = swap(normed_mlp, "col", 2), swap(normed_mlp, "col", 1)
    feed_thirds = tuple(swap(piece, "row", 1) for piece in feed_seconds[:2])
    token_two, token_one = lax.optimization_barrier((token_two, token_one))
    token_three = swap(token_two, "col", 1)
    feed_pieces = named_pieces(feed_own, feed_firsts, feed_seconds, feed_thirds)
    feed_w, part_two, part_one, part_own = feed_first_call(
        [token_two, token_one, normed_mlp], feed_pieces, [bf16, bf16, f32]
    )
    near, far = feed_last_call(token_three, feed_w, count * 5 // 8)
    passed, got_far = swap(near, "col", 1), swap(far, "col", 3)
    part_two = sum_call(part_two, passed)
    got_two = swap(part_two, "col", 2)
    _, got_far, part_one = lax.optimization_barrier((part_two, got_far, part_one))
    got_one = swap(part_one, "col", 1)
    return last_call(residual, part_own, got_two, got_one, got_far)


def on_device(*args):
    rows, cols = lax.axis_size("row"), lax.axis_size("col")
    if (rows, cols) == (8, 4):
        return tuned(*args)
    return plain(*args)


def solution(mesh):
    placed = (
        P(("row", "col"), None),
        P(),
        P("row", None, "col"),
        P(None, None, "col"),
        P("col", "row"),
        P("row", None, "col", None),
        P("row"),
        P("row", None),
        P("row", None),
        P("row", None, None),
        P("row", None, None),
        P(),
        P("row", "col"),
        P("row", "col"),
        P("col", "row"),
    )
    return jax.shard_map(
        on_device, mesh=mesh, in_specs=placed, out_specs=P(("row", "col"), None), check_vma=False
    )
```

```python
import functools

import jax
import jax.numpy as jnp
from jax import lax
from jax.experimental import pallas as pl
from jax.experimental.pallas import tpu as pltpu
from jax.sharding import PartitionSpec as P

HD = 112


epsilon = 1e-05


def rms_scaled(values, gain_row):
    mean_square = jnp.mean(values * values, axis=-1, keepdims=True)
    return values * lax.rsqrt(mean_square + epsilon) * gain_row


def layout(lengths_row, tok_count):
    finish = jnp.cumsum(lengths_row)
    begins = finish - lengths_row
    places = jnp.arange(tok_count, dtype=jnp.int32)
    segment = jnp.sum((places[:, None] >= finish[None, :]).astype(jnp.int32), axis=1)
    member = segment[:, None] == jnp.arange(lengths_row.shape[0], dtype=jnp.int32)[None, :]
    inside = places - jnp.sum(jnp.where(member, begins[None, :], 0), axis=1)
    return (segment, inside)


def shifted(values, offset, inside):
    moved_rows = jnp.pad(values[: values.shape[0] - offset], ((offset, 0), (0, 0)))
    return jnp.where((inside >= offset)[:, None], moved_rows, jnp.zeros_like(moved_rows))


def convolve(values, taps, inside):
    running = jnp.zeros_like(values)
    for offset in range(taps.shape[0]):
        running = running + taps[offset][None, :] * shifted(values, offset, inside)
    return running


def make_qkv(qkv_mixed, filter_taps, inside):
    queries = qkv_mixed[:, 0].astype(jnp.bfloat16)
    keys_used = convolve(qkv_mixed[:, 1], filter_taps[:, 0], inside).astype(jnp.bfloat16)
    raw_values = qkv_mixed[:, 2]
    gates = jax.nn.sigmoid(convolve(raw_values, filter_taps[:, 1], inside))
    values_used = (raw_values * gates).astype(jnp.bfloat16)
    return (queries, keys_used, values_used)


def split_cache(window_key_value, head_size):
    requests_here, head_count = (window_key_value.shape[0], window_key_value.shape[2])
    window = window_key_value.shape[3] // head_size
    split_kv = window_key_value.reshape(requests_here, 2, head_count, window, head_size)
    cached_key_rows = jnp.transpose(split_kv[:, 0], (0, 2, 1, 3)).reshape(
        requests_here * window, head_count, head_size
    )
    cached_value_rows = jnp.transpose(split_kv[:, 1], (0, 2, 1, 3)).reshape(
        requests_here * window, head_count, head_size
    )
    return (cached_key_rows, cached_value_rows, window)


def attend(
    queries,
    keys_used,
    values_used,
    window_key_value,
    segment,
    inside,
    cache_valid_length,
    head_size,
):
    tok_count = queries.shape[0]
    head_count = queries.shape[1] // head_size
    requests_here = window_key_value.shape[0]
    cached_key_rows, cached_value_rows, window = split_cache(window_key_value, head_size)
    query_per_head = queries.reshape(tok_count, head_count, head_size)
    key_h = keys_used.reshape(tok_count, head_count, head_size)
    value_per_head = values_used.reshape(tok_count, head_count, head_size)
    attention_score_scale = head_size ** (-0.5)
    places = jnp.arange(tok_count, dtype=jnp.int32)
    local_mask = (
        (segment[:, None] == segment[None, :])
        & (places[None, :] <= places[:, None])
        & (places[None, :] > places[:, None] - window)
    )
    slot_ids = jnp.arange(requests_here * window, dtype=jnp.int32)
    owner_req = slot_ids // window
    within = slot_ids % window
    slot_ages = jnp.repeat(cache_valid_length, window)
    cache_mask = (
        (segment[:, None] == owner_req[None, :])
        & (within[None, :] >= window - slot_ages[None, :])
        & (within[None, :] > inside[:, None])
    )
    local_scores = (
        jnp.einsum("thd,jhd->htj", query_per_head, key_h, preferred_element_type=jnp.float32)
        * attention_score_scale
    )
    cached_score_rows = (
        jnp.einsum(
            "sek,yek->esy", query_per_head, cached_key_rows, preferred_element_type=jnp.float32
        )
        * attention_score_scale
    )
    local_scores = jnp.where(local_mask[None], local_scores, -jnp.inf)
    cached_score_rows = jnp.where(cache_mask[None], cached_score_rows, -jnp.inf)
    row_max = jnp.maximum(
        jnp.max(local_scores, axis=-1, keepdims=True),
        jnp.max(cached_score_rows, axis=-1, keepdims=True),
    )
    local_exp = jnp.exp(local_scores - row_max)
    cache_exp = jnp.exp(cached_score_rows - row_max)
    denominator = jnp.sum(local_exp, axis=-1, keepdims=True) + jnp.sum(
        cache_exp, axis=-1, keepdims=True
    )
    window_attention_weight = (local_exp / denominator).astype(jnp.bfloat16)
    cached_attention_weight = (cache_exp / denominator).astype(jnp.bfloat16)
    joined_output = jnp.einsum(
        "zkc,czu->kzu", window_attention_weight, value_per_head, preferred_element_type=jnp.float32
    )
    joined_output = joined_output + jnp.einsum(
        "lar,rlx->alx",
        cached_attention_weight,
        cached_value_rows,
        preferred_element_type=jnp.float32,
    )
    return joined_output.reshape(tok_count, head_count * head_size).astype(jnp.bfloat16)


def plain(
    inputs,
    attention_norm_gain,
    query_key_value_weight,
    filter_taps,
    output_projection,
    window_key_value,
    cache_valid_length,
    lengths,
    token_adapter_index,
    adapter_down_map,
    adapter_up_map,
    feed_forward_gain,
    gate_projection,
    up_projection,
    down_projection,
):
    own_count = inputs.shape[0]
    column = lax.axis_index("col")
    row_count = lax.axis_size("row")
    gathered = lax.all_gather(inputs, "col", axis=0, tiled=True)
    tok_count = gathered.shape[0]
    normalized_input = rms_scaled(gathered.astype(jnp.float32), attention_norm_gain).astype(
        jnp.bfloat16
    )
    qkv_mixed = jnp.einsum(
        "td,dka->tka",
        normalized_input,
        lax.all_gather(query_key_value_weight, "row", axis=0, tiled=True),
        preferred_element_type=jnp.float32,
    )
    segment, inside = layout(lengths[0], tok_count)
    queries, keys_used, values_used = make_qkv(qkv_mixed, filter_taps, inside)
    attended = attend(
        queries, keys_used, values_used, window_key_value, segment, inside, cache_valid_length, HD
    )
    kept_count = adapter_down_map.shape[0]
    every_adapter = kept_count * row_count
    capacity = max(2, 2 * own_count // every_adapter)
    first_row = column * own_count
    own_rows = lax.dynamic_slice_in_dim(normalized_input, first_row, own_count, 0)
    own_ids = lax.dynamic_slice_in_dim(token_adapter_index[:, 0], first_row, own_count, 0)
    member = (own_ids[:, None] == jnp.arange(every_adapter, dtype=jnp.int32)[None, :]).astype(
        jnp.int32
    )
    before = jnp.cumsum(member, axis=0) - member
    slot_rank = jnp.sum(before * member, axis=1)
    target = own_ids * capacity + slot_rank
    placer = (
        target[None, :] == jnp.arange(every_adapter * capacity, dtype=jnp.int32)[:, None]
    ).astype(jnp.bfloat16)
    outgoing = jnp.dot(placer, own_rows, preferred_element_type=jnp.float32).astype(jnp.bfloat16)
    outgoing = outgoing.reshape(row_count, kept_count, capacity, normalized_input.shape[1])
    reduced_rank_input = jnp.einsum(
        "sakd,adr->sakr",
        lax.all_to_all(outgoing, "row", split_axis=0, concat_axis=0, tiled=True),
        adapter_down_map,
        preferred_element_type=jnp.float32,
    ).astype(jnp.bfloat16)
    answered = jnp.einsum(
        "zjbf,jfm->zjbm", reduced_rank_input, adapter_up_map, preferred_element_type=jnp.float32
    ).astype(jnp.bfloat16)
    returned = lax.all_to_all(answered, "row", split_axis=0, concat_axis=0, tiled=True).reshape(
        every_adapter * capacity, normalized_input.shape[1]
    )
    delta_rows = jnp.dot(jnp.transpose(placer), returned, preferred_element_type=jnp.float32)
    out_term = jnp.dot(
        attended,
        lax.all_gather(output_projection, "row", axis=1, tiled=True),
        preferred_element_type=jnp.float32,
    )
    own_term = lax.dynamic_slice_in_dim(out_term, first_row, own_count, 0) + delta_rows
    out_term = lax.dynamic_update_slice_in_dim(out_term, own_term, first_row, 0)
    attn_share = lax.psum_scatter(
        out_term.astype(jnp.bfloat16), "col", scatter_dimension=0, tiled=True
    ).astype(jnp.float32)
    residual = (inputs.astype(jnp.float32) + attn_share).astype(jnp.bfloat16)
    whole_mixed = lax.all_gather(residual, "col", axis=0, tiled=True)
    normed_mlp = rms_scaled(whole_mixed.astype(jnp.float32), feed_forward_gain).astype(jnp.bfloat16)

    def add_rows(piece):
        return jnp.dot(normed_mlp, piece, preferred_element_type=jnp.float32)

    gate = add_rows(lax.all_gather(gate_projection, "row", axis=0, tiled=True))
    up_part = add_rows(lax.all_gather(up_projection, "row", axis=0, tiled=True))
    hidden = (jax.nn.silu(gate) * up_part).astype(jnp.bfloat16)
    down_term = jnp.dot(
        hidden,
        lax.all_gather(down_projection, "row", axis=1, tiled=True),
        preferred_element_type=jnp.float32,
    )
    mlp_added = lax.psum_scatter(
        down_term.astype(jnp.bfloat16), "col", scatter_dimension=0, tiled=True
    ).astype(jnp.float32)
    return (residual.astype(jnp.float32) + mlp_added).astype(jnp.bfloat16)


LANES = 128
MIB = 1 << 20


LIGHT = pl.CostEstimate(flops=1, bytes_accessed=1, transcendentals=0)


def params(mib):
    return pltpu.CompilerParams(vmem_limit_bytes=mib * MIB)


HBM = pl.BlockSpec(memory_space=pl.ANY)
VMEM = pl.BlockSpec(memory_space=pltpu.VMEM)
SMEM = pl.BlockSpec(memory_space=pltpu.SMEM)
NT = (((1,), (1,)), ((), ()))


def normed(values, gain):
    mean_square = jnp.mean(values * values, axis=-1, keepdims=True)
    return (values * lax.rsqrt(mean_square + epsilon) * gain).astype(jnp.bfloat16)


def entry_kernel(*refs):
    sources, (normed_ref, packed_ref) = refs[:6], refs[6:8]
    targets, sems = refs[8:14], refs[14]
    loads = [
        pltpu.make_async_copy(source, target, sems.at[i])
        for i, (source, target) in enumerate(zip(sources, targets))
    ]
    for load in loads:
        load.start()
    x_ref, qkv_ref, out_ref, gain_ref, down_ref, up_ref = targets
    rows, part, ranks = qkv_ref.shape[1], qkv_ref.shape[2], down_ref.shape[0]
    loads[0].wait()
    loads[3].wait()
    normed_ref[...] = normed(x_ref[...].astype(jnp.float32), gain_ref[...][None, :])
    for at in (1, 2, 4, 5):
        loads[at].wait()
    for place, which in enumerate((1, 0, 2)):
        packed_ref[:rows, place * part : (place + 1) * part] = qkv_ref[which]
    out_rows = jnp.transpose(out_ref[...].astype(jnp.float32)).astype(jnp.bfloat16)
    packed_ref[:rows, 3 * part :] = out_rows
    packed_ref[rows : rows + ranks, :] = down_ref[...]
    packed_ref[rows + ranks :, :] = up_ref[...]


def entry_call(rows, qkv, out, gain, down, up):
    sources = (rows, qkv, out, gain, down, up)
    return pl.pallas_call(
        entry_kernel,
        out_shape=[
            jax.ShapeDtypeStruct(rows.shape, jnp.bfloat16),
            jax.ShapeDtypeStruct((qkv.shape[1] + 2 * down.shape[0], 4 * qkv.shape[2]), jnp.bfloat16),
        ],
        in_specs=[HBM] * len(sources),
        out_specs=[VMEM] * 2,
        scratch_shapes=[pltpu.VMEM(source.shape, source.dtype) for source in sources]
        + [pltpu.SemaphoreType.DMA((len(sources),))],
        compiler_params=params(60),
        cost_estimate=LIGHT,
    )(*sources)


def residual_kernel(x_ref, own_ref, two_ref, one_ref, gain_ref, residual_ref, normed_ref):
    total = own_ref[...] + one_ref[...].astype(jnp.float32) + two_ref[...].astype(jnp.float32)
    residual = (x_ref[...].astype(jnp.float32) + total).astype(jnp.bfloat16)
    residual_ref[...] = residual
    normed_ref[...] = normed(residual.astype(jnp.float32), gain_ref[...])


def residual_call(rows, own, two, one, gain):
    block = jax.ShapeDtypeStruct(rows.shape, jnp.bfloat16)
    return pl.pallas_call(
        residual_kernel,
        out_shape=[block, block],
        in_specs=[VMEM] * 5,
        out_specs=[VMEM] * 2,
        compiler_params=params(12),
        cost_estimate=LIGHT,
    )(rows, own, two, one, gain[None, :])


def adapter_term(x_ref, ids_ref, down_ref, up_ref, rank):
    low = lax.dot_general(x_ref[...], down_ref[...], NT, preferred_element_type=jnp.float32)
    adapter = lax.broadcasted_iota(jnp.int32, low.shape, 1) // rank
    low = jnp.where(ids_ref[...] == adapter, low, 0.0).astype(jnp.bfloat16)
    return jnp.dot(low, up_ref[...], preferred_element_type=jnp.float32).astype(jnp.bfloat16)


def xor_pairs(count, mask):
    return [(i, i ^ mask) for i in range(count)]


def swap(value, axis, mask):
    return lax.ppermute(value, axis, xor_pairs(lax.axis_size(axis), mask))


def first_hops(own):
    return swap(own, "row", 2), swap(own, "row", 4)


def second_hops(own, from_x, from_y):
    half = own.shape[-2] // 2
    diagonal = swap(from_x[..., :half, :], "row", 4), swap(from_y[..., half:, :], "row", 2)
    return diagonal + tuple(swap(piece, "row", 1) for piece in (own, from_x, from_y))


def named_pieces(own, firsts, seconds, thirds):
    half = own.shape[-2] // 2
    masks = [(0, 0), (2, 0), (4, 0), (6, 0), (6, half), (1, 0), (3, 0), (5, 0), (7, 0), (7, half)]
    return [(piece, *at) for piece, at in zip((own,) + firsts + seconds + thirds, masks)]


def shard_starts(places, shard):
    row = lax.axis_index("row")
    return [pl.multiple_of((row ^ mask) * shard + first, 16) for mask, first in places]


def request_columns(lengths_ref, begin, count):
    place = begin + lax.broadcasted_iota(jnp.int32, (count, 1), 0)
    segment, first = jnp.zeros_like(place), jnp.zeros_like(place)
    finish = jnp.int32(0)
    for s in range(lengths_ref.shape[1]):
        finish = finish + lengths_ref[0, s]
        later = place >= finish
        segment = segment + later.astype(jnp.int32)
        first = jnp.where(later, finish, first)
    return place, segment, first


def attend_block(mask, count, base, lengths_ref, valid_ref, q_ref, k_ref, v_ref, cache_ref):
    col = lax.axis_index("col")
    _, heads, slots, lanes = cache_ref.shape
    requests = valid_ref.shape[0]
    window = slots // requests
    scale = HD ** (-0.5)
    begin = pl.multiple_of((col ^ mask) * count, count)
    key_begin = pl.multiple_of(jnp.maximum(begin - window, 0), window)
    key_count = count + window
    place, segment, first = request_columns(lengths_ref, begin, count)
    first_key = jnp.maximum(first, place - window + 1)
    keys = key_begin + lax.broadcasted_iota(jnp.int32, (count, key_count), 1)
    local_mask = (keys >= first_key) & (keys <= place)
    slot = lax.broadcasted_iota(jnp.int32, (1, slots), 1)
    owner, within = slot // window, slot % window
    oldest = jnp.full_like(slot, window)
    for s in range(requests):
        oldest = jnp.where(owner == s, window - valid_ref[s], oldest)
    within = jnp.where(within >= oldest, within, -1)
    cache_mask = (owner == segment) & (within > place - first)
    outs = []
    own_rows = pl.ds(pl.multiple_of(begin - base, count), count)
    key_rows = pl.ds(pl.multiple_of(key_begin - base, window), key_count)
    for h in range(heads):
        cols = slice(h * lanes, (h + 1) * lanes)
        q, k, v = q_ref[own_rows, cols], k_ref[key_rows, cols], v_ref[key_rows, cols]
        local = lax.dot_general(q, k, NT, preferred_element_type=jnp.float32)
        cached = lax.dot_general(q, cache_ref[0, h], NT, preferred_element_type=jnp.float32)
        local = jnp.where(local_mask, local * scale, -jnp.inf)
        cached = jnp.where(cache_mask, cached * scale, -jnp.inf)
        top = jnp.maximum(
            jnp.max(local, axis=-1, keepdims=True), jnp.max(cached, axis=-1, keepdims=True)
        )
        local = jnp.exp(local - top)
        cached = jnp.exp(cached - top)
        total = jnp.sum(local, axis=-1, keepdims=True) + jnp.sum(cached, axis=-1, keepdims=True)
        summed = jnp.dot(local.astype(jnp.bfloat16), v, preferred_element_type=jnp.float32)
        summed = summed + jnp.dot(
            cached.astype(jnp.bfloat16), cache_ref[1, h], preferred_element_type=jnp.float32
        )
        outs.append((summed / total).astype(jnp.bfloat16)[:, :HD])
    blank = jnp.zeros((count, heads * (lanes - HD)), jnp.bfloat16)
    return jnp.concatenate([blank] + outs, axis=1)


def mix_rows(x, base, w_ref, taps_ref, lengths_ref, q_ref, k_ref, v_ref, padded):
    rows, part = x.shape[0], taps_ref.shape[2]
    padded[0:8, :] = jnp.zeros((8, part), jnp.float32)
    place, _, first = request_columns(lengths_ref, base, rows)
    inside = place - first
    mixed = jnp.dot(x, w_ref[...], preferred_element_type=jnp.float32)

    def convolved(raw, which):
        padded[8:, :] = raw
        running = taps_ref[0, which : which + 1, :] * raw
        for offset in range(1, taps_ref.shape[0]):
            moved = padded[8 - offset : 8 - offset + rows, :]
            tap = taps_ref[offset, which : which + 1, :]
            running = running + jnp.where(inside >= offset, tap * moved, 0.0)
        return running

    def store_heads(ref, value):
        blank = jnp.zeros((rows, LANES - HD), jnp.bfloat16)
        for h in range(part // HD):
            ref[:, h * LANES : h * LANES + HD] = value[:, h * HD : (h + 1) * HD].astype(jnp.bfloat16)
            ref[:, h * LANES + HD : (h + 1) * LANES] = blank

    store_heads(k_ref, convolved(mixed[:, :part], 0))
    store_heads(q_ref, mixed[:, part : 2 * part])
    raw_values = mixed[:, 2 * part : 3 * part]
    store_heads(v_ref, raw_values * jax.nn.sigmoid(convolved(raw_values, 1)))


def first_kernel(places, n_x, n_w, *refs):
    x_refs, w_refs = refs[:n_x], refs[n_x : n_x + n_w]
    taps_ref, lengths_ref, valid_ref, cache_ref = refs[n_x + n_w : n_x + n_w + 4]
    x_all, w_all, out_w, down_ref, up_ref, part_ref, q_ref, k_ref, v_ref, padded = refs[n_x + n_w + 4 :]
    col = lax.axis_index("col")
    count, width = x_refs[0].shape
    lanes, mixed_lanes = out_w.shape[1], w_all.shape[1]
    for i, ref in enumerate(x_refs):
        x_all[pl.ds(pl.multiple_of((col ^ i) * count, 16), count), :] = ref[...]
    shard = width // lax.axis_size("row")
    ranks = down_ref.shape[0] // lax.axis_size("row")
    starts = shard_starts(places, shard)
    for ref, start, (mask, first) in zip(w_refs, starts, places):
        rows = min(ref.shape[0], shard - first)
        w_all[pl.ds(start, rows), :] = ref[:rows, :mixed_lanes]
        out_w[pl.ds(start, rows), :] = ref[:rows, ref.shape[1] - lanes :]
        if rows < ref.shape[0]:
            at = pl.multiple_of((lax.axis_index("row") ^ mask) * ranks, 16)
            down_ref[pl.ds(at, ranks), :] = ref[rows : rows + ranks, :]
            up_ref[pl.ds(at, ranks), :] = ref[rows + ranks :, :]
    base = pl.multiple_of(jnp.maximum((col ^ (n_x - 1)) * count - count, 0), count)
    x = x_all[pl.ds(base, 2 * count), :]
    mix_rows(x, base, w_all, taps_ref, lengths_ref, q_ref, k_ref, v_ref, padded)
    attended = attend_block(
        n_x - 1, count, base, lengths_ref, valid_ref, q_ref, k_ref, v_ref, cache_ref
    )
    part_ref[...] = lax.dot_general(
        attended, out_w[...], NT, preferred_element_type=jnp.float32
    ).astype(jnp.bfloat16)


def first_call(blocks, pieces, ranks, taps, lengths, valid, cache):
    (count, width), n_x, n_w = blocks[0].shape, len(blocks), len(pieces)
    tokens, part = count * n_x, taps.shape[2]
    lanes = part // HD * LANES
    mixed_lanes = -(-3 * part // LANES) * LANES
    places = [(mask, first) for _, mask, first in pieces]
    shapes = [(tokens, width), (width, mixed_lanes), (width, lanes), (ranks, width), (ranks, width), (count, width)]
    return pl.pallas_call(
        functools.partial(first_kernel, places, n_x, n_w),
        out_shape=[pltpu.VMEM(shape, jnp.bfloat16) for shape in shapes[:3]]
        + [jax.ShapeDtypeStruct(shape, jnp.bfloat16) for shape in shapes[3:]],
        in_specs=[VMEM] * (n_x + n_w + 1) + [SMEM, SMEM, VMEM],
        out_specs=[VMEM] * len(shapes),
        scratch_shapes=[pltpu.VMEM((2 * count, lanes), jnp.bfloat16)] * 3
        + [pltpu.VMEM((2 * count + 8, part), jnp.float32)],
        compiler_params=params(28),
        cost_estimate=LIGHT,
    )(*blocks, *(piece for piece, _, _ in pieces), taps, lengths, valid, cache)


def rest_kernel(masks, x_all, w_all, out_w, taps_ref, lengths_ref, valid_ref, cache_ref, *refs):
    q_ref, k_ref, v_ref = refs[:3]
    out_refs, padded = refs[3:-1], refs[-1]
    mix_rows(x_all[...], 0, w_all, taps_ref, lengths_ref, q_ref, k_ref, v_ref, padded)
    for mask, out_ref in zip(masks, out_refs):
        attended = attend_block(
            mask, out_ref.shape[0], 0, lengths_ref, valid_ref, q_ref, k_ref, v_ref, cache_ref
        )
        out_ref[...] = lax.dot_general(
            attended, out_w[...], NT, preferred_element_type=jnp.float32
        ).astype(out_ref.dtype)


def rest_call(masks, count, x_all, w_all, out_w, taps, lengths, valid, cache):
    (tokens, width), lanes = x_all.shape, out_w.shape[1]
    shapes = [(tokens, lanes)] * 3 + [(count, width)] * len(masks)
    return pl.pallas_call(
        functools.partial(rest_kernel, masks),
        out_shape=[jax.ShapeDtypeStruct(shape, jnp.bfloat16) for shape in shapes],
        in_specs=[VMEM] * 4 + [SMEM, SMEM, VMEM],
        out_specs=[VMEM] * len(shapes),
        scratch_shapes=[pltpu.VMEM((tokens + 8, taps.shape[2]), jnp.float32)],
        compiler_params=params(32),
        cost_estimate=LIGHT,
    )(x_all, w_all, out_w, taps, lengths, valid, cache)


def own_kernel(rank, q_ref, k_ref, v_ref, out_w, x_ref, ids_ref, down_ref, up_ref, *refs):
    lengths_ref, valid_ref, cache_ref, out_ref = refs
    attended = attend_block(
        0, out_ref.shape[0], 0, lengths_ref, valid_ref, q_ref, k_ref, v_ref, cache_ref
    )
    part = lax.dot_general(attended, out_w[...], NT, preferred_element_type=jnp.float32)
    out_ref[...] = part + adapter_term(x_ref, ids_ref, down_ref, up_ref, rank).astype(jnp.float32)


def own_call(rank, q, k, v, out_w, x, ids, down, up, lengths, valid, cache):
    return pl.pallas_call(
        functools.partial(own_kernel, rank),
        out_shape=jax.ShapeDtypeStruct(x.shape, jnp.float32),
        in_specs=[VMEM] * 8 + [SMEM, SMEM, VMEM],
        out_specs=VMEM,
        compiler_params=params(20),
        cost_estimate=LIGHT,
    )(q, k, v, out_w, x, ids, down, up, lengths, valid, cache)


def feed(x, all_w):
    gate = jnp.dot(x, all_w[0], preferred_element_type=jnp.float32)
    up = jnp.dot(x, all_w[1], preferred_element_type=jnp.float32)
    act = (jax.nn.silu(gate) * up).astype(jnp.bfloat16)
    return lax.dot_general(act, all_w[2], NT, preferred_element_type=jnp.float32)


def feed_first_kernel(places, n_x, n_w, *refs):
    x_refs, w_refs = refs[:n_x], refs[n_x : n_x + n_w]
    all_w, out_refs = refs[n_x + n_w], refs[n_x + n_w + 1 :]
    starts = shard_starts(places, all_w.shape[1] // lax.axis_size("row"))
    for part in range(3):
        for ref, start in zip(w_refs, starts):
            all_w[part, pl.ds(start, ref.shape[1]), :] = ref[part]
    down = feed(jnp.concatenate([ref[...] for ref in x_refs], axis=0), all_w)
    count = x_refs[0].shape[0]
    for i, ref in enumerate(out_refs):
        ref[...] = down[i * count : (i + 1) * count].astype(ref.dtype)


def feed_first_call(blocks, pieces, out_types):
    n_x, n_w, (count, width) = len(blocks), len(pieces), blocks[0].shape
    places = [(mask, first) for _, mask, first in pieces]
    hidden = pieces[0][0].shape[2]
    return pl.pallas_call(
        functools.partial(feed_first_kernel, places, n_x, n_w),
        out_shape=[pltpu.VMEM((3, width, hidden), jnp.bfloat16)]
        + [jax.ShapeDtypeStruct((count, width), t) for t in out_types],
        in_specs=[VMEM] * (n_x + n_w),
        out_specs=[VMEM] * (n_x + 1),
        compiler_params=params(28),
        cost_estimate=LIGHT,
    )(*blocks, *(piece for piece, _, _ in pieces))


def feed_last_kernel(x_ref, all_w, near_ref, far_ref):
    down = feed(x_ref[...], all_w).astype(near_ref.dtype)
    near_ref[...] = down[: near_ref.shape[0]]
    far_ref[...] = down[near_ref.shape[0] :]


def feed_last_call(block, all_w, near):
    count, width = block.shape
    return pl.pallas_call(
        feed_last_kernel,
        out_shape=[
            jax.ShapeDtypeStruct((rows, width), jnp.bfloat16) for rows in (near, count - near)
        ],
        in_specs=[VMEM] * 2,
        out_specs=[VMEM] * 2,
        compiler_params=params(20),
        cost_estimate=LIGHT,
    )(block, all_w)


def sum_kernel(part_ref, passed_ref, out_ref):
    near = passed_ref.shape[0]
    both = part_ref[:near].astype(jnp.float32) + passed_ref[...].astype(jnp.float32)
    out_ref[:near] = both.astype(out_ref.dtype)
    out_ref[near:] = part_ref[near:]


def sum_call(part, passed):
    return pl.pallas_call(
        sum_kernel,
        out_shape=jax.ShapeDtypeStruct(part.shape, jnp.bfloat16),
        in_specs=[VMEM] * 2,
        out_specs=VMEM,
        compiler_params=params(12),
        cost_estimate=LIGHT,
    )(part, passed)


def last_kernel(residual_ref, own_ref, two_ref, one_ref, far_ref, out_ref):
    near = out_ref.shape[0] - far_ref.shape[0]
    total = own_ref[...] + one_ref[...].astype(jnp.float32) + two_ref[...].astype(jnp.float32)
    residual = residual_ref[...].astype(jnp.float32)
    far = total[near:] + far_ref[...].astype(jnp.float32)
    out_ref[:near] = (residual[:near] + total[:near]).astype(out_ref.dtype)
    out_ref[near:] = (residual[near:] + far).astype(out_ref.dtype)


def last_call(residual, own, two, one, far):
    return pl.pallas_call(
        last_kernel,
        out_shape=jax.ShapeDtypeStruct(residual.shape, jnp.bfloat16),
        in_specs=[VMEM] * 5,
        out_specs=VMEM,
        compiler_params=params(12),
        cost_estimate=LIGHT,
    )(residual, own, two, one, far)


def tuned(
    inputs,
    attention_norm_gain,
    query_key_value_weight,
    filter_taps,
    output_projection,
    window_key_value,
    cache_valid_length,
    lengths,
    token_adapter_index,
    adapter_down_map,
    adapter_up_map,
    feed_forward_gain,
    gate_projection,
    up_projection,
    down_projection,
):
    bf16, f32 = jnp.bfloat16, jnp.float32
    col = lax.axis_index("col")
    count, width = inputs.shape
    heads = window_key_value.shape[2]

    rank, kept = adapter_down_map.shape[2], adapter_down_map.shape[0]
    normed_attention, packed = entry_call(
        inputs,
        jnp.transpose(query_key_value_weight, (1, 0, 2)),
        output_projection,
        attention_norm_gain,
        jnp.transpose(adapter_down_map, (0, 2, 1)).reshape(kept * rank, width),
        adapter_up_map.reshape(kept * rank, width),
    )
    token_two, token_one = swap(normed_attention, "col", 2), swap(normed_attention, "col", 1)
    firsts = first_hops(packed)
    requests = window_key_value.shape[0]
    window = window_key_value.shape[3] // HD
    cache = window_key_value.reshape(requests, 2, heads, window, HD)
    cache = jnp.transpose(cache, (1, 2, 0, 3, 4)).reshape(2, heads, requests * window, HD)
    cache = jnp.pad(cache, ((0, 0), (0, 0), (0, 0), (0, LANES - HD)))
    own_ids = lax.dynamic_slice_in_dim(token_adapter_index, col * count, count, 0)
    feed_own = jnp.concatenate(
        [gate_projection[None], up_projection[None], jnp.transpose(down_projection)[None]], axis=0
    )
    firsts, cache, own_ids, feed_own = lax.optimization_barrier((firsts, cache, own_ids, feed_own))
    token_two, token_one, cache = lax.optimization_barrier((token_two, token_one, cache))
    token_three = swap(token_two, "col", 1)
    seconds = second_hops(packed, *firsts)
    token_three, diagonal, feed_own = lax.optimization_barrier((token_three, seconds[:2], feed_own))
    seconds = diagonal + seconds[2:]
    thirds = tuple(swap(piece, "row", 1) for piece in diagonal)
    feed_firsts = first_hops(feed_own)

    pieces = named_pieces(packed, firsts, seconds, thirds)
    blocks = [normed_attention, token_one, token_two, token_three]
    requests_here = (lengths, cache_valid_length, cache)
    ranks = kept * rank * lax.axis_size("row")
    x_all, w_all, out_w, down_maps, up_maps, part_three = first_call(
        blocks, pieces, ranks, filter_taps, *requests_here
    )
    passed = swap(part_three, "col", 1)
    q, k, v, part_two, part_one = rest_call(
        [2, 1], count, x_all, w_all, out_w, filter_taps, *requests_here
    )
    part_own = own_call(
        rank, q, k, v, out_w, normed_attention, own_ids, down_maps, up_maps, *requests_here
    )
    got_one = swap(part_one, "col", 1)
    got_two = swap((part_two.astype(f32) + passed.astype(f32)).astype(bf16), "col", 2)
    got_one, *hops = lax.optimization_barrier((got_one, *feed_firsts))
    feed_seconds = second_hops(feed_own, *hops)
    residual, normed_mlp = residual_call(inputs, part_own, got_two, got_one, feed_forward_gain)
    token_two, token_one = swap(normed_mlp, "col", 2), swap(normed_mlp, "col", 1)
    feed_thirds = tuple(swap(piece, "row", 1) for piece in feed_seconds[:2])
    token_two, token_one = lax.optimization_barrier((token_two, token_one))
    token_three = swap(token_two, "col", 1)
    feed_pieces = named_pieces(feed_own, feed_firsts, feed_seconds, feed_thirds)
    feed_w, part_two, part_one, part_own = feed_first_call(
        [token_two, token_one, normed_mlp], feed_pieces, [bf16, bf16, f32]
    )
    near, far = feed_last_call(token_three, feed_w, count * 5 // 8)
    passed, got_far = swap(near, "col", 1), swap(far, "col", 3)
    part_two = sum_call(part_two, passed)
    got_two = swap(part_two, "col", 2)
    _, got_far, part_one = lax.optimization_barrier((part_two, got_far, part_one))
    got_one = swap(part_one, "col", 1)
    return last_call(residual, part_own, got_two, got_one, got_far)


def on_device(*args):
    rows, cols = lax.axis_size("row"), lax.axis_size("col")
    if (rows, cols) == (8, 4):
        return tuned(*args)
    return plain(*args)


def solution(mesh):
    placed = (
        P(("row", "col"), None),
        P(),
        P("row", None, "col"),
        P(None, None, "col"),
        P("col", "row"),
        P("row", None, "col", None),
        P("row"),
        P("row", None),
        P("row", None),
        P("row", None, None),
        P("row", None, None),
        P(),
        P("row", "col"),
        P("row", "col"),
        P("col", "row"),
    )
    return jax.shard_map(
        on_device, mesh=mesh, in_specs=placed, out_specs=P(("row", "col"), None), check_vma=False
    )
```

```python
import functools

import jax
import jax.numpy as jnp
from jax import lax
from jax.experimental import pallas as pl
from jax.experimental.pallas import tpu as pltpu
from jax.sharding import PartitionSpec as P

HD = 112


epsilon = 1e-05


def rms_scaled(values, gain_row):
    mean_square = jnp.mean(values * values, axis=-1, keepdims=True)
    return values * lax.rsqrt(mean_square + epsilon) * gain_row


def layout(lengths_row, tok_count):
    finish = jnp.cumsum(lengths_row)
    begins = finish - lengths_row
    places = jnp.arange(tok_count, dtype=jnp.int32)
    segment = jnp.sum((places[:, None] >= finish[None, :]).astype(jnp.int32), axis=1)
    member = segment[:, None] == jnp.arange(lengths_row.shape[0], dtype=jnp.int32)[None, :]
    inside = places - jnp.sum(jnp.where(member, begins[None, :], 0), axis=1)
    return (segment, inside)


def shifted(values, offset, inside):
    moved_rows = jnp.pad(values[: values.shape[0] - offset], ((offset, 0), (0, 0)))
    return jnp.where((inside >= offset)[:, None], moved_rows, jnp.zeros_like(moved_rows))


def convolve(values, taps, inside):
    running = jnp.zeros_like(values)
    for offset in range(taps.shape[0]):
        running = running + taps[offset][None, :] * shifted(values, offset, inside)
    return running


def make_qkv(qkv_mixed, filter_taps, inside):
    queries = qkv_mixed[:, 0].astype(jnp.bfloat16)
    keys_used = convolve(qkv_mixed[:, 1], filter_taps[:, 0], inside).astype(jnp.bfloat16)
    raw_values = qkv_mixed[:, 2]
    gates = jax.nn.sigmoid(convolve(raw_values, filter_taps[:, 1], inside))
    values_used = (raw_values * gates).astype(jnp.bfloat16)
    return (queries, keys_used, values_used)


def split_cache(window_key_value, head_size):
    requests_here, head_count = (window_key_value.shape[0], window_key_value.shape[2])
    window = window_key_value.shape[3] // head_size
    split_kv = window_key_value.reshape(requests_here, 2, head_count, window, head_size)
    cached_key_rows = jnp.transpose(split_kv[:, 0], (0, 2, 1, 3)).reshape(
        requests_here * window, head_count, head_size
    )
    cached_value_rows = jnp.transpose(split_kv[:, 1], (0, 2, 1, 3)).reshape(
        requests_here * window, head_count, head_size
    )
    return (cached_key_rows, cached_value_rows, window)


def attend(
    queries,
    keys_used,
    values_used,
    window_key_value,
    segment,
    inside,
    cache_valid_length,
    head_size,
):
    tok_count = queries.shape[0]
    head_count = queries.shape[1] // head_size
    requests_here = window_key_value.shape[0]
    cached_key_rows, cached_value_rows, window = split_cache(window_key_value, head_size)
    query_per_head = queries.reshape(tok_count, head_count, head_size)
    key_h = keys_used.reshape(tok_count, head_count, head_size)
    value_per_head = values_used.reshape(tok_count, head_count, head_size)
    attention_score_scale = head_size ** (-0.5)
    places = jnp.arange(tok_count, dtype=jnp.int32)
    local_mask = (
        (segment[:, None] == segment[None, :])
        & (places[None, :] <= places[:, None])
        & (places[None, :] > places[:, None] - window)
    )
    slot_ids = jnp.arange(requests_here * window, dtype=jnp.int32)
    owner_req = slot_ids // window
    within = slot_ids % window
    slot_ages = jnp.repeat(cache_valid_length, window)
    cache_mask = (
        (segment[:, None] == owner_req[None, :])
        & (within[None, :] >= window - slot_ages[None, :])
        & (within[None, :] > inside[:, None])
    )
    local_scores = (
        jnp.einsum("thd,jhd->htj", query_per_head, key_h, preferred_element_type=jnp.float32)
        * attention_score_scale
    )
    cached_score_rows = (
        jnp.einsum(
            "sek,yek->esy", query_per_head, cached_key_rows, preferred_element_type=jnp.float32
        )
        * attention_score_scale
    )
    local_scores = jnp.where(local_mask[None], local_scores, -jnp.inf)
    cached_score_rows = jnp.where(cache_mask[None], cached_score_rows, -jnp.inf)
    row_max = jnp.maximum(
        jnp.max(local_scores, axis=-1, keepdims=True),
        jnp.max(cached_score_rows, axis=-1, keepdims=True),
    )
    local_exp = jnp.exp(local_scores - row_max)
    cache_exp = jnp.exp(cached_score_rows - row_max)
    denominator = jnp.sum(local_exp, axis=-1, keepdims=True) + jnp.sum(
        cache_exp, axis=-1, keepdims=True
    )
    window_attention_weight = (local_exp / denominator).astype(jnp.bfloat16)
    cached_attention_weight = (cache_exp / denominator).astype(jnp.bfloat16)
    joined_output = jnp.einsum(
        "zkc,czu->kzu", window_attention_weight, value_per_head, preferred_element_type=jnp.float32
    )
    joined_output = joined_output + jnp.einsum(
        "lar,rlx->alx",
        cached_attention_weight,
        cached_value_rows,
        preferred_element_type=jnp.float32,
    )
    return joined_output.reshape(tok_count, head_count * head_size).astype(jnp.bfloat16)


def plain(
    inputs,
    attention_norm_gain,
    query_key_value_weight,
    filter_taps,
    output_projection,
    window_key_value,
    cache_valid_length,
    lengths,
    token_adapter_index,
    adapter_down_map,
    adapter_up_map,
    feed_forward_gain,
    gate_projection,
    up_projection,
    down_projection,
):
    own_count = inputs.shape[0]
    column = lax.axis_index("col")
    row_count = lax.axis_size("row")
    gathered = lax.all_gather(inputs, "col", axis=0, tiled=True)
    tok_count = gathered.shape[0]
    normalized_input = rms_scaled(gathered.astype(jnp.float32), attention_norm_gain).astype(
        jnp.bfloat16
    )
    qkv_mixed = jnp.einsum(
        "td,dka->tka",
        normalized_input,
        lax.all_gather(query_key_value_weight, "row", axis=0, tiled=True),
        preferred_element_type=jnp.float32,
    )
    segment, inside = layout(lengths[0], tok_count)
    queries, keys_used, values_used = make_qkv(qkv_mixed, filter_taps, inside)
    attended = attend(
        queries, keys_used, values_used, window_key_value, segment, inside, cache_valid_length, HD
    )
    kept_count = adapter_down_map.shape[0]
    every_adapter = kept_count * row_count
    capacity = max(2, 2 * own_count // every_adapter)
    first_row = column * own_count
    own_rows = lax.dynamic_slice_in_dim(normalized_input, first_row, own_count, 0)
    own_ids = lax.dynamic_slice_in_dim(token_adapter_index[:, 0], first_row, own_count, 0)
    member = (own_ids[:, None] == jnp.arange(every_adapter, dtype=jnp.int32)[None, :]).astype(
        jnp.int32
    )
    before = jnp.cumsum(member, axis=0) - member
    slot_rank = jnp.sum(before * member, axis=1)
    target = own_ids * capacity + slot_rank
    placer = (
        target[None, :] == jnp.arange(every_adapter * capacity, dtype=jnp.int32)[:, None]
    ).astype(jnp.bfloat16)
    outgoing = jnp.dot(placer, own_rows, preferred_element_type=jnp.float32).astype(jnp.bfloat16)
    outgoing = outgoing.reshape(row_count, kept_count, capacity, normalized_input.shape[1])
    reduced_rank_input = jnp.einsum(
        "sakd,adr->sakr",
        lax.all_to_all(outgoing, "row", split_axis=0, concat_axis=0, tiled=True),
        adapter_down_map,
        preferred_element_type=jnp.float32,
    ).astype(jnp.bfloat16)
    answered = jnp.einsum(
        "zjbf,jfm->zjbm", reduced_rank_input, adapter_up_map, preferred_element_type=jnp.float32
    ).astype(jnp.bfloat16)
    returned = lax.all_to_all(answered, "row", split_axis=0, concat_axis=0, tiled=True).reshape(
        every_adapter * capacity, normalized_input.shape[1]
    )
    delta_rows = jnp.dot(jnp.transpose(placer), returned, preferred_element_type=jnp.float32)
    out_term = jnp.dot(
        attended,
        lax.all_gather(output_projection, "row", axis=1, tiled=True),
        preferred_element_type=jnp.float32,
    )
    own_term = lax.dynamic_slice_in_dim(out_term, first_row, own_count, 0) + delta_rows
    out_term = lax.dynamic_update_slice_in_dim(out_term, own_term, first_row, 0)
    attn_share = lax.psum_scatter(
        out_term.astype(jnp.bfloat16), "col", scatter_dimension=0, tiled=True
    ).astype(jnp.float32)
    residual = (inputs.astype(jnp.float32) + attn_share).astype(jnp.bfloat16)
    whole_mixed = lax.all_gather(residual, "col", axis=0, tiled=True)
    normed_mlp = rms_scaled(whole_mixed.astype(jnp.float32), feed_forward_gain).astype(jnp.bfloat16)

    def add_rows(piece):
        return jnp.dot(normed_mlp, piece, preferred_element_type=jnp.float32)

    gate = add_rows(lax.all_gather(gate_projection, "row", axis=0, tiled=True))
    up_part = add_rows(lax.all_gather(up_projection, "row", axis=0, tiled=True))
    hidden = (jax.nn.silu(gate) * up_part).astype(jnp.bfloat16)
    down_term = jnp.dot(
        hidden,
        lax.all_gather(down_projection, "row", axis=1, tiled=True),
        preferred_element_type=jnp.float32,
    )
    mlp_added = lax.psum_scatter(
        down_term.astype(jnp.bfloat16), "col", scatter_dimension=0, tiled=True
    ).astype(jnp.float32)
    return (residual.astype(jnp.float32) + mlp_added).astype(jnp.bfloat16)


LANES = 128
MIB = 1 << 20


LIGHT = pl.CostEstimate(flops=1, bytes_accessed=1, transcendentals=0)


def params(mib):
    return pltpu.CompilerParams(vmem_limit_bytes=mib * MIB)


HBM = pl.BlockSpec(memory_space=pl.ANY)
VMEM = pl.BlockSpec(memory_space=pltpu.VMEM)
SMEM = pl.BlockSpec(memory_space=pltpu.SMEM)
NT = (((1,), (1,)), ((), ()))


def normed(values, gain):
    mean_square = jnp.mean(values * values, axis=-1, keepdims=True)
    return (values * lax.rsqrt(mean_square + epsilon) * gain).astype(jnp.bfloat16)


def entry_kernel(*refs):
    sources, (normed_ref, packed_ref) = refs[:6], refs[6:8]
    targets, sems = refs[8:14], refs[14]
    loads = [
        pltpu.make_async_copy(source, target, sems.at[i])
        for i, (source, target) in enumerate(zip(sources, targets))
    ]
    for load in loads:
        load.start()
    x_ref, qkv_ref, out_ref, gain_ref, down_ref, up_ref = targets
    rows, part, ranks = qkv_ref.shape[1], qkv_ref.shape[2], down_ref.shape[0]
    loads[0].wait()
    loads[3].wait()
    normed_ref[...] = normed(x_ref[...].astype(jnp.float32), gain_ref[...][None, :])
    for at in (1, 2, 4, 5):
        loads[at].wait()
    for place, which in enumerate((1, 0, 2)):
        packed_ref[:rows, place * part : (place + 1) * part] = qkv_ref[which]
    out_rows = jnp.transpose(out_ref[...].astype(jnp.float32)).astype(jnp.bfloat16)
    packed_ref[:rows, 3 * part :] = out_rows
    packed_ref[rows : rows + ranks, :] = down_ref[...]
    packed_ref[rows + ranks :, :] = up_ref[...]


def entry_call(rows, qkv, out, gain, down, up):
    sources = (rows, qkv, out, gain, down, up)
    return pl.pallas_call(
        entry_kernel,
        out_shape=[
            jax.ShapeDtypeStruct(rows.shape, jnp.bfloat16),
            jax.ShapeDtypeStruct((qkv.shape[1] + 2 * down.shape[0], 4 * qkv.shape[2]), jnp.bfloat16),
        ],
        in_specs=[HBM] * len(sources),
        out_specs=[VMEM] * 2,
        scratch_shapes=[pltpu.VMEM(source.shape, source.dtype) for source in sources]
        + [pltpu.SemaphoreType.DMA((len(sources),))],
        compiler_params=params(60),
        cost_estimate=LIGHT,
    )(*sources)


def residual_kernel(x_ref, own_ref, two_ref, one_ref, gain_ref, residual_ref, normed_ref):
    total = own_ref[...] + one_ref[...].astype(jnp.float32) + two_ref[...].astype(jnp.float32)
    residual = (x_ref[...].astype(jnp.float32) + total).astype(jnp.bfloat16)
    residual_ref[...] = residual
    normed_ref[...] = normed(residual.astype(jnp.float32), gain_ref[...])


def residual_call(rows, own, two, one, gain):
    block = jax.ShapeDtypeStruct(rows.shape, jnp.bfloat16)
    return pl.pallas_call(
        residual_kernel,
        out_shape=[block, block],
        in_specs=[VMEM] * 5,
        out_specs=[VMEM] * 2,
        compiler_params=params(12),
        cost_estimate=LIGHT,
    )(rows, own, two, one, gain[None, :])


def adapter_term(x_ref, ids_ref, down_ref, up_ref, rank):
    low = lax.dot_general(x_ref[...], down_ref[...], NT, preferred_element_type=jnp.float32)
    adapter = lax.broadcasted_iota(jnp.int32, low.shape, 1) // rank
    low = jnp.where(ids_ref[...] == adapter, low, 0.0).astype(jnp.bfloat16)
    return jnp.dot(low, up_ref[...], preferred_element_type=jnp.float32).astype(jnp.bfloat16)


def xor_pairs(count, mask):
    return [(i, i ^ mask) for i in range(count)]


def swap(value, axis, mask):
    return lax.ppermute(value, axis, xor_pairs(lax.axis_size(axis), mask))


def first_hops(own):
    return swap(own, "row", 2), swap(own, "row", 4)


def second_hops(own, from_x, from_y):
    half = own.shape[-2] // 2
    diagonal = swap(from_x[..., :half, :], "row", 4), swap(from_y[..., half:, :], "row", 2)
    return diagonal + tuple(swap(piece, "row", 1) for piece in (own, from_x, from_y))


def named_pieces(own, firsts, seconds, thirds):
    half = own.shape[-2] // 2
    masks = [(0, 0), (2, 0), (4, 0), (6, 0), (6, half), (1, 0), (3, 0), (5, 0), (7, 0), (7, half)]
    return [(piece, *at) for piece, at in zip((own,) + firsts + seconds + thirds, masks)]


def shard_starts(places, shard):
    row = lax.axis_index("row")
    return [pl.multiple_of((row ^ mask) * shard + first, 16) for mask, first in places]


def request_columns(lengths_ref, begin, count):
    place = begin + lax.broadcasted_iota(jnp.int32, (count, 1), 0)
    segment, first = jnp.zeros_like(place), jnp.zeros_like(place)
    finish = jnp.int32(0)
    for s in range(lengths_ref.shape[1]):
        finish = finish + lengths_ref[0, s]
        later = place >= finish
        segment = segment + later.astype(jnp.int32)
        first = jnp.where(later, finish, first)
    return place, segment, first


def attend_block(mask, count, base, lengths_ref, valid_ref, q_ref, k_ref, v_ref, cache_ref):
    col = lax.axis_index("col")
    _, heads, slots, lanes = cache_ref.shape
    requests = valid_ref.shape[0]
    window = slots // requests
    scale = HD ** (-0.5)
    begin = pl.multiple_of((col ^ mask) * count, count)
    key_begin = pl.multiple_of(jnp.maximum(begin - window, 0), window)
    key_count = count + window
    place, segment, first = request_columns(lengths_ref, begin, count)
    first_key = jnp.maximum(first, place - window + 1)
    keys = key_begin + lax.broadcasted_iota(jnp.int32, (count, key_count), 1)
    local_mask = (keys >= first_key) & (keys <= place)
    slot = lax.broadcasted_iota(jnp.int32, (1, slots), 1)
    owner, within = slot // window, slot % window
    oldest = jnp.full_like(slot, window)
    for s in range(requests):
        oldest = jnp.where(owner == s, window - valid_ref[s], oldest)
    within = jnp.where(within >= oldest, within, -1)
    cache_mask = (owner == segment) & (within > place - first)
    outs = []
    own_rows = pl.ds(pl.multiple_of(begin - base, count), count)
    key_rows = pl.ds(pl.multiple_of(key_begin - base, window), key_count)
    for h in range(heads):
        cols = slice(h * lanes, (h + 1) * lanes)
        q, k, v = q_ref[own_rows, cols], k_ref[key_rows, cols], v_ref[key_rows, cols]
        local = lax.dot_general(q, k, NT, preferred_element_type=jnp.float32)
        cached = lax.dot_general(q, cache_ref[0, h], NT, preferred_element_type=jnp.float32)
        local = jnp.where(local_mask, local * scale, -jnp.inf)
        cached = jnp.where(cache_mask, cached * scale, -jnp.inf)
        top = jnp.maximum(
            jnp.max(local, axis=-1, keepdims=True), jnp.max(cached, axis=-1, keepdims=True)
        )
        local = jnp.exp(local - top)
        cached = jnp.exp(cached - top)
        total = jnp.sum(local, axis=-1, keepdims=True) + jnp.sum(cached, axis=-1, keepdims=True)
        summed = jnp.dot(local.astype(jnp.bfloat16), v, preferred_element_type=jnp.float32)
        summed = summed + jnp.dot(
            cached.astype(jnp.bfloat16), cache_ref[1, h], preferred_element_type=jnp.float32
        )
        outs.append((summed / total).astype(jnp.bfloat16)[:, :HD])
    blank = jnp.zeros((count, heads * (lanes - HD)), jnp.bfloat16)
    return jnp.concatenate([blank] + outs, axis=1)


def mix_rows(x, base, w_ref, taps_ref, lengths_ref, q_ref, k_ref, v_ref, padded):
    rows, part = x.shape[0], taps_ref.shape[2]
    padded[0:8, :] = jnp.zeros((8, part), jnp.float32)
    place, _, first = request_columns(lengths_ref, base, rows)
    inside = place - first
    mixed = jnp.dot(x, w_ref[...], preferred_element_type=jnp.float32)

    def convolved(raw, which):
        padded[8:, :] = raw
        running = taps_ref[0, which : which + 1, :] * raw
        for offset in range(1, taps_ref.shape[0]):
            moved = padded[8 - offset : 8 - offset + rows, :]
            tap = taps_ref[offset, which : which + 1, :]
            running = running + jnp.where(inside >= offset, tap * moved, 0.0)
        return running

    def store_heads(ref, value):
        blank = jnp.zeros((rows, LANES - HD), jnp.bfloat16)
        for h in range(part // HD):
            ref[:, h * LANES : h * LANES + HD] = value[:, h * HD : (h + 1) * HD].astype(jnp.bfloat16)
            ref[:, h * LANES + HD : (h + 1) * LANES] = blank

    store_heads(k_ref, convolved(mixed[:, :part], 0))
    store_heads(q_ref, mixed[:, part : 2 * part])
    raw_values = mixed[:, 2 * part : 3 * part]
    store_heads(v_ref, raw_values * jax.nn.sigmoid(convolved(raw_values, 1)))


def first_kernel(places, n_x, n_w, *refs):
    x_refs, w_refs = refs[:n_x], refs[n_x : n_x + n_w]
    taps_ref, lengths_ref, valid_ref, cache_ref = refs[n_x + n_w : n_x + n_w + 4]
    x_all, w_all, out_w, down_ref, up_ref, part_ref, q_ref, k_ref, v_ref, padded = refs[n_x + n_w + 4 :]
    col = lax.axis_index("col")
    count, width = x_refs[0].shape
    lanes, mixed_lanes = out_w.shape[1], w_all.shape[1]
    for i, ref in enumerate(x_refs):
        x_all[pl.ds(pl.multiple_of((col ^ i) * count, 16), count), :] = ref[...]
    shard = width // lax.axis_size("row")
    ranks = down_ref.shape[0] // lax.axis_size("row")
    starts = shard_starts(places, shard)
    for ref, start, (mask, first) in zip(w_refs, starts, places):
        rows = min(ref.shape[0], shard - first)
        w_all[pl.ds(start, rows), :] = ref[:rows, :mixed_lanes]
        out_w[pl.ds(start, rows), :] = ref[:rows, ref.shape[1] - lanes :]
        if rows < ref.shape[0]:
            at = pl.multiple_of((lax.axis_index("row") ^ mask) * ranks, 16)
            down_ref[pl.ds(at, ranks), :] = ref[rows : rows + ranks, :]
            up_ref[pl.ds(at, ranks), :] = ref[rows + ranks :, :]
    base = pl.multiple_of(jnp.maximum((col ^ (n_x - 1)) * count - count, 0), count)
    x = x_all[pl.ds(base, 2 * count), :]
    mix_rows(x, base, w_all, taps_ref, lengths_ref, q_ref, k_ref, v_ref, padded)
    attended = attend_block(
        n_x - 1, count, base, lengths_ref, valid_ref, q_ref, k_ref, v_ref, cache_ref
    )
    part_ref[...] = lax.dot_general(
        attended, out_w[...], NT, preferred_element_type=jnp.float32
    ).astype(jnp.bfloat16)


def first_call(blocks, pieces, ranks, taps, lengths, valid, cache):
    (count, width), n_x, n_w = blocks[0].shape, len(blocks), len(pieces)
    tokens, part = count * n_x, taps.shape[2]
    lanes = part // HD * LANES
    mixed_lanes = -(-3 * part // LANES) * LANES
    places = [(mask, first) for _, mask, first in pieces]
    shapes = [(tokens, width), (width, mixed_lanes), (width, lanes), (ranks, width), (ranks, width), (count, width)]
    return pl.pallas_call(
        functools.partial(first_kernel, places, n_x, n_w),
        out_shape=[pltpu.VMEM(shape, jnp.bfloat16) for shape in shapes[:3]]
        + [jax.ShapeDtypeStruct(shape, jnp.bfloat16) for shape in shapes[3:]],
        in_specs=[VMEM] * (n_x + n_w + 1) + [SMEM, SMEM, VMEM],
        out_specs=[VMEM] * len(shapes),
        scratch_shapes=[pltpu.VMEM((2 * count, lanes), jnp.bfloat16)] * 3
        + [pltpu.VMEM((2 * count + 8, part), jnp.float32)],
        compiler_params=params(28),
        cost_estimate=LIGHT,
    )(*blocks, *(piece for piece, _, _ in pieces), taps, lengths, valid, cache)


def rest_kernel(masks, x_all, w_all, out_w, taps_ref, lengths_ref, valid_ref, cache_ref, *refs):
    q_ref, k_ref, v_ref = refs[:3]
    out_refs, padded = refs[3:-1], refs[-1]
    mix_rows(x_all[...], 0, w_all, taps_ref, lengths_ref, q_ref, k_ref, v_ref, padded)
    for mask, out_ref in zip(masks, out_refs):
        attended = attend_block(
            mask, out_ref.shape[0], 0, lengths_ref, valid_ref, q_ref, k_ref, v_ref, cache_ref
        )
        out_ref[...] = lax.dot_general(
            attended, out_w[...], NT, preferred_element_type=jnp.float32
        ).astype(out_ref.dtype)


def rest_call(masks, count, x_all, w_all, out_w, taps, lengths, valid, cache):
    (tokens, width), lanes = x_all.shape, out_w.shape[1]
    shapes = [(tokens, lanes)] * 3 + [(count, width)] * len(masks)
    return pl.pallas_call(
        functools.partial(rest_kernel, masks),
        out_shape=[jax.ShapeDtypeStruct(shape, jnp.bfloat16) for shape in shapes],
        in_specs=[VMEM] * 4 + [SMEM, SMEM, VMEM],
        out_specs=[VMEM] * len(shapes),
        scratch_shapes=[pltpu.VMEM((tokens + 8, taps.shape[2]), jnp.float32)],
        compiler_params=params(32),
        cost_estimate=LIGHT,
    )(x_all, w_all, out_w, taps, lengths, valid, cache)


def own_kernel(rank, q_ref, k_ref, v_ref, out_w, x_ref, ids_ref, down_ref, up_ref, *refs):
    lengths_ref, valid_ref, cache_ref, out_ref = refs
    attended = attend_block(
        0, out_ref.shape[0], 0, lengths_ref, valid_ref, q_ref, k_ref, v_ref, cache_ref
    )
    part = lax.dot_general(attended, out_w[...], NT, preferred_element_type=jnp.float32)
    out_ref[...] = part + adapter_term(x_ref, ids_ref, down_ref, up_ref, rank).astype(jnp.float32)


def own_call(rank, q, k, v, out_w, x, ids, down, up, lengths, valid, cache):
    return pl.pallas_call(
        functools.partial(own_kernel, rank),
        out_shape=jax.ShapeDtypeStruct(x.shape, jnp.float32),
        in_specs=[VMEM] * 8 + [SMEM, SMEM, VMEM],
        out_specs=VMEM,
        compiler_params=params(20),
        cost_estimate=LIGHT,
    )(q, k, v, out_w, x, ids, down, up, lengths, valid, cache)


def feed(x, all_w):
    gate = jnp.dot(x, all_w[0], preferred_element_type=jnp.float32)
    up = jnp.dot(x, all_w[1], preferred_element_type=jnp.float32)
    act = (jax.nn.silu(gate) * up).astype(jnp.bfloat16)
    return lax.dot_general(act, all_w[2], NT, preferred_element_type=jnp.float32)


def feed_first_kernel(places, n_x, n_w, *refs):
    x_refs, w_refs = refs[:n_x], refs[n_x : n_x + n_w]
    all_w, out_refs = refs[n_x + n_w], refs[n_x + n_w + 1 :]
    starts = shard_starts(places, all_w.shape[1] // lax.axis_size("row"))
    for part in range(3):
        for ref, start in zip(w_refs, starts):
            all_w[part, pl.ds(start, ref.shape[1]), :] = ref[part]
    down = feed(jnp.concatenate([ref[...] for ref in x_refs], axis=0), all_w)
    count = x_refs[0].shape[0]
    for i, ref in enumerate(out_refs):
        ref[...] = down[i * count : (i + 1) * count].astype(ref.dtype)


def feed_first_call(blocks, pieces, out_types):
    n_x, n_w, (count, width) = len(blocks), len(pieces), blocks[0].shape
    places = [(mask, first) for _, mask, first in pieces]
    hidden = pieces[0][0].shape[2]
    return pl.pallas_call(
        functools.partial(feed_first_kernel, places, n_x, n_w),
        out_shape=[pltpu.VMEM((3, width, hidden), jnp.bfloat16)]
        + [jax.ShapeDtypeStruct((count, width), t) for t in out_types],
        in_specs=[VMEM] * (n_x + n_w),
        out_specs=[VMEM] * (n_x + 1),
        compiler_params=params(28),
        cost_estimate=LIGHT,
    )(*blocks, *(piece for piece, _, _ in pieces))


def feed_last_kernel(x_ref, all_w, out_ref):
    out_ref[...] = feed(x_ref[...], all_w).astype(out_ref.dtype)


def feed_last_call(rows, all_w):
    return pl.pallas_call(
        feed_last_kernel,
        out_shape=jax.ShapeDtypeStruct(rows.shape, jnp.bfloat16),
        in_specs=[VMEM] * 2,
        out_specs=VMEM,
        compiler_params=params(20),
        cost_estimate=LIGHT,
    )(rows, all_w)


def sum_kernel(part_ref, near_ref, far_ref, out_ref):
    passed = jnp.concatenate([near_ref[...], far_ref[...]], axis=0).astype(jnp.float32)
    out_ref[...] = (part_ref[...].astype(jnp.float32) + passed).astype(out_ref.dtype)


def sum_call(part, near, far):
    return pl.pallas_call(
        sum_kernel,
        out_shape=jax.ShapeDtypeStruct(part.shape, jnp.bfloat16),
        in_specs=[VMEM] * 3,
        out_specs=VMEM,
        compiler_params=params(12),
        cost_estimate=LIGHT,
    )(part, near, far)


def last_kernel(residual_ref, own_ref, two_ref, one_ref, out_ref):
    total = own_ref[...] + one_ref[...].astype(jnp.float32) + two_ref[...].astype(jnp.float32)
    out_ref[...] = (residual_ref[...].astype(jnp.float32) + total).astype(out_ref.dtype)


def last_call(residual, own, two, one):
    return pl.pallas_call(
        last_kernel,
        out_shape=jax.ShapeDtypeStruct(residual.shape, jnp.bfloat16),
        in_specs=[VMEM] * 4,
        out_specs=VMEM,
        compiler_params=params(12),
        cost_estimate=LIGHT,
    )(residual, own, two, one)


def tuned(
    inputs,
    attention_norm_gain,
    query_key_value_weight,
    filter_taps,
    output_projection,
    window_key_value,
    cache_valid_length,
    lengths,
    token_adapter_index,
    adapter_down_map,
    adapter_up_map,
    feed_forward_gain,
    gate_projection,
    up_projection,
    down_projection,
):
    bf16, f32 = jnp.bfloat16, jnp.float32
    col = lax.axis_index("col")
    count, width = inputs.shape
    heads = window_key_value.shape[2]

    rank, kept = adapter_down_map.shape[2], adapter_down_map.shape[0]
    normed_attention, packed = entry_call(
        inputs,
        jnp.transpose(query_key_value_weight, (1, 0, 2)),
        output_projection,
        attention_norm_gain,
        jnp.transpose(adapter_down_map, (0, 2, 1)).reshape(kept * rank, width),
        adapter_up_map.reshape(kept * rank, width),
    )
    token_two, token_one = swap(normed_attention, "col", 2), swap(normed_attention, "col", 1)
    firsts = first_hops(packed)
    requests = window_key_value.shape[0]
    window = window_key_value.shape[3] // HD
    cache = window_key_value.reshape(requests, 2, heads, window, HD)
    cache = jnp.transpose(cache, (1, 2, 0, 3, 4)).reshape(2, heads, requests * window, HD)
    cache = jnp.pad(cache, ((0, 0), (0, 0), (0, 0), (0, LANES - HD)))
    own_ids = lax.dynamic_slice_in_dim(token_adapter_index, col * count, count, 0)
    feed_own = jnp.concatenate(
        [gate_projection[None], up_projection[None], jnp.transpose(down_projection)[None]], axis=0
    )
    firsts, cache, own_ids, feed_own = lax.optimization_barrier((firsts, cache, own_ids, feed_own))
    token_two, token_one, cache = lax.optimization_barrier((token_two, token_one, cache))
    token_three = swap(token_two, "col", 1)
    seconds = second_hops(packed, *firsts)
    token_three, diagonal, feed_own = lax.optimization_barrier((token_three, seconds[:2], feed_own))
    seconds = diagonal + seconds[2:]
    thirds = tuple(swap(piece, "row", 1) for piece in diagonal)
    feed_firsts = first_hops(feed_own)

    pieces = named_pieces(packed, firsts, seconds, thirds)
    blocks = [normed_attention, token_one, token_two, token_three]
    requests_here = (lengths, cache_valid_length, cache)
    ranks = kept * rank * lax.axis_size("row")
    x_all, w_all, out_w, down_maps, up_maps, part_three = first_call(
        blocks, pieces, ranks, filter_taps, *requests_here
    )
    passed = swap(part_three, "col", 1)
    q, k, v, part_two, part_one = rest_call(
        [2, 1], count, x_all, w_all, out_w, filter_taps, *requests_here
    )
    part_own = own_call(
        rank, q, k, v, out_w, normed_attention, own_ids, down_maps, up_maps, *requests_here
    )
    got_one = swap(part_one, "col", 1)
    got_two = swap((part_two.astype(f32) + passed.astype(f32)).astype(bf16), "col", 2)
    got_one, *hops = lax.optimization_barrier((got_one, *feed_firsts))
    feed_seconds = second_hops(feed_own, *hops)
    residual, normed_mlp = residual_call(inputs, part_own, got_two, got_one, feed_forward_gain)
    token_two, token_one = swap(normed_mlp, "col", 2), swap(normed_mlp, "col", 1)
    feed_thirds = tuple(swap(piece, "row", 1) for piece in feed_seconds[:2])
    token_two, token_one = lax.optimization_barrier((token_two, token_one))
    split = count * 5 // 8
    three = [swap(rows, "col", 1) for rows in (token_two[:split], token_two[split:])]
    feed_pieces = named_pieces(feed_own, feed_firsts, feed_seconds, feed_thirds)
    feed_w, part_two, part_one, part_own = feed_first_call(
        [token_two, token_one, normed_mlp], feed_pieces, [bf16, bf16, f32]
    )
    near, far = (feed_last_call(rows, feed_w) for rows in three)
    part_two = sum_call(part_two, swap(near, "col", 1), swap(far, "col", 1))
    part_two, part_one = lax.optimization_barrier((part_two, part_one))
    got_two, got_one = swap(part_two, "col", 2), swap(part_one, "col", 1)
    return last_call(residual, part_own, got_two, got_one)


def on_device(*args):
    rows, cols = lax.axis_size("row"), lax.axis_size("col")
    if (rows, cols) == (8, 4):
        return tuned(*args)
    return plain(*args)


def solution(mesh):
    placed = (
        P(("row", "col"), None),
        P(),
        P("row", None, "col"),
        P(None, None, "col"),
        P("col", "row"),
        P("row", None, "col", None),
        P("row"),
        P("row", None),
        P("row", None),
        P("row", None, None),
        P("row", None, None),
        P(),
        P("row", "col"),
        P("row", "col"),
        P("col", "row"),
    )
    return jax.shard_map(
        on_device, mesh=mesh, in_specs=placed, out_specs=P(("row", "col"), None), check_vma=False
    )
```

```python
import functools

import jax
import jax.numpy as jnp
from jax import lax
from jax.experimental import pallas as pl
from jax.experimental.pallas import tpu as pltpu
from jax.sharding import PartitionSpec as P

HD = 112


epsilon = 1e-05


def rms_scaled(values, gain_row):
    mean_square = jnp.mean(values * values, axis=-1, keepdims=True)
    return values * lax.rsqrt(mean_square + epsilon) * gain_row


def layout(lengths_row, tok_count):
    finish = jnp.cumsum(lengths_row)
    begins = finish - lengths_row
    places = jnp.arange(tok_count, dtype=jnp.int32)
    segment = jnp.sum((places[:, None] >= finish[None, :]).astype(jnp.int32), axis=1)
    member = segment[:, None] == jnp.arange(lengths_row.shape[0], dtype=jnp.int32)[None, :]
    inside = places - jnp.sum(jnp.where(member, begins[None, :], 0), axis=1)
    return (segment, inside)


def shifted(values, offset, inside):
    moved_rows = jnp.pad(values[: values.shape[0] - offset], ((offset, 0), (0, 0)))
    return jnp.where((inside >= offset)[:, None], moved_rows, jnp.zeros_like(moved_rows))


def convolve(values, taps, inside):
    running = jnp.zeros_like(values)
    for offset in range(taps.shape[0]):
        running = running + taps[offset][None, :] * shifted(values, offset, inside)
    return running


def make_qkv(qkv_mixed, filter_taps, inside):
    queries = qkv_mixed[:, 0].astype(jnp.bfloat16)
    keys_used = convolve(qkv_mixed[:, 1], filter_taps[:, 0], inside).astype(jnp.bfloat16)
    raw_values = qkv_mixed[:, 2]
    gates = jax.nn.sigmoid(convolve(raw_values, filter_taps[:, 1], inside))
    values_used = (raw_values * gates).astype(jnp.bfloat16)
    return (queries, keys_used, values_used)


def split_cache(window_key_value, head_size):
    requests_here, head_count = (window_key_value.shape[0], window_key_value.shape[2])
    window = window_key_value.shape[3] // head_size
    split_kv = window_key_value.reshape(requests_here, 2, head_count, window, head_size)
    cached_key_rows = jnp.transpose(split_kv[:, 0], (0, 2, 1, 3)).reshape(
        requests_here * window, head_count, head_size
    )
    cached_value_rows = jnp.transpose(split_kv[:, 1], (0, 2, 1, 3)).reshape(
        requests_here * window, head_count, head_size
    )
    return (cached_key_rows, cached_value_rows, window)


def attend(
    queries,
    keys_used,
    values_used,
    window_key_value,
    segment,
    inside,
    cache_valid_length,
    head_size,
):
    tok_count = queries.shape[0]
    head_count = queries.shape[1] // head_size
    requests_here = window_key_value.shape[0]
    cached_key_rows, cached_value_rows, window = split_cache(window_key_value, head_size)
    query_per_head = queries.reshape(tok_count, head_count, head_size)
    key_h = keys_used.reshape(tok_count, head_count, head_size)
    value_per_head = values_used.reshape(tok_count, head_count, head_size)
    attention_score_scale = head_size ** (-0.5)
    places = jnp.arange(tok_count, dtype=jnp.int32)
    local_mask = (
        (segment[:, None] == segment[None, :])
        & (places[None, :] <= places[:, None])
        & (places[None, :] > places[:, None] - window)
    )
    slot_ids = jnp.arange(requests_here * window, dtype=jnp.int32)
    owner_req = slot_ids // window
    within = slot_ids % window
    slot_ages = jnp.repeat(cache_valid_length, window)
    cache_mask = (
        (segment[:, None] == owner_req[None, :])
        & (within[None, :] >= window - slot_ages[None, :])
        & (within[None, :] > inside[:, None])
    )
    local_scores = (
        jnp.einsum("thd,jhd->htj", query_per_head, key_h, preferred_element_type=jnp.float32)
        * attention_score_scale
    )
    cached_score_rows = (
        jnp.einsum(
            "sek,yek->esy", query_per_head, cached_key_rows, preferred_element_type=jnp.float32
        )
        * attention_score_scale
    )
    local_scores = jnp.where(local_mask[None], local_scores, -jnp.inf)
    cached_score_rows = jnp.where(cache_mask[None], cached_score_rows, -jnp.inf)
    row_max = jnp.maximum(
        jnp.max(local_scores, axis=-1, keepdims=True),
        jnp.max(cached_score_rows, axis=-1, keepdims=True),
    )
    local_exp = jnp.exp(local_scores - row_max)
    cache_exp = jnp.exp(cached_score_rows - row_max)
    denominator = jnp.sum(local_exp, axis=-1, keepdims=True) + jnp.sum(
        cache_exp, axis=-1, keepdims=True
    )
    window_attention_weight = (local_exp / denominator).astype(jnp.bfloat16)
    cached_attention_weight = (cache_exp / denominator).astype(jnp.bfloat16)
    joined_output = jnp.einsum(
        "zkc,czu->kzu", window_attention_weight, value_per_head, preferred_element_type=jnp.float32
    )
    joined_output = joined_output + jnp.einsum(
        "lar,rlx->alx",
        cached_attention_weight,
        cached_value_rows,
        preferred_element_type=jnp.float32,
    )
    return joined_output.reshape(tok_count, head_count * head_size).astype(jnp.bfloat16)


def plain(
    inputs,
    attention_norm_gain,
    query_key_value_weight,
    filter_taps,
    output_projection,
    window_key_value,
    cache_valid_length,
    lengths,
    token_adapter_index,
    adapter_down_map,
    adapter_up_map,
    feed_forward_gain,
    gate_projection,
    up_projection,
    down_projection,
):
    own_count = inputs.shape[0]
    column = lax.axis_index("col")
    row_count = lax.axis_size("row")
    gathered = lax.all_gather(inputs, "col", axis=0, tiled=True)
    tok_count = gathered.shape[0]
    normalized_input = rms_scaled(gathered.astype(jnp.float32), attention_norm_gain).astype(
        jnp.bfloat16
    )
    qkv_mixed = jnp.einsum(
        "td,dka->tka",
        normalized_input,
        lax.all_gather(query_key_value_weight, "row", axis=0, tiled=True),
        preferred_element_type=jnp.float32,
    )
    segment, inside = layout(lengths[0], tok_count)
    queries, keys_used, values_used = make_qkv(qkv_mixed, filter_taps, inside)
    attended = attend(
        queries, keys_used, values_used, window_key_value, segment, inside, cache_valid_length, HD
    )
    kept_count = adapter_down_map.shape[0]
    every_adapter = kept_count * row_count
    capacity = max(2, 2 * own_count // every_adapter)
    first_row = column * own_count
    own_rows = lax.dynamic_slice_in_dim(normalized_input, first_row, own_count, 0)
    own_ids = lax.dynamic_slice_in_dim(token_adapter_index[:, 0], first_row, own_count, 0)
    member = (own_ids[:, None] == jnp.arange(every_adapter, dtype=jnp.int32)[None, :]).astype(
        jnp.int32
    )
    before = jnp.cumsum(member, axis=0) - member
    slot_rank = jnp.sum(before * member, axis=1)
    target = own_ids * capacity + slot_rank
    placer = (
        target[None, :] == jnp.arange(every_adapter * capacity, dtype=jnp.int32)[:, None]
    ).astype(jnp.bfloat16)
    outgoing = jnp.dot(placer, own_rows, preferred_element_type=jnp.float32).astype(jnp.bfloat16)
    outgoing = outgoing.reshape(row_count, kept_count, capacity, normalized_input.shape[1])
    reduced_rank_input = jnp.einsum(
        "sakd,adr->sakr",
        lax.all_to_all(outgoing, "row", split_axis=0, concat_axis=0, tiled=True),
        adapter_down_map,
        preferred_element_type=jnp.float32,
    ).astype(jnp.bfloat16)
    answered = jnp.einsum(
        "zjbf,jfm->zjbm", reduced_rank_input, adapter_up_map, preferred_element_type=jnp.float32
    ).astype(jnp.bfloat16)
    returned = lax.all_to_all(answered, "row", split_axis=0, concat_axis=0, tiled=True).reshape(
        every_adapter * capacity, normalized_input.shape[1]
    )
    delta_rows = jnp.dot(jnp.transpose(placer), returned, preferred_element_type=jnp.float32)
    out_term = jnp.dot(
        attended,
        lax.all_gather(output_projection, "row", axis=1, tiled=True),
        preferred_element_type=jnp.float32,
    )
    own_term = lax.dynamic_slice_in_dim(out_term, first_row, own_count, 0) + delta_rows
    out_term = lax.dynamic_update_slice_in_dim(out_term, own_term, first_row, 0)
    attn_share = lax.psum_scatter(
        out_term.astype(jnp.bfloat16), "col", scatter_dimension=0, tiled=True
    ).astype(jnp.float32)
    residual = (inputs.astype(jnp.float32) + attn_share).astype(jnp.bfloat16)
    whole_mixed = lax.all_gather(residual, "col", axis=0, tiled=True)
    normed_mlp = rms_scaled(whole_mixed.astype(jnp.float32), feed_forward_gain).astype(jnp.bfloat16)

    def add_rows(piece):
        return jnp.dot(normed_mlp, piece, preferred_element_type=jnp.float32)

    gate = add_rows(lax.all_gather(gate_projection, "row", axis=0, tiled=True))
    up_part = add_rows(lax.all_gather(up_projection, "row", axis=0, tiled=True))
    hidden = (jax.nn.silu(gate) * up_part).astype(jnp.bfloat16)
    down_term = jnp.dot(
        hidden,
        lax.all_gather(down_projection, "row", axis=1, tiled=True),
        preferred_element_type=jnp.float32,
    )
    mlp_added = lax.psum_scatter(
        down_term.astype(jnp.bfloat16), "col", scatter_dimension=0, tiled=True
    ).astype(jnp.float32)
    return (residual.astype(jnp.float32) + mlp_added).astype(jnp.bfloat16)


LANES = 128
MIB = 1 << 20


LIGHT = pl.CostEstimate(flops=1, bytes_accessed=1, transcendentals=0)


def params(mib):
    return pltpu.CompilerParams(vmem_limit_bytes=mib * MIB)


HBM = pl.BlockSpec(memory_space=pl.ANY)
VMEM = pl.BlockSpec(memory_space=pltpu.VMEM)
SMEM = pl.BlockSpec(memory_space=pltpu.SMEM)
NT = (((1,), (1,)), ((), ()))


def normed(values, gain):
    mean_square = jnp.mean(values * values, axis=-1, keepdims=True)
    return (values * lax.rsqrt(mean_square + epsilon) * gain).astype(jnp.bfloat16)


def entry_kernel(*refs):
    sources, (normed_ref, packed_ref) = refs[:6], refs[6:8]
    targets, sems = refs[8:14], refs[14]
    loads = [
        pltpu.make_async_copy(source, target, sems.at[i])
        for i, (source, target) in enumerate(zip(sources, targets))
    ]
    for load in loads:
        load.start()
    x_ref, qkv_ref, out_ref, gain_ref, down_ref, up_ref = targets
    rows, part, ranks = qkv_ref.shape[1], qkv_ref.shape[2], down_ref.shape[0]
    loads[0].wait()
    loads[3].wait()
    normed_ref[...] = normed(x_ref[...].astype(jnp.float32), gain_ref[...][None, :])
    for at in (1, 2, 4, 5):
        loads[at].wait()
    for place, which in enumerate((1, 0, 2)):
        packed_ref[:rows, place * part : (place + 1) * part] = qkv_ref[which]
    out_rows = jnp.transpose(out_ref[...].astype(jnp.float32)).astype(jnp.bfloat16)
    packed_ref[:rows, 3 * part :] = out_rows
    packed_ref[rows : rows + ranks, :] = down_ref[...]
    packed_ref[rows + ranks :, :] = up_ref[...]


def entry_call(rows, qkv, out, gain, down, up):
    sources = (rows, qkv, out, gain, down, up)
    return pl.pallas_call(
        entry_kernel,
        out_shape=[
            jax.ShapeDtypeStruct(rows.shape, jnp.bfloat16),
            jax.ShapeDtypeStruct((qkv.shape[1] + 2 * down.shape[0], 4 * qkv.shape[2]), jnp.bfloat16),
        ],
        in_specs=[HBM] * len(sources),
        out_specs=[VMEM] * 2,
        scratch_shapes=[pltpu.VMEM(source.shape, source.dtype) for source in sources]
        + [pltpu.SemaphoreType.DMA((len(sources),))],
        compiler_params=params(60),
        cost_estimate=LIGHT,
    )(*sources)


def residual_kernel(x_ref, own_ref, two_ref, one_ref, gain_ref, residual_ref, normed_ref):
    total = own_ref[...] + one_ref[...].astype(jnp.float32) + two_ref[...].astype(jnp.float32)
    residual = (x_ref[...].astype(jnp.float32) + total).astype(jnp.bfloat16)
    residual_ref[...] = residual
    normed_ref[...] = normed(residual.astype(jnp.float32), gain_ref[...])


def residual_call(rows, own, two, one, gain):
    block = jax.ShapeDtypeStruct(rows.shape, jnp.bfloat16)
    return pl.pallas_call(
        residual_kernel,
        out_shape=[block, block],
        in_specs=[VMEM] * 5,
        out_specs=[VMEM] * 2,
        compiler_params=params(12),
        cost_estimate=LIGHT,
    )(rows, own, two, one, gain[None, :])


def adapter_term(x_ref, ids_ref, down_ref, up_ref, rank):
    low = lax.dot_general(x_ref[...], down_ref[...], NT, preferred_element_type=jnp.float32)
    adapter = lax.broadcasted_iota(jnp.int32, low.shape, 1) // rank
    low = jnp.where(ids_ref[...] == adapter, low, 0.0).astype(jnp.bfloat16)
    return jnp.dot(low, up_ref[...], preferred_element_type=jnp.float32).astype(jnp.bfloat16)


def xor_pairs(count, mask):
    return [(i, i ^ mask) for i in range(count)]


def swap(value, axis, mask):
    return lax.ppermute(value, axis, xor_pairs(lax.axis_size(axis), mask))


def first_hops(own):
    return swap(own, "row", 2), swap(own, "row", 4)


def second_hops(own, from_x, from_y):
    half = own.shape[-2] // 2
    diagonal = swap(from_x[..., :half, :], "row", 4), swap(from_y[..., half:, :], "row", 2)
    return diagonal + tuple(swap(piece, "row", 1) for piece in (own, from_x, from_y))


def named_pieces(own, firsts, seconds, thirds):
    half = own.shape[-2] // 2
    masks = [(0, 0), (2, 0), (4, 0), (6, 0), (6, half), (1, 0), (3, 0), (5, 0), (7, 0), (7, half)]
    return [(piece, *at) for piece, at in zip((own,) + firsts + seconds + thirds, masks)]


def shard_starts(places, shard):
    row = lax.axis_index("row")
    return [pl.multiple_of((row ^ mask) * shard + first, 16) for mask, first in places]


def request_columns(lengths_ref, begin, count):
    place = begin + lax.broadcasted_iota(jnp.int32, (count, 1), 0)
    segment, first = jnp.zeros_like(place), jnp.zeros_like(place)
    finish = jnp.int32(0)
    for s in range(lengths_ref.shape[1]):
        finish = finish + lengths_ref[0, s]
        later = place >= finish
        segment = segment + later.astype(jnp.int32)
        first = jnp.where(later, finish, first)
    return place, segment, first


def attend_block(mask, count, base, lengths_ref, valid_ref, q_ref, k_ref, v_ref, cache_ref):
    col = lax.axis_index("col")
    _, heads, slots, lanes = cache_ref.shape
    requests = valid_ref.shape[0]
    window = slots // requests
    scale = HD ** (-0.5)
    begin = pl.multiple_of((col ^ mask) * count, count)
    key_begin = pl.multiple_of(jnp.maximum(begin - window, 0), window)
    key_count = count + window
    place, segment, first = request_columns(lengths_ref, begin, count)
    first_key = jnp.maximum(first, place - window + 1)
    keys = key_begin + lax.broadcasted_iota(jnp.int32, (count, key_count), 1)
    local_mask = (keys >= first_key) & (keys <= place)
    slot = lax.broadcasted_iota(jnp.int32, (1, slots), 1)
    owner, within = slot // window, slot % window
    oldest = jnp.full_like(slot, window)
    for s in range(requests):
        oldest = jnp.where(owner == s, window - valid_ref[s], oldest)
    within = jnp.where(within >= oldest, within, -1)
    cache_mask = (owner == segment) & (within > place - first)
    outs = []
    own_rows = pl.ds(pl.multiple_of(begin - base, count), count)
    key_rows = pl.ds(pl.multiple_of(key_begin - base, window), key_count)
    for h in range(heads):
        cols = slice(h * lanes, (h + 1) * lanes)
        q, k, v = q_ref[own_rows, cols], k_ref[key_rows, cols], v_ref[key_rows, cols]
        local = lax.dot_general(q, k, NT, preferred_element_type=jnp.float32)
        cached = lax.dot_general(q, cache_ref[0, h], NT, preferred_element_type=jnp.float32)
        local = jnp.where(local_mask, local * scale, -jnp.inf)
        cached = jnp.where(cache_mask, cached * scale, -jnp.inf)
        top = jnp.maximum(
            jnp.max(local, axis=-1, keepdims=True), jnp.max(cached, axis=-1, keepdims=True)
        )
        local = jnp.exp(local - top)
        cached = jnp.exp(cached - top)
        total = jnp.sum(local, axis=-1, keepdims=True) + jnp.sum(cached, axis=-1, keepdims=True)
        summed = jnp.dot(local.astype(jnp.bfloat16), v, preferred_element_type=jnp.float32)
        summed = summed + jnp.dot(
            cached.astype(jnp.bfloat16), cache_ref[1, h], preferred_element_type=jnp.float32
        )
        outs.append((summed / total).astype(jnp.bfloat16)[:, :HD])
    blank = jnp.zeros((count, heads * (lanes - HD)), jnp.bfloat16)
    return jnp.concatenate([blank] + outs, axis=1)


def mix_rows(x, base, w_ref, taps_ref, lengths_ref, q_ref, k_ref, v_ref, padded):
    rows, part = x.shape[0], taps_ref.shape[2]
    padded[0:8, :] = jnp.zeros((8, part), jnp.float32)
    place, _, first = request_columns(lengths_ref, base, rows)
    inside = place - first
    mixed = jnp.dot(x, w_ref[...], preferred_element_type=jnp.float32)

    def convolved(raw, which):
        padded[8:, :] = raw
        running = taps_ref[0, which : which + 1, :] * raw
        for offset in range(1, taps_ref.shape[0]):
            moved = padded[8 - offset : 8 - offset + rows, :]
            tap = taps_ref[offset, which : which + 1, :]
            running = running + jnp.where(inside >= offset, tap * moved, 0.0)
        return running

    def store_heads(ref, value):
        blank = jnp.zeros((rows, LANES - HD), jnp.bfloat16)
        for h in range(part // HD):
            ref[:, h * LANES : h * LANES + HD] = value[:, h * HD : (h + 1) * HD].astype(jnp.bfloat16)
            ref[:, h * LANES + HD : (h + 1) * LANES] = blank

    store_heads(k_ref, convolved(mixed[:, :part], 0))
    store_heads(q_ref, mixed[:, part : 2 * part])
    raw_values = mixed[:, 2 * part : 3 * part]
    store_heads(v_ref, raw_values * jax.nn.sigmoid(convolved(raw_values, 1)))


def first_kernel(places, n_x, n_w, *refs):
    x_refs, w_refs = refs[:n_x], refs[n_x : n_x + n_w]
    taps_ref, lengths_ref, valid_ref, cache_ref = refs[n_x + n_w : n_x + n_w + 4]
    x_all, w_all, out_w, down_ref, up_ref, part_ref, q_ref, k_ref, v_ref, padded = refs[n_x + n_w + 4 :]
    col = lax.axis_index("col")
    count, width = x_refs[0].shape
    lanes, mixed_lanes = out_w.shape[1], w_all.shape[1]
    for i, ref in enumerate(x_refs):
        x_all[pl.ds(pl.multiple_of((col ^ i) * count, 16), count), :] = ref[...]
    shard = width // lax.axis_size("row")
    ranks = down_ref.shape[0] // lax.axis_size("row")
    starts = shard_starts(places, shard)
    for ref, start, (mask, first) in zip(w_refs, starts, places):
        rows = min(ref.shape[0], shard - first)
        w_all[pl.ds(start, rows), :] = ref[:rows, :mixed_lanes]
        out_w[pl.ds(start, rows), :] = ref[:rows, ref.shape[1] - lanes :]
        if rows < ref.shape[0]:
            at = pl.multiple_of((lax.axis_index("row") ^ mask) * ranks, 16)
            down_ref[pl.ds(at, ranks), :] = ref[rows : rows + ranks, :]
            up_ref[pl.ds(at, ranks), :] = ref[rows + ranks :, :]
    base = pl.multiple_of(jnp.maximum((col ^ (n_x - 1)) * count - count, 0), count)
    x = x_all[pl.ds(base, 2 * count), :]
    mix_rows(x, base, w_all, taps_ref, lengths_ref, q_ref, k_ref, v_ref, padded)
    attended = attend_block(
        n_x - 1, count, base, lengths_ref, valid_ref, q_ref, k_ref, v_ref, cache_ref
    )
    part_ref[...] = lax.dot_general(
        attended, out_w[...], NT, preferred_element_type=jnp.float32
    ).astype(jnp.bfloat16)


def first_call(blocks, pieces, ranks, taps, lengths, valid, cache):
    (count, width), n_x, n_w = blocks[0].shape, len(blocks), len(pieces)
    tokens, part = count * n_x, taps.shape[2]
    lanes = part // HD * LANES
    mixed_lanes = -(-3 * part // LANES) * LANES
    places = [(mask, first) for _, mask, first in pieces]
    shapes = [(tokens, width), (width, mixed_lanes), (width, lanes), (ranks, width), (ranks, width), (count, width)]
    return pl.pallas_call(
        functools.partial(first_kernel, places, n_x, n_w),
        out_shape=[pltpu.VMEM(shape, jnp.bfloat16) for shape in shapes[:3]]
        + [jax.ShapeDtypeStruct(shape, jnp.bfloat16) for shape in shapes[3:]],
        in_specs=[VMEM] * (n_x + n_w + 1) + [SMEM, SMEM, VMEM],
        out_specs=[VMEM] * len(shapes),
        scratch_shapes=[pltpu.VMEM((2 * count, lanes), jnp.bfloat16)] * 3
        + [pltpu.VMEM((2 * count + 8, part), jnp.float32)],
        compiler_params=params(28),
        cost_estimate=LIGHT,
    )(*blocks, *(piece for piece, _, _ in pieces), taps, lengths, valid, cache)


def rest_kernel(masks, x_all, w_all, out_w, taps_ref, lengths_ref, valid_ref, cache_ref, *refs):
    q_ref, k_ref, v_ref = refs[:3]
    out_refs, padded = refs[3:-1], refs[-1]
    mix_rows(x_all[...], 0, w_all, taps_ref, lengths_ref, q_ref, k_ref, v_ref, padded)
    for mask, out_ref in zip(masks, out_refs):
        attended = attend_block(
            mask, out_ref.shape[0], 0, lengths_ref, valid_ref, q_ref, k_ref, v_ref, cache_ref
        )
        out_ref[...] = lax.dot_general(
            attended, out_w[...], NT, preferred_element_type=jnp.float32
        ).astype(out_ref.dtype)


def rest_call(masks, count, x_all, w_all, out_w, taps, lengths, valid, cache):
    (tokens, width), lanes = x_all.shape, out_w.shape[1]
    shapes = [(tokens, lanes)] * 3 + [(count, width)] * len(masks)
    return pl.pallas_call(
        functools.partial(rest_kernel, masks),
        out_shape=[jax.ShapeDtypeStruct(shape, jnp.bfloat16) for shape in shapes],
        in_specs=[VMEM] * 4 + [SMEM, SMEM, VMEM],
        out_specs=[VMEM] * len(shapes),
        scratch_shapes=[pltpu.VMEM((tokens + 8, taps.shape[2]), jnp.float32)],
        compiler_params=params(32),
        cost_estimate=LIGHT,
    )(x_all, w_all, out_w, taps, lengths, valid, cache)


def own_kernel(rank, q_ref, k_ref, v_ref, out_w, x_ref, ids_ref, down_ref, up_ref, *refs):
    lengths_ref, valid_ref, cache_ref, out_ref = refs
    attended = attend_block(
        0, out_ref.shape[0], 0, lengths_ref, valid_ref, q_ref, k_ref, v_ref, cache_ref
    )
    part = lax.dot_general(attended, out_w[...], NT, preferred_element_type=jnp.float32)
    out_ref[...] = part + adapter_term(x_ref, ids_ref, down_ref, up_ref, rank).astype(jnp.float32)


def own_call(rank, q, k, v, out_w, x, ids, down, up, lengths, valid, cache):
    return pl.pallas_call(
        functools.partial(own_kernel, rank),
        out_shape=jax.ShapeDtypeStruct(x.shape, jnp.float32),
        in_specs=[VMEM] * 8 + [SMEM, SMEM, VMEM],
        out_specs=VMEM,
        compiler_params=params(20),
        cost_estimate=LIGHT,
    )(q, k, v, out_w, x, ids, down, up, lengths, valid, cache)


def feed(x, all_w):
    gate = jnp.dot(x, all_w[0], preferred_element_type=jnp.float32)
    up = jnp.dot(x, all_w[1], preferred_element_type=jnp.float32)
    act = (jax.nn.silu(gate) * up).astype(jnp.bfloat16)
    return lax.dot_general(act, all_w[2], NT, preferred_element_type=jnp.float32)


def feed_first_kernel(places, n_x, n_w, *refs):
    x_refs, w_refs = refs[:n_x], refs[n_x : n_x + n_w]
    all_w, out_refs = refs[n_x + n_w], refs[n_x + n_w + 1 :]
    starts = shard_starts(places, all_w.shape[1] // lax.axis_size("row"))
    for part in range(3):
        for ref, start in zip(w_refs, starts):
            all_w[part, pl.ds(start, ref.shape[1]), :] = ref[part]
    down = feed(jnp.concatenate([ref[...] for ref in x_refs], axis=0), all_w)
    count = x_refs[0].shape[0]
    for i, ref in enumerate(out_refs):
        ref[...] = down[i * count : (i + 1) * count].astype(ref.dtype)


def feed_first_call(blocks, pieces, out_types):
    n_x, n_w, (count, width) = len(blocks), len(pieces), blocks[0].shape
    places = [(mask, first) for _, mask, first in pieces]
    hidden = pieces[0][0].shape[2]
    return pl.pallas_call(
        functools.partial(feed_first_kernel, places, n_x, n_w),
        out_shape=[pltpu.VMEM((3, width, hidden), jnp.bfloat16)]
        + [jax.ShapeDtypeStruct((count, width), t) for t in out_types],
        in_specs=[VMEM] * (n_x + n_w),
        out_specs=[VMEM] * (n_x + 1),
        compiler_params=params(28),
        cost_estimate=LIGHT,
    )(*blocks, *(piece for piece, _, _ in pieces))


def feed_last_kernel(x_ref, all_w, out_ref):
    out_ref[...] = feed(x_ref[...], all_w).astype(out_ref.dtype)


def feed_last_call(rows, all_w):
    return pl.pallas_call(
        feed_last_kernel,
        out_shape=jax.ShapeDtypeStruct(rows.shape, jnp.bfloat16),
        in_specs=[VMEM] * 2,
        out_specs=VMEM,
        compiler_params=params(20),
        cost_estimate=LIGHT,
    )(rows, all_w)


def sum_kernel(part_ref, near_ref, far_ref, out_ref):
    passed = jnp.concatenate([near_ref[...], far_ref[...]], axis=0).astype(jnp.float32)
    out_ref[...] = (part_ref[...].astype(jnp.float32) + passed).astype(out_ref.dtype)


def sum_call(part, near, far):
    return pl.pallas_call(
        sum_kernel,
        out_shape=jax.ShapeDtypeStruct(part.shape, jnp.bfloat16),
        in_specs=[VMEM] * 3,
        out_specs=VMEM,
        compiler_params=params(12),
        cost_estimate=LIGHT,
    )(part, near, far)


def last_kernel(residual_ref, own_ref, two_ref, one_ref, out_ref):
    total = own_ref[...] + one_ref[...].astype(jnp.float32) + two_ref[...].astype(jnp.float32)
    out_ref[...] = (residual_ref[...].astype(jnp.float32) + total).astype(out_ref.dtype)


def last_call(residual, own, two, one):
    return pl.pallas_call(
        last_kernel,
        out_shape=jax.ShapeDtypeStruct(residual.shape, jnp.bfloat16),
        in_specs=[VMEM] * 4,
        out_specs=VMEM,
        compiler_params=params(12),
        cost_estimate=LIGHT,
    )(residual, own, two, one)


def tuned(
    inputs,
    attention_norm_gain,
    query_key_value_weight,
    filter_taps,
    output_projection,
    window_key_value,
    cache_valid_length,
    lengths,
    token_adapter_index,
    adapter_down_map,
    adapter_up_map,
    feed_forward_gain,
    gate_projection,
    up_projection,
    down_projection,
):
    bf16, f32 = jnp.bfloat16, jnp.float32
    col = lax.axis_index("col")
    count, width = inputs.shape
    heads = window_key_value.shape[2]

    rank, kept = adapter_down_map.shape[2], adapter_down_map.shape[0]
    normed_attention, packed = entry_call(
        inputs,
        jnp.transpose(query_key_value_weight, (1, 0, 2)),
        output_projection,
        attention_norm_gain,
        jnp.transpose(adapter_down_map, (0, 2, 1)).reshape(kept * rank, width),
        adapter_up_map.reshape(kept * rank, width),
    )
    token_two, token_one = swap(normed_attention, "col", 2), swap(normed_attention, "col", 1)
    firsts = first_hops(packed)
    requests = window_key_value.shape[0]
    window = window_key_value.shape[3] // HD
    cache = window_key_value.reshape(requests, 2, heads, window, HD)
    cache = jnp.transpose(cache, (1, 2, 0, 3, 4)).reshape(2, heads, requests * window, HD)
    cache = jnp.pad(cache, ((0, 0), (0, 0), (0, 0), (0, LANES - HD)))
    own_ids = lax.dynamic_slice_in_dim(token_adapter_index, col * count, count, 0)
    feed_own = jnp.concatenate(
        [gate_projection[None], up_projection[None], jnp.transpose(down_projection)[None]], axis=0
    )
    firsts, cache, own_ids, feed_own = lax.optimization_barrier((firsts, cache, own_ids, feed_own))
    token_two, token_one, cache = lax.optimization_barrier((token_two, token_one, cache))
    token_three = swap(token_two, "col", 1)
    seconds = second_hops(packed, *firsts)
    token_three, diagonal, feed_own = lax.optimization_barrier((token_three, seconds[:2], feed_own))
    seconds = diagonal + seconds[2:]
    thirds = tuple(swap(piece, "row", 1) for piece in diagonal)
    feed_firsts = first_hops(feed_own)

    pieces = named_pieces(packed, firsts, seconds, thirds)
    blocks = [normed_attention, token_one, token_two, token_three]
    requests_here = (lengths, cache_valid_length, cache)
    ranks = kept * rank * lax.axis_size("row")
    x_all, w_all, out_w, down_maps, up_maps, part_three = first_call(
        blocks, pieces, ranks, filter_taps, *requests_here
    )
    passed = swap(part_three, "col", 1)
    q, k, v, part_two, part_one = rest_call(
        [2, 1], count, x_all, w_all, out_w, filter_taps, *requests_here
    )
    part_own = own_call(
        rank, q, k, v, out_w, normed_attention, own_ids, down_maps, up_maps, *requests_here
    )
    got_one = swap(part_one, "col", 1)
    got_two = swap((part_two.astype(f32) + passed.astype(f32)).astype(bf16), "col", 2)
    got_one, *hops = lax.optimization_barrier((got_one, *feed_firsts))
    feed_seconds = second_hops(feed_own, *hops)
    residual, normed_mlp = residual_call(inputs, part_own, got_two, got_one, feed_forward_gain)
    token_two, token_one = swap(normed_mlp, "col", 2), swap(normed_mlp, "col", 1)
    feed_thirds = tuple(swap(piece, "row", 1) for piece in feed_seconds[:2])
    token_two, token_one = lax.optimization_barrier((token_two, token_one))
    split = count // 2
    three = [swap(rows, "col", 1) for rows in (token_two[:split], token_two[split:])]
    feed_pieces = named_pieces(feed_own, feed_firsts, feed_seconds, feed_thirds)
    feed_w, part_two, part_one, part_own = feed_first_call(
        [token_two, token_one, normed_mlp], feed_pieces, [bf16, bf16, f32]
    )
    near, far = (feed_last_call(rows, feed_w) for rows in three)
    part_two = sum_call(part_two, swap(near, "col", 1), swap(far, "col", 1))
    part_two, part_one = lax.optimization_barrier((part_two, part_one))
    got_two, got_one = swap(part_two, "col", 2), swap(part_one, "col", 1)
    return last_call(residual, part_own, got_two, got_one)


def on_device(*args):
    rows, cols = lax.axis_size("row"), lax.axis_size("col")
    if (rows, cols) == (8, 4):
        return tuned(*args)
    return plain(*args)


def solution(mesh):
    placed = (
        P(("row", "col"), None),
        P(),
        P("row", None, "col"),
        P(None, None, "col"),
        P("col", "row"),
        P("row", None, "col", None),
        P("row"),
        P("row", None),
        P("row", None),
        P("row", None, None),
        P("row", None, None),
        P(),
        P("row", "col"),
        P("row", "col"),
        P("col", "row"),
    )
    return jax.shard_map(
        on_device, mesh=mesh, in_specs=placed, out_specs=P(("row", "col"), None), check_vma=False
    )
```
